32 devices in a mesh: dp: 8 (over z, y), head: 4 (over x, core).
Axes of the slice: x: 2, y: 2, z: 4, core: 2. Of those that a mesh axis runs over, the one named last changes fastest.
Arguments:
- decoder_in: bfloat16 [8192, 768], P(('dp', 'head')), may hold values from -6 to 6
- encoder_out: bfloat16 [32, 1024, 768], P('dp', 'head'), may hold values from -6 to 6
- encoder_segment: int32 [32, 1024], P('dp'), may hold values from 0 to 15, never falling along the last dimension, each value on 1 to 512 neighbouring positions
- slot_segment: int32 [32, 16], P('dp'), may hold values from 0 to 15, each once within a row
- position_bucket: int32 [16, 16], replicated, may hold values from 0 to 31
- self_gain: float32 [768], replicated, may hold values from 0.5 to 1.5
- self_query: bfloat16 [768, 768], replicated, may hold values from -0.4375 to 0.4375
- self_key: bfloat16 [768, 768], replicated, may hold values from -0.21875 to 0.21875
- self_value: bfloat16 [768, 768], replicated, may hold values from -0.21875 to 0.21875
- self_output: bfloat16 [768, 768], replicated, may hold values from -0.4375 to 0.4375
- position_bias: float32 [32, 12], replicated, may hold values from -4 to 4
- cross_gain: float32 [768], replicated, may hold values from 0.5 to 1.5
- cross_query: bfloat16 [768, 768], replicated, may hold values from -0.4375 to 0.4375
- cross_key: bfloat16 [768, 768], replicated, may hold values from -0.21875 to 0.21875
- cross_value: bfloat16 [768, 768], replicated, may hold values from -0.21875 to 0.21875
- cross_output: bfloat16 [768, 768], replicated, may hold values from -0.875 to 0.875
- feed_gain: float32 [768], replicated, may hold values from 0.5 to 1.5
- feed_in: bfloat16 [768, 3072], replicated, may hold values from -0.21875 to 0.21875
- feed_out: bfloat16 [3072, 768], replicated, may hold values from -0.15625 to 0.15625
- score_row: bfloat16 [768], replicated, may hold values from -6 to 6
- grad_hidden: float32 [8192, 768], P(('dp', 'head')), may hold values from -6 to 6
- grad_score: float32 [8192], P(('dp', 'head')), may hold values from -6 to 6
Outputs:
- hidden_out: bfloat16 [8192, 768], P(('dp', 'head'))
- ranking_score: float32 [8192], P(('dp', 'head'))
- decoder_grad: float32 [8192, 768], P(('dp', 'head'))
- encoder_grad: float32 [32, 1024, 768], P('dp', 'head')
- self_gain_grad: float32 [768], P('head')
- self_query_grad: float32 [768, 768], P('head')
- self_key_grad: float32 [768, 768], P('head')
- self_value_grad: float32 [768, 768], P('head')
- self_output_grad: float32 [768, 768], P('head')
- position_bias_grad: float32 [32, 12], P('head')
- cross_gain_grad: float32 [768], P('head')
- cross_query_grad: float32 [768, 768], P('head')
- cross_key_grad: float32 [768, 768], P('head')
- cross_value_grad: float32 [768, 768], P('head')
- cross_output_grad: float32 [768, 768], P('head')
- feed_gain_grad: float32 [768], P('head')
- feed_in_grad: float32 [768, 3072], P('head')
- feed_out_grad: float32 [3072, 768], P('head')
- score_row_grad: float32 [768], P('head')
The draws below stay inside these ranges and needn't reach their ends.
Inputs may be any that keep to these rules, and one draw needn't show every extreme that they name: `encoder_segment`: in every row the numbers never fall along the 1024 positions, each of 0 to 15 occurs, no segment holds more than 512 positions and some segment holds exactly that many. `slot_segment`: each row's 16 slots name each of that row's segments once.
All inputs are finite; a program needn't handle non-finite values.
Results may differ from the reference program's by a relative error of at most 0.022.
The reference program's roundings to bfloat16 on the way count: a program that leaves them out, or rounds other values in their place, can miss the bound.
Values may be sent and summed in bfloat16 or wider, within the bound.
No kernel may reach another device: no remote copies, remote signals or barrier semaphores. Data moves between devices by JAX's collectives and lax.ppermute only.
A program may use at most 192 MiB of HBM per device.

```python
import math
import jax
import jax.numpy as jnp
import numpy as np
from jax import lax

D = 768
FF = 3072
HEADS = 12
HEAD_DIM = 64
NB = 32
PAIRS = 16
STEPS = 16
SEQ = 1024
ROWS = 32
DEC = 8192


def with_ends(result, key, least, largest):
    spot = [jax.random.randint(jax.random.fold_in(key, axis), (), 0, length) for axis, length in enumerate(result.shape)]
    main_axis = result.shape.index(max(result.shape))
    neighbour = spot[:main_axis] + [(spot[main_axis] + 1) % result.shape[main_axis]] + spot[main_axis + 1:]
    return result.at[tuple(spot)].set(least).at[tuple(neighbour)].set(largest)


def steps_of(rng, shape, cuts, least, top_value):
    def one(position, blocks):
        steps = jax.random.uniform(jax.random.fold_in(jax.random.fold_in(rng, 6), position), (blocks,), jnp.float32, least / len(cuts), top_value / len(cuts))
        return jnp.repeat(jnp.exp(steps), shape[position] // blocks).reshape((-1,) + (1,) * (len(shape) - position - 1))

    gain = one(*cuts[0])
    for cut in cuts[1:]:
        gain = gain * one(*cut)
    return gain


def split_up(amount, total, bound, skew):
    portions = [(1 << 20) // math.isqrt(grade ** skew) + 1 for grade in range(2, amount + 1)]
    surplus, counts = total - bound - (amount - 1), [1] * (amount - 1)
    while surplus > 0:
        free = [i for i in range(amount - 1) if counts[i] < bound]
        pool, budget = sum([portions[i] for i in free]), surplus
        for i in free:
            more = min(bound - counts[i], max(1, budget * portions[i] // pool), surplus)
            counts[i] = counts[i] + more
            surplus = surplus - more
    return np.array([bound] + counts)


def uneven_parts(key, count, total, bound, skew):
    if count == 2:
        one = jax.random.randint(key, (), max(1, total - bound), min(bound, total - 1) + 1)
        return jnp.stack([one, total - one])
    tallies = jnp.asarray(split_up(count, total, bound, skew), jnp.int32)
    pairs = (count - 1) // 2
    donor, sink = tallies[1:1 + 2 * pairs:2], tallies[2:2 + 2 * pairs:2]
    room = jnp.minimum(donor - 1, bound - sink)
    shifted = jax.random.randint(jax.random.fold_in(key, 1), (pairs,), 0, 1 << 20) % (room + 1)
    tallies = tallies.at[1:1 + 2 * pairs:2].set(donor - shifted).at[2:2 + 2 * pairs:2].set(sink + shifted)
    return tallies[jax.random.permutation(jax.random.fold_in(key, 2), count)]


def bell_draw(rng, dims, deviation, reach, pieces=(), kind=jnp.bfloat16):
    factor_of = steps_of(rng, dims, pieces, -0.22, 0.18) if pieces else 1.0
    array = jax.random.normal(rng, dims, jnp.float32) * deviation * factor_of
    return jnp.minimum(jnp.maximum(array, -reach), reach).astype(kind)


def setup_inputs(seed: int = 0) -> dict:
    keys = jax.random.split(jax.random.key(seed), 23)
    decoder_in = bell_draw(keys[0], (DEC, D), 1.0, 6.0, ((0, 32),))
    encoder_out = bell_draw(keys[1], (ROWS, SEQ, D), 1.0, 6.0, ((0, 8), (1, 4)))
    encoder_segment = jax.vmap(lambda own: jnp.searchsorted(jnp.cumsum(uneven_parts(own, PAIRS, SEQ, SEQ // 2, 1)), jnp.arange(SEQ), side="right"))(jax.random.split(keys[2], ROWS)).reshape((ROWS, SEQ)).astype(jnp.int32)
    slot_segment = jax.vmap(lambda own: jax.random.permutation(own, PAIRS))(jax.random.split(keys[3], ROWS)).reshape((ROWS, PAIRS)).astype(jnp.int32)
    position_bucket = with_ends(jax.random.randint(keys[4], (STEPS, STEPS), 0, NB), jax.random.fold_in(keys[4], 1), 0, NB - 1).astype(jnp.int32)
    self_gain = jnp.clip(1.0 + 0.1 * jax.random.normal(keys[5], (D,), jnp.float32), 0.5, 1.5)
    self_query = bell_draw(keys[6], (D, D), (D // 4) ** -0.5, 0.4375)
    self_key = bell_draw(keys[7], (D, D), D ** -0.5, 0.21875)
    self_value = bell_draw(keys[8], (D, D), D ** -0.5, 0.21875)
    self_output = bell_draw(keys[9], (D, D), (D // 4) ** -0.5, 0.4375)
    position_bias = bell_draw(keys[10], (NB, HEADS), 1.0, 4.0, (), jnp.float32)
    cross_gain = jnp.clip(1.0 + 0.1 * jax.random.normal(keys[11], (D,), jnp.float32), 0.5, 1.5)
    cross_query = bell_draw(keys[12], (D, D), (D // 4) ** -0.5, 0.4375)
    cross_key = bell_draw(keys[13], (D, D), D ** -0.5, 0.21875)
    cross_value = bell_draw(keys[14], (D, D), D ** -0.5, 0.21875)
    cross_output = bell_draw(keys[15], (D, D), (D // 16) ** -0.5, 0.875)
    feed_gain = jnp.clip(1.0 + 0.1 * jax.random.normal(keys[16], (D,), jnp.float32), 0.5, 1.5)
    feed_in = bell_draw(keys[17], (D, FF), D ** -0.5, 0.21875)
    feed_out = bell_draw(keys[18], (FF, D), (FF // 2) ** -0.5, 0.15625)
    score_row = bell_draw(keys[19], (D,), 1.0, 6.0)
    grad_hidden = bell_draw(keys[20], (DEC, D), 1.0, 6.0, ((0, 32),), jnp.float32)
    grad_score = bell_draw(keys[21], (DEC,), 1.0, 6.0, ((0, 32),), jnp.float32)
    return dict(decoder_in=decoder_in, encoder_out=encoder_out, encoder_segment=encoder_segment, slot_segment=slot_segment, position_bucket=position_bucket, self_gain=self_gain, self_query=self_query, self_key=self_key, self_value=self_value, self_output=self_output, position_bias=position_bias, cross_gain=cross_gain, cross_query=cross_query, cross_key=cross_key, cross_value=cross_value, cross_output=cross_output, feed_gain=feed_gain, feed_in=feed_in, feed_out=feed_out, score_row=score_row, grad_hidden=grad_hidden, grad_score=grad_score)


EPSILON = 1e-06
MASKED = -1e+30
PRECISE = lax.Precision.HIGHEST

@jax.custom_vjp
def low(v):
    return lax.optimization_barrier(v.astype(jnp.bfloat16)).astype(jnp.float32)

@jax.custom_vjp
def low_back(v):
    return v

def low_keep(v):
    return (low(v), None)

def low_pass(kept, grad):
    return (grad,)

def back_keep(v):
    return (v, None)

def back_low(kept, grad):
    return (low(grad),)
low.defvjp(low_keep, low_pass)
low_back.defvjp(back_keep, back_low)

def matmul(first_factor, second_factor):
    return jnp.dot(first_factor, second_factor, precision=PRECISE, preferred_element_type=jnp.float32)

def rms_norm(hidden, norm_gain):
    return hidden * lax.rsqrt(lax.optimization_barrier(jnp.mean(hidden * hidden, axis=-1, keepdims=True)) + EPSILON) * norm_gain

def gelu_curve(values):
    return jax.nn.gelu(values, approximate=True)

def self_attend(normed, query_w, key_w, value_w, output_w, position_bias, position_bucket):
    activation = low(normed)
    slot_count = normed.shape[0] // STEPS

    def heads_of(matrix):
        return low(low_back(matmul(activation, matrix))).reshape(slot_count, STEPS, HEADS, HEAD_DIM)
    query_heads = heads_of(query_w)
    key_heads = heads_of(key_w)
    value_heads = heads_of(value_w)
    onehot = (position_bucket[:, :, None] == jnp.arange(NB, dtype=jnp.int32)[None, None, :]).astype(jnp.float32)
    bias_table = jnp.einsum('ijb,bh->hij', onehot, position_bias, precision=PRECISE)
    products = jnp.einsum('nihd,njhd->nhij', query_heads, key_heads, precision=PRECISE)
    scores = low_back(products * HEAD_DIM ** (-0.5) + bias_table[None])
    causal = jnp.arange(STEPS)[:, None] >= jnp.arange(STEPS)[None, :]
    attention = jax.nn.softmax(jnp.where(causal, scores, MASKED), axis=-1)
    weights = low(attention)
    mixed_heads = jnp.einsum('nhij,njhd->nihd', weights, value_heads, precision=PRECISE).reshape(normed.shape)
    return low_back(matmul(low(low_back(mixed_heads)), output_w))

def cross_block(members):
    query_heads, key_heads, value_heads, query_segment, key_segment = members
    allowed = query_segment[:, None, :, None] == key_segment[:, None, None, :]
    products = jnp.einsum('rqhd,rkhd->rhqk', query_heads, key_heads, precision=PRECISE)
    scores = jnp.where(allowed, low_back(products * HEAD_DIM ** (-0.5)), MASKED)
    log_totals = jax.nn.logsumexp(scores, axis=-1, keepdims=True)
    weights = low(jnp.exp(scores - log_totals))
    return jnp.einsum('rhqk,rkhd->rqhd', weights, value_heads, precision=PRECISE)

def cross_attend(normed, encoder, query_w, key_w, value_w, output_w, encoder_segment, slot_segment):
    activation = low(normed)
    query_all = low(low_back(matmul(activation, query_w)))
    encoder_rows = encoder.reshape(ROWS * SEQ, D)
    key_all = low(low_back(matmul(encoder_rows, key_w)))
    value_all = low(low_back(matmul(encoder_rows, value_w)))
    rows_each = math.gcd(ROWS, 4)
    block_count = ROWS // rows_each
    per_row = PAIRS * STEPS
    query_segment = jnp.repeat(slot_segment, STEPS, axis=1)
    members = (query_all.reshape(block_count, rows_each, per_row, HEADS, HEAD_DIM), key_all.reshape(block_count, rows_each, SEQ, HEADS, HEAD_DIM), value_all.reshape(block_count, rows_each, SEQ, HEADS, HEAD_DIM), query_segment.reshape(block_count, rows_each, per_row), encoder_segment.reshape(block_count, rows_each, SEQ))
    mixed_heads = lax.map(jax.checkpoint(cross_block), members).reshape(ROWS * per_row, D)
    return low_back(matmul(low(low_back(mixed_heads)), output_w))

def feed_forward(normed, input_w, output_w):
    activation = low(normed)
    pre_act = low_back(matmul(activation, input_w))
    hidden = low(gelu_curve(pre_act))
    return low_back(matmul(hidden, output_w))

def forward(decoder_in, encoder_out, self_gain, self_query, self_key, self_value, self_output, position_bias, cross_gain, cross_query, cross_key, cross_value, cross_output, feed_gain, feed_in, feed_out, score_row, encoder_segment, slot_segment, position_bucket):
    residual_one = decoder_in + self_attend(rms_norm(decoder_in, self_gain), self_query, self_key, self_value, self_output, position_bias, position_bucket)
    residual_two = residual_one + cross_attend(rms_norm(residual_one, cross_gain), encoder_out, cross_query, cross_key, cross_value, cross_output, encoder_segment, slot_segment)
    residual_three = residual_two + feed_forward(rms_norm(residual_two, feed_gain), feed_in, feed_out)
    ranking = lax.optimization_barrier(jnp.sum(residual_three * score_row, axis=-1)) * D ** (-0.5)
    return (residual_three, ranking)

def reference(decoder_in, encoder_out, encoder_segment, slot_segment, position_bucket, self_gain, self_query, self_key, self_value, self_output, position_bias, cross_gain, cross_query, cross_key, cross_value, cross_output, feed_gain, feed_in, feed_out, score_row, grad_hidden, grad_score):
    floats = tuple((member.astype(jnp.float32) for member in (decoder_in, encoder_out, self_gain, self_query, self_key, self_value, self_output, position_bias, cross_gain, cross_query, cross_key, cross_value, cross_output, feed_gain, feed_in, feed_out, score_row)))

    def closed(*values):
        return forward(*values, encoder_segment, slot_segment, position_bucket)
    (residual_three, ranking), pullback = jax.vjp(closed, *floats)
    gradients = pullback((grad_hidden, grad_score))
    return (residual_three.astype(jnp.bfloat16), ranking, gradients[0], gradients[1], gradients[2], gradients[3], gradients[4], gradients[5], gradients[6], gradients[7], gradients[8], gradients[9], gradients[10], gradients[11], gradients[12], gradients[13], gradients[14], gradients[15], gradients[16])
```

```python
import jax
import jax.numpy as jnp
from jax import lax
from jax.sharding import PartitionSpec as P

EPSILON = 1e-06
MASKED = -1e30
PRECISE = lax.Precision.HIGHEST


def rms_norm(hidden, norm_gain):
    return (
        hidden * lax.rsqrt(jnp.mean(hidden * hidden, axis=-1, keepdims=True) + EPSILON) * norm_gain
    )


def norm_back(hidden, norm_gain, upstream):
    normed, pullback = jax.vjp(rms_norm, hidden, norm_gain)
    return pullback(upstream)


def gelu_curve(values):
    return jax.nn.gelu(values, approximate=True)


def matmul(first_factor, second_factor):
    return jnp.dot(first_factor, second_factor, preferred_element_type=jnp.float32)


def contract_rows(first_factor, second_factor):
    return lax.dot_general(
        first_factor, second_factor, (((0,), (0,)), ((), ())), preferred_element_type=jnp.float32
    )


def contract_cols(first_factor, second_factor):
    return lax.dot_general(
        first_factor, second_factor, (((1,), (1,)), ((), ())), preferred_element_type=jnp.float32
    )


def masked_scores(query_heads, key_heads, query_segment, key_segment):
    products = jnp.einsum(
        "rqhd,rkhd->rhqk", query_heads, key_heads, preferred_element_type=jnp.float32
    )
    allowed = query_segment[:, None, :, None] == key_segment[:, None, None, :]
    return (jnp.where(allowed, products * query_heads.shape[-1] ** (-0.5), MASKED), allowed)


def attend_whole(query_heads, key_heads, value_heads, query_segment, key_segment):
    scores, allowed = masked_scores(query_heads, key_heads, query_segment, key_segment)
    highest = jnp.max(scores, axis=-1)
    masses = jnp.sum(jnp.where(allowed, jnp.exp(scores - highest[..., None]), 0.0), axis=-1)
    log_totals = highest + jnp.log(masses)
    weights = jnp.where(allowed, jnp.exp(scores - log_totals[..., None]), 0.0).astype(jnp.bfloat16)
    outputs = jnp.einsum(
        "rhqk,rkhd->rqhd", weights, value_heads, preferred_element_type=jnp.float32
    )
    return (outputs, log_totals)


def softmax_pieces(
    query_heads, key_heads, value_heads, grad_heads, query_segment, key_segment, log_totals
):
    scores, allowed = masked_scores(query_heads, key_heads, query_segment, key_segment)
    weights = jnp.where(allowed, jnp.exp(scores - log_totals[..., None]), 0.0)
    grad_weights = jnp.einsum(
        "rqhd,rkhd->rhqk", grad_heads, value_heads, preferred_element_type=jnp.float32
    )
    return (weights, grad_weights)


def finish_grads(query_heads, key_heads, grad_heads, weights, grad_weights, dot_sums):
    grad_scores = (weights * (grad_weights - dot_sums[..., None])).astype(jnp.bfloat16)
    score_scale = query_heads.shape[-1] ** (-0.5)
    grad_query = (
        jnp.einsum("rhqk,rkhd->rqhd", grad_scores, key_heads, preferred_element_type=jnp.float32)
        * score_scale
    )
    grad_key = (
        jnp.einsum("rhqk,rqhd->rkhd", grad_scores, query_heads, preferred_element_type=jnp.float32)
        * score_scale
    )
    grad_value = jnp.einsum(
        "rhqk,rqhd->rkhd",
        weights.astype(jnp.bfloat16),
        grad_heads,
        preferred_element_type=jnp.float32,
    )
    return (grad_query, grad_key, grad_value)


def local_grads(
    query_heads, key_heads, value_heads, grad_heads, query_segment, key_segment, log_totals
):
    weights, grad_weights = softmax_pieces(
        query_heads, key_heads, value_heads, grad_heads, query_segment, key_segment, log_totals
    )
    return finish_grads(
        query_heads,
        key_heads,
        grad_heads,
        weights,
        grad_weights,
        jnp.sum(weights * grad_weights, axis=-1),
    )


def ring_maps(dp_size, head_size):
    length = dp_size // 2

    def of(move):
        pairs = []
        for outer in range(dp_size):
            for inner in range(head_size):
                goal = move(outer, inner)
                if goal is not None:
                    pairs.append((outer * head_size + inner, goal[0] * head_size + goal[1]))
        return pairs

    def along(move):
        def step(outer, inner):
            spot = move(outer // 2)
            return None if spot is None else (spot * 2 + outer % 2, inner)

        return of(step)

    half = length // 2
    inward = [
        along(
            lambda spot, step=step: spot + 1
            if spot == step
            else (spot - 1 if spot == length - 1 - step else None)
        )
        for step in range(half - 1)
    ]
    middle = along(
        lambda spot: length - 1 - spot if spot in (half - 1, half) else None
    )
    outward = [
        along(
            lambda spot, step=step: spot - 1
            if spot == step + 1
            else (spot + 1 if spot == length - 2 - step else None)
        )
        for step in range(half - 1)
    ]
    return {
        "core": of(lambda outer, inner: (outer, inner ^ 1)),
        "chip": of(lambda outer, inner: (outer, inner ^ 2)),
        "cross": of(lambda outer, inner: (outer, inner ^ 3)),
        "pair": of(lambda outer, inner: (outer ^ 1, inner)),
        "inward": inward,
        "middle": middle,
        "outward": outward,
    }


AXES = ("dp", "head")


def add_low(first, second):
    return (first.astype(jnp.float32) + second.astype(jnp.float32)).astype(jnp.bfloat16)


def line_sum(part, maps, line):
    for perm in maps["inward"]:
        part = add_low(part, lax.ppermute(part, AXES, perm))
    part = add_low(part, lax.ppermute(part, AXES, maps["middle"]))
    length = lax.axis_size("dp") // 2
    for step in range(len(maps["outward"]) - 1, -1, -1):
        came = lax.ppermute(part, AXES, maps["outward"][step])
        takes = (line == step) | (line == length - 1 - step)
        part = jnp.where(takes, came, part)
    return part


def reduce_weight(partial, maps, place):
    chip, core, pair, line = place
    rows = partial.shape[0] // 4
    parts = partial.astype(jnp.bfloat16).reshape(2, 2, rows, partial.shape[1])
    mine = lax.dynamic_index_in_dim(parts, core, 1, keepdims=False)
    other = lax.dynamic_index_in_dim(parts, 1 - core, 1, keepdims=False)
    both = add_low(mine, lax.ppermute(other, AXES, maps["core"]))
    keep = lax.dynamic_index_in_dim(both, chip, 0, keepdims=False)
    send = lax.dynamic_index_in_dim(both, 1 - chip, 0, keepdims=False)
    group = add_low(keep, lax.ppermute(send, AXES, maps["chip"]))
    halves = group.reshape(2, rows // 2, partial.shape[1])
    keep = lax.dynamic_index_in_dim(halves, pair, 0, keepdims=False)
    send = lax.dynamic_index_in_dim(halves, 1 - pair, 0, keepdims=False)
    half = add_low(keep, lax.ppermute(send, AXES, maps["pair"]))
    total = line_sum(half, maps, line)
    came = lax.ppermute(total, AXES, maps["pair"])
    first = jnp.where(pair == 0, total, came)
    second = jnp.where(pair == 0, came, total)
    return jnp.concatenate([first, second], axis=0).astype(jnp.float32)


def body(
    decoder_in,
    encoder_out,
    encoder_segment,
    slot_segment,
    position_bucket,
    self_gain,
    self_query,
    self_key,
    self_value,
    self_output,
    position_bias,
    cross_gain,
    cross_query,
    cross_key,
    cross_value,
    cross_output,
    feed_gain,
    feed_in,
    feed_out,
    score_row,
    grad_hidden,
    grad_score,
):
    tokens = decoder_in.astype(jnp.float32)
    tok_count = tokens.shape[0]
    model_width = tokens.shape[1]
    bucket_count = position_bias.shape[0]
    head_count = position_bias.shape[1]
    head_width = model_width // head_count
    step_count = position_bucket.shape[0]
    slot_count = tok_count // step_count
    group_size = lax.axis_size("head")
    row_count = encoder_out.shape[0]
    part_len = encoder_out.shape[1]
    score_scale = head_width ** (-0.5)
    maps = ring_maps(lax.axis_size("dp"), group_size)
    head_index = lax.axis_index("head")
    dp_index = lax.axis_index("dp")
    place = (head_index // 2, head_index % 2, dp_index % 2, dp_index // 2)
    blocks = [lax.dynamic_index_in_dim(encoder_out, head_index ^ near, 0, keepdims=False) for near in range(4)]
    encoder_rows = jnp.concatenate(
        [blocks[0]]
        + [
            lax.ppermute(blocks[near], AXES, maps[name])
            for near, name in ((1, "core"), (2, "chip"), (3, "cross"))
        ],
        axis=0,
    )
    own_slots = lax.dynamic_index_in_dim(slot_segment, head_index, 0, keepdims=False)
    own_segment = lax.dynamic_index_in_dim(encoder_segment, head_index, 0, keepdims=False)
    own_segment = own_segment.reshape(group_size, part_len)
    key_segment = jnp.stack(
        [lax.dynamic_index_in_dim(own_segment, head_index ^ near, 0, keepdims=False) for near in range(4)]
    ).reshape(1, -1)

    def slot_heads(matrix):
        return matrix.reshape(slot_count, step_count, head_count, head_width)

    act_one = rms_norm(tokens, self_gain).astype(jnp.bfloat16)
    query_one = slot_heads(matmul(act_one, self_query).astype(jnp.bfloat16))
    key_one = slot_heads(matmul(act_one, self_key).astype(jnp.bfloat16))
    value_one = slot_heads(matmul(act_one, self_value).astype(jnp.bfloat16))
    onehot = (
        position_bucket[:, :, None] == jnp.arange(bucket_count, dtype=jnp.int32)[None, None, :]
    ).astype(jnp.float32)
    bias_table = jnp.einsum("ijb,bh->hij", onehot, position_bias, precision=PRECISE)
    products_one = jnp.einsum(
        "nihd,njhd->nhij", query_one, key_one, preferred_element_type=jnp.float32
    )
    causal = jnp.arange(step_count)[:, None] >= jnp.arange(step_count)[None, :]
    scores_one = jnp.where(causal, products_one * score_scale + bias_table[None], MASKED)
    shifted = jnp.exp(scores_one - jnp.max(scores_one, axis=-1, keepdims=True))
    attention_one = shifted / jnp.sum(shifted, axis=-1, keepdims=True)
    weights_one = attention_one.astype(jnp.bfloat16)
    mixed_one = jnp.einsum(
        "nhij,njhd->nihd", weights_one, value_one, preferred_element_type=jnp.float32
    )
    mixed_one = mixed_one.reshape(tok_count, model_width).astype(jnp.bfloat16)
    residual_one = tokens + matmul(mixed_one, self_output)
    act_two = rms_norm(residual_one, cross_gain).astype(jnp.bfloat16)
    query_two = matmul(act_two, cross_query).astype(jnp.bfloat16)
    key_len = group_size * part_len
    key_two = matmul(encoder_rows, cross_key).astype(jnp.bfloat16)
    value_two = matmul(encoder_rows, cross_value).astype(jnp.bfloat16)
    query_segment = jnp.repeat(own_slots, step_count)[None, :]
    local_query = query_two.reshape(1, tok_count, head_count, head_width)
    key_heads = key_two.reshape(1, key_len, head_count, head_width)
    value_heads = value_two.reshape(1, key_len, head_count, head_width)
    outputs, log_totals = attend_whole(
        local_query, key_heads, value_heads, query_segment, key_segment
    )
    mixed_two = outputs.astype(jnp.bfloat16).reshape(tok_count, model_width)
    residual_two = residual_one + matmul(mixed_two, cross_output)
    act_three = rms_norm(residual_two, feed_gain).astype(jnp.bfloat16)
    pre_act = matmul(act_three, feed_in)
    hidden_full, gelu_back = jax.vjp(gelu_curve, pre_act)
    hidden_low = hidden_full.astype(jnp.bfloat16)
    residual_three = residual_two + matmul(hidden_low, feed_out)
    row_float = score_row.astype(jnp.float32)
    ranking_score = jnp.sum(residual_three * row_float, axis=-1) * model_width ** (-0.5)
    scaled_grad = grad_score * model_width ** (-0.5)
    upstream = grad_hidden + scaled_grad[:, None] * row_float
    grad_row = jnp.sum(scaled_grad[:, None] * residual_three, axis=0)
    upstream_low = upstream.astype(jnp.bfloat16)
    grad_feed_out = contract_rows(hidden_low, upstream_low)
    grad_pre = gelu_back(contract_cols(upstream_low, feed_out))[0].astype(jnp.bfloat16)
    grad_feed_in = contract_rows(act_three, grad_pre)
    grad_norm_three, grad_feed_gain = norm_back(
        residual_two, feed_gain, contract_cols(grad_pre, feed_in)
    )
    grad_two = upstream + grad_norm_three
    grad_two_low = grad_two.astype(jnp.bfloat16)
    grad_cross_output = contract_rows(mixed_two, grad_two_low)
    grad_mixed = contract_cols(grad_two_low, cross_output).astype(jnp.bfloat16)
    grad_heads = grad_mixed.reshape(1, tok_count, head_count, head_width)
    grad_query, grad_key, grad_value = local_grads(
        local_query, key_heads, value_heads, grad_heads, query_segment, key_segment, log_totals
    )
    query_back = grad_query.astype(jnp.bfloat16).reshape(tok_count, model_width)
    key_flat = grad_key.astype(jnp.bfloat16).reshape(key_len, model_width)
    value_flat = grad_value.astype(jnp.bfloat16).reshape(key_len, model_width)
    grad_cross_query = contract_rows(act_two, query_back)
    grad_cross_key = contract_rows(encoder_rows, key_flat)
    grad_cross_value = contract_rows(encoder_rows, value_flat)
    grad_rows = contract_cols(key_flat, cross_key) + contract_cols(value_flat, cross_value)
    grad_rows = grad_rows.reshape(group_size, part_len, model_width)
    pieces = [grad_rows[0]] + [
        lax.ppermute(grad_rows[near].astype(jnp.bfloat16), AXES, maps[name]).astype(jnp.float32)
        for near, name in ((1, "core"), (2, "chip"), (3, "cross"))
    ]
    grad_encoder = jnp.zeros((row_count, part_len, model_width), jnp.float32)
    for near in range(group_size):
        grad_encoder = lax.dynamic_update_index_in_dim(
            grad_encoder, pieces[near], head_index ^ near, 0
        )
    grad_norm_two, grad_cross_gain = norm_back(
        residual_one, cross_gain, contract_cols(query_back, cross_query)
    )
    grad_one = grad_two + grad_norm_two
    grad_one_low = grad_one.astype(jnp.bfloat16)
    grad_self_output = contract_rows(mixed_one, grad_one_low)
    grad_mixed_one = slot_heads(contract_cols(grad_one_low, self_output).astype(jnp.bfloat16))
    grad_weights_one = jnp.einsum(
        "nihd,njhd->nhij", grad_mixed_one, value_one, preferred_element_type=jnp.float32
    )
    dots_one = jnp.sum(attention_one * grad_weights_one, axis=-1, keepdims=True)
    grad_scores_one = (attention_one * (grad_weights_one - dots_one)).astype(jnp.bfloat16)
    grad_bias = jnp.einsum(
        "nhij,ijb->bh", grad_scores_one.astype(jnp.float32), onehot, precision=PRECISE
    )
    query_grad_one = (
        (
            jnp.einsum(
                "nhij,njhd->nihd", grad_scores_one, key_one, preferred_element_type=jnp.float32
            )
            * score_scale
        )
        .astype(jnp.bfloat16)
        .reshape(tok_count, model_width)
    )
    key_grad_one = (
        (
            jnp.einsum(
                "nhij,nihd->njhd", grad_scores_one, query_one, preferred_element_type=jnp.float32
            )
            * score_scale
        )
        .astype(jnp.bfloat16)
        .reshape(tok_count, model_width)
    )
    value_grad_one = (
        jnp.einsum(
            "nhij,nihd->njhd", weights_one, grad_mixed_one, preferred_element_type=jnp.float32
        )
        .astype(jnp.bfloat16)
        .reshape(tok_count, model_width)
    )
    grad_self_query = contract_rows(act_one, query_grad_one)
    grad_self_key = contract_rows(act_one, key_grad_one)
    grad_self_value = contract_rows(act_one, value_grad_one)
    upstream_one = (
        contract_cols(query_grad_one, self_query)
        + contract_cols(key_grad_one, self_key)
        + contract_cols(value_grad_one, self_value)
    )
    grad_norm_one, grad_self_gain = norm_back(tokens, self_gain, upstream_one)
    grad_input = grad_one + grad_norm_one
    small = jnp.concatenate(
        [member.reshape(group_size, -1) for member in (grad_self_gain, grad_bias, grad_cross_gain, grad_feed_gain, grad_row)], axis=1
    )
    small = lax.psum(lax.psum_scatter(small, "head", scatter_dimension=0, tiled=True), "dp")[0]
    width = model_width // group_size
    bias_size = grad_bias.size // group_size
    sums = [reduce_weight(member, maps, place) for member in (
        grad_self_query, grad_self_key, grad_self_value, grad_self_output,
        grad_cross_query, grad_cross_key, grad_cross_value, grad_cross_output,
        grad_feed_in, grad_feed_out)]
    rest = width + bias_size
    return (
        residual_three.astype(jnp.bfloat16),
        ranking_score,
        grad_input,
        grad_encoder,
        small[:width],
        *sums[:4],
        small[width:rest].reshape(-1, head_count),
        small[rest : rest + width],
        *sums[4:8],
        small[rest + width : rest + 2 * width],
        *sums[8:],
        small[rest + 2 * width :],
    )


def solution(mesh):
    in_specs = (
        P(("dp", "head"), None),
        P("dp", "head", None),
        P("dp", None),
        P("dp", None),
        P(),
        P(),
        P(),
        P(),
        P(),
        P(),
        P(),
        P(),
        P(),
        P(),
        P(),
        P(),
        P(),
        P(),
        P(),
        P(),
        P(("dp", "head"), None),
        P(("dp", "head")),
    )
    out_specs = (
        P(("dp", "head"), None),
        P(("dp", "head")),
        P(("dp", "head"), None),
        P("dp", "head", None),
        P("head"),
        P("head", None),
        P("head", None),
        P("head", None),
        P("head", None),
        P("head", None),
        P("head"),
        P("head", None),
        P("head", None),
        P("head", None),
        P("head", None),
        P("head"),
        P("head", None),
        P("head", None),
        P("head"),
    )
    return jax.shard_map(body, mesh=mesh, in_specs=in_specs, out_specs=out_specs, check_vma=False)
```

```python
import functools
import jax
import jax.numpy as jnp
from jax import lax
from jax.experimental import pallas as pl
from jax.experimental.pallas import tpu as pltpu
from jax.sharding import PartitionSpec as P

EPSILON = 1e-06
MASKED = -1e30
HBM = pl.BlockSpec(memory_space=pl.ANY)
WHOLE = pl.BlockSpec(memory_space=pltpu.VMEM)
SCALARS = pl.BlockSpec(memory_space=pltpu.SMEM)
LOW = jnp.bfloat16
WIDE = jnp.float32


def shape_of(*dims, kind=LOW):
    return jax.ShapeDtypeStruct(dims, kind)


def params(megabytes=56):
    return pltpu.CompilerParams(vmem_limit_bytes=megabytes * 2**20)


def cost(flops, bytes_moved=0):
    return pl.CostEstimate(flops=flops, bytes_accessed=bytes_moved, transcendentals=0)


def mul(first, second):
    return jnp.dot(first, second, preferred_element_type=WIDE)


def mul_cols(first, second):
    return lax.dot_general(
        first, second, (((1,), (1,)), ((), ())), preferred_element_type=WIDE
    )


def mul_rows(first, second):
    return lax.dot_general(
        first, second, (((0,), (0,)), ((), ())), preferred_element_type=WIDE
    )


def inverse_root(hidden):
    return lax.rsqrt(jnp.mean(hidden * hidden, axis=-1, keepdims=True) + EPSILON)


def norm_grads(hidden, gain, upstream):
    inverse = inverse_root(hidden)
    scaled = hidden * inverse
    gain_grad = jnp.sum(upstream * scaled, axis=0, keepdims=True)
    weighted = upstream * gain
    dots = jnp.mean(weighted * scaled, axis=-1, keepdims=True)
    return inverse * (weighted - scaled * dots), gain_grad


def load_all(sources, buffers, semaphores):
    copies = [
        pltpu.make_async_copy(source, buffer, semaphores.at[spot])
        for spot, (source, buffer) in enumerate(zip(sources, buffers))
    ]
    for copy in copies:
        copy.start()
    return copies


def two_heads(pair):
    width = pair.shape[1] // 2
    lane = lax.broadcasted_iota(jnp.int32, pair.shape, 1)
    zero = jnp.zeros_like(pair)
    return jnp.concatenate(
        [jnp.where(lane < width, pair, zero), jnp.where(lane < width, zero, pair)], axis=0
    )


def bias_masks(bucket_ref, bias_ref, mask_ref, block, steps):
    buckets, heads = bias_ref.shape
    spots = bucket_ref[...]
    row = lax.broadcasted_iota(jnp.int32, (block, block), 0)
    column = lax.broadcasted_iota(jnp.int32, (block, block), 1)
    allowed = (row // steps == column // steps) & (row >= column)
    for head in range(heads):
        table = jnp.zeros(spots.shape, WIDE)
        for bucket in range(buckets):
            table = jnp.where(spots == bucket, bias_ref[bucket, head], table)
        tiled = jnp.concatenate([table] * (block // steps), axis=0)
        side = (head % 2) * block
        mask_ref[head // 2, :, side : side + block] = jnp.where(allowed, tiled, MASKED)


def pair_softmax(scores, block):
    parts = []
    for side in range(2):
        part = scores[:, side * block : (side + 1) * block]
        part = jnp.exp(part - jnp.max(part, axis=-1, keepdims=True))
        parts.append(part / jnp.sum(part, axis=-1, keepdims=True))
    return jnp.concatenate(parts, axis=1)


def self_forward_kernel(
    scale, steps, pairs, block,
    dec_ref, self_gain_ref, cross_gain_ref, bucket_ref, bias_ref,
    query_w, key_w, value_w, output_w, cross_w,
    act_one_ref, query_ref, key_ref, value_ref, mixed_ref, residual_ref, act_two_ref, query_two_ref,
    weight_buf, mask_ref, semaphores,
):
    copies = load_all(
        (query_w, key_w, value_w, output_w, cross_w), [weight_buf.at[i] for i in range(5)], semaphores
    )
    tokens = dec_ref[...].astype(WIDE)
    act_one = (tokens * inverse_root(tokens) * self_gain_ref[...]).astype(LOW)
    act_one_ref[...] = act_one
    bias_masks(bucket_ref, bias_ref, mask_ref, block, steps)
    for spot, ref in ((0, query_ref), (1, key_ref), (2, value_ref)):
        copies[spot].wait()
        ref[...] = mul(act_one, weight_buf[spot]).astype(LOW)
    for start in range(0, tokens.shape[0], block):
        for pair in range(pairs):
            rows, cols = slice(start, start + block), slice(pair * block, (pair + 1) * block)
            scores = mul_cols(query_ref[rows, cols], two_heads(key_ref[rows, cols])) * scale
            weights = pair_softmax(scores + mask_ref[pair], block).astype(LOW)
            mixed_ref[rows, cols] = mul(weights, two_heads(value_ref[rows, cols])).astype(LOW)
    copies[3].wait()
    residual = tokens + mul(mixed_ref[...], weight_buf[3])
    residual_ref[...] = residual
    act_two = (residual * inverse_root(residual) * cross_gain_ref[...]).astype(LOW)
    act_two_ref[...] = act_two
    copies[4].wait()
    query_two_ref[...] = mul(act_two, weight_buf[4]).astype(LOW)


def self_forward(dec, self_gain, cross_gain, bucket_tile, bias, query_w, key_w, value_w, output_w, cross_w, steps):
    tokens, width = dec.shape
    block = bucket_tile.shape[1]
    heads = bias.shape[1]
    low = shape_of(tokens, width)
    return pl.pallas_call(
        functools.partial(
            self_forward_kernel, (width // heads) ** (-0.5), steps, heads // 2, block
        ),
        out_shape=[low] * 5 + [shape_of(tokens, width, kind=WIDE), low, low],
        in_specs=[WHOLE] * 4 + [SCALARS] + [HBM] * 5,
        out_specs=[WHOLE] * 8,
        scratch_shapes=[
            pltpu.VMEM((5, width, width), LOW),
            pltpu.VMEM((heads // 2, block, 2 * block), WIDE),
            pltpu.SemaphoreType.DMA((5,)),
        ],
        compiler_params=params(),
        cost_estimate=cost(10 * tokens * width * width, 10 * width * width),
        name="self_forward",
    )(dec, self_gain, cross_gain, bucket_tile, bias, query_w, key_w, value_w, output_w, cross_w)


def key_value_kernel(first_ref, second_ref, key_w, value_w, key_ref, value_ref, weight_buf, semaphores):
    copies = load_all((key_w, value_w), [weight_buf.at[0], weight_buf.at[1]], semaphores)
    rows = first_ref.shape[0]
    for spot, ref in ((0, key_ref), (1, value_ref)):
        copies[spot].wait()
        ref[:rows] = mul(first_ref[...], weight_buf[spot]).astype(LOW)
        ref[rows:] = mul(second_ref[...], weight_buf[spot]).astype(LOW)


def key_value(first, second, key_w, value_w):
    rows, width = first.shape
    return pl.pallas_call(
        key_value_kernel,
        out_shape=[shape_of(2 * rows, width)] * 2,
        in_specs=[WHOLE] * 2 + [HBM] * 2,
        out_specs=[WHOLE] * 2,
        scratch_shapes=[pltpu.VMEM((2, width, width), LOW), pltpu.SemaphoreType.DMA((2,))],
        compiler_params=params(),
        cost_estimate=cost(8 * rows * width * width, 4 * width * width),
        name="key_value",
    )(first, second, key_w, value_w)


def attend_mask(key_segment_ref, query_segment_ref, mask_ref):
    count = 16
    keys = lax.broadcasted_iota(jnp.int32, (count, key_segment_ref.shape[1]), 0)
    asks = lax.broadcasted_iota(jnp.int32, (count, query_segment_ref.shape[1]), 0)
    one = jnp.ones((), WIDE)
    zero = jnp.zeros((), WIDE)
    key_hot = jnp.where(keys == key_segment_ref[...], one, zero).astype(LOW)
    ask_hot = jnp.where(asks == query_segment_ref[...], one, zero).astype(LOW)
    mask_ref[...] = jnp.where(mul_rows(key_hot, ask_hot) > 0.5, 0.0, MASKED)


def one_head(pair, side):
    width = pair.shape[1] // 2
    lane = lax.broadcasted_iota(jnp.int32, pair.shape, 1)
    return jnp.where((lane < width) == (side == 0), pair, jnp.zeros_like(pair))


def cross_forward_kernel(
    scale, pairs,
    query_ref, key_a_ref, value_a_ref, third_ref, fourth_ref, key_segment_ref, query_segment_ref,
    residual_ref, gain_ref, key_w, value_w, output_w,
    key_b_ref, value_b_ref, mixed_ref, totals_ref, residual_two_ref, act_ref,
    weight_buf, mask_ref, semaphores,
):
    copies = load_all(
        (key_w, value_w, output_w), [weight_buf.at[i] for i in range(3)], semaphores
    )
    attend_mask(key_segment_ref, query_segment_ref, mask_ref)
    rows = third_ref.shape[0]
    half = 2 * rows
    for spot, ref in ((0, key_b_ref), (1, value_b_ref)):
        copies[spot].wait()
        ref[:rows] = mul(third_ref[...], weight_buf[spot]).astype(LOW)
        ref[rows:] = mul(fourth_ref[...], weight_buf[spot]).astype(LOW)
    lanes = 128
    for pair in range(pairs):
        cols = slice(pair * lanes, (pair + 1) * lanes)
        query = query_ref[:, cols] * scale
        mixed = []
        for side in range(2):
            ask = one_head(query, side)
            scores = [
                mul_cols(ref[:, cols], ask) + mask_ref[spot * half : (spot + 1) * half]
                for spot, ref in enumerate((key_a_ref, key_b_ref))
            ]
            highest = jnp.maximum(
                jnp.max(scores[0], axis=0, keepdims=True), jnp.max(scores[1], axis=0, keepdims=True)
            )
            raised = [jnp.exp(part - highest) for part in scores]
            mass = jnp.sum(raised[0], axis=0, keepdims=True) + jnp.sum(raised[1], axis=0, keepdims=True)
            totals_ref[2 * pair + side : 2 * pair + side + 1, :] = highest + jnp.log(mass)
            inverse = 1.0 / mass
            weights = [(part * inverse).astype(LOW) for part in raised]
            mixed.append(
                mul_rows(weights[0], value_a_ref[:, cols]) + mul_rows(weights[1], value_b_ref[:, cols])
            )
        lane = lax.broadcasted_iota(jnp.int32, mixed[0].shape, 1)
        mixed_ref[:, cols] = jnp.where(lane < lanes // 2, mixed[0], mixed[1]).astype(LOW)
    copies[2].wait()
    residual = residual_ref[...] + mul(mixed_ref[...], weight_buf[2])
    residual_two_ref[...] = residual
    act_ref[...] = (residual * inverse_root(residual) * gain_ref[...]).astype(LOW)


def cross_forward(query, key_a, value_a, third, fourth, key_segment, query_segment, residual, gain, key_w, value_w, output_w, heads):
    tokens, width = query.shape
    rows = third.shape[0]
    keys = 4 * rows
    return pl.pallas_call(
        functools.partial(cross_forward_kernel, (width // heads) ** (-0.5), heads // 2),
        out_shape=[
            shape_of(2 * rows, width), shape_of(2 * rows, width), shape_of(tokens, width),
            shape_of(heads, tokens, kind=WIDE), shape_of(tokens, width, kind=WIDE), shape_of(tokens, width),
        ],
        in_specs=[WHOLE] * 9 + [HBM] * 3,
        out_specs=[WHOLE] * 6,
        scratch_shapes=[
            pltpu.VMEM((3, width, width), LOW),
            pltpu.VMEM((keys, tokens), WIDE),
            pltpu.SemaphoreType.DMA((3,)),
        ],
        compiler_params=params(),
        cost_estimate=cost(8 * rows * width * width + 8 * tokens * keys * width + 2 * tokens * width * width, 6 * width * width),
        name="cross_forward",
    )(query, key_a, value_a, third, fourth, key_segment, query_segment, residual, gain, key_w, value_w, output_w)


def feed_kernel(
    order_ref,
    act_ref, upstream_low_ref, residual_ref, grad_hidden_ref, grad_score_ref, row_ref, gain_ref,
    in_ref, out_ref, cross_w,
    hidden_other_ref, hidden_mine_ref, grad_pre_ref,
    result_ref, ranking_ref, row_grad_ref, gain_grad_ref, grad_two_ref, grad_two_low_ref, grad_mixed_ref,
    total, upward, cross_buf, semaphore,
):
    step = pl.program_id(0)
    copy = pltpu.make_async_copy(cross_w, cross_buf, semaphore)

    @pl.when(step == 0)
    def _():
        copy.start()
        total[...] = jnp.zeros_like(total)
        upward[...] = jnp.zeros_like(upward)

    pre = mul(act_ref[...], in_ref[...])
    root = 0.7978845608028654
    square = pre * pre
    curve = jnp.tanh(root * (pre + 0.044715 * (square * pre)))
    ahead = 0.5 * (1.0 + curve)
    hidden = (pre * ahead).astype(LOW)
    slope = ahead + (0.5 * root) * pre * (1.0 - curve * curve) * (1.0 + (3 * 0.044715) * square)
    grad_pre = (mul_cols(upstream_low_ref[...], out_ref[...]) * slope).astype(LOW)
    grad_pre_ref[...] = grad_pre

    @pl.when(step < 2)
    def _():
        hidden_other_ref[0] = hidden

    @pl.when(step >= 2)
    def _():
        hidden_mine_ref[0] = hidden

    total[...] += mul(hidden, out_ref[...])
    upward[...] += mul_cols(grad_pre, in_ref[...])

    @pl.when(step == pl.num_programs(0) - 1)
    def _():
        residual = residual_ref[...]
        row = row_ref[...]
        factor = row.shape[1] ** (-0.5)
        final = residual + total[...]
        result_ref[...] = final.astype(LOW)
        ranking_ref[...] = jnp.sum(final * row, axis=-1, keepdims=True) * factor
        scaled = grad_score_ref[...] * factor
        row_grad_ref[...] = jnp.sum(scaled * final, axis=0, keepdims=True)
        back, gain_grad = norm_grads(residual, gain_ref[...], upward[...])
        gain_grad_ref[...] = gain_grad
        grad_two = grad_hidden_ref[...] + scaled * row + back
        grad_two_ref[...] = grad_two
        grad_two_low = grad_two.astype(LOW)
        grad_two_low_ref[...] = grad_two_low
        copy.wait()
        grad_mixed_ref[...] = mul_cols(grad_two_low, cross_buf[...]).astype(LOW)


def feed(order, act, upstream_low, residual, grad_hidden, grad_score, row, gain, feed_in, feed_out, cross_output):
    tokens, width = act.shape
    hidden = feed_in.shape[1]
    part = hidden // 4
    whole = lambda *dims: pl.BlockSpec(dims, lambda step, order: (0,) * len(dims))
    full = whole(tokens, width)
    return pl.pallas_call(
        feed_kernel,
        grid_spec=pltpu.PrefetchScalarGridSpec(
            num_scalar_prefetch=1,
            grid=(4,),
            in_specs=[
                full, full, full, full, whole(tokens, 1), whole(1, width), whole(1, width),
                pl.BlockSpec((width, part), lambda step, order: (0, order[step])),
                pl.BlockSpec((part, width), lambda step, order: (order[step], 0)),
                HBM,
            ],
            out_specs=[
                pl.BlockSpec((1, tokens, part), lambda step, order: (jnp.minimum(step, 1), 0, 0)),
                pl.BlockSpec((1, tokens, part), lambda step, order: (jnp.maximum(step - 2, 0), 0, 0)),
                pl.BlockSpec((tokens, part), lambda step, order: (0, order[step])),
                full, whole(tokens, 1), whole(1, width), whole(1, width), full, full, full,
            ],
            scratch_shapes=[
                pltpu.VMEM((tokens, width), WIDE),
                pltpu.VMEM((tokens, width), WIDE),
                pltpu.VMEM((width, width), LOW),
                pltpu.SemaphoreType.DMA,
            ],
        ),
        out_shape=[
            shape_of(2, tokens, part), shape_of(2, tokens, part), shape_of(tokens, hidden),
            shape_of(tokens, width), shape_of(tokens, 1, kind=WIDE), shape_of(1, width, kind=WIDE),
            shape_of(1, width, kind=WIDE), shape_of(tokens, width, kind=WIDE), shape_of(tokens, width),
            shape_of(tokens, width),
        ],
        compiler_params=params(),
        cost_estimate=cost(8 * tokens * width * hidden, 4 * width * hidden),
        name="feed",
    )(order, act, upstream_low, residual, grad_hidden, grad_score, row, gain, feed_in, feed_out, cross_output)


def cross_backward_kernel(
    scale, pairs,
    query_ref, key_a_ref, value_a_ref, key_b_ref, value_b_ref, totals_ref, grad_mixed_ref,
    key_segment_ref, query_segment_ref, residual_ref, gain_ref, grad_two_ref, query_w, key_w, value_w, output_w,
    grad_query_ref, grad_key_ref, grad_value_ref, grad_own_ref, grad_core_ref, grad_chip_ref, grad_far_ref,
    grad_one_ref, grad_one_low_ref, grad_mixed_one_ref, gain_grad_ref,
    weight_buf, mask_ref, semaphores,
):
    copies = load_all(
        (query_w, output_w, key_w, value_w), [weight_buf.at[i] for i in range(4)], semaphores
    )
    attend_mask(key_segment_ref, query_segment_ref, mask_ref)
    half = key_a_ref.shape[0]
    lanes = 128
    for pair in range(pairs):
        cols = slice(pair * lanes, (pair + 1) * lanes)
        query = query_ref[:, cols] * scale
        keys = (key_a_ref, key_b_ref)
        values = (value_a_ref, value_b_ref)
        query_parts = []
        key_parts = [[], []]
        value_parts = [[], []]
        for side in range(2):
            ask = one_head(query, side)
            grad = one_head(grad_mixed_ref[:, cols], side)
            head = 2 * pair + side
            total = totals_ref[head : head + 1, :]
            weights, grad_weights = [], []
            for spot in range(2):
                rows = slice(spot * half, (spot + 1) * half)
                scores = mul_cols(keys[spot][:, cols], ask) + mask_ref[rows]
                weights.append(jnp.exp(scores - total))
                grad_weights.append(mul_cols(values[spot][:, cols], grad))
            dots = sum(
                jnp.sum(one * other, axis=0, keepdims=True) for one, other in zip(weights, grad_weights)
            )
            part = 0.0
            for spot in range(2):
                grad_scores = (weights[spot] * (grad_weights[spot] - dots)).astype(LOW)
                part += mul_rows(grad_scores, keys[spot][:, cols])
                key_parts[spot].append(mul(grad_scores, ask))
                value_parts[spot].append(mul(weights[spot].astype(LOW), grad))
            query_parts.append(part)
        lane = lax.broadcasted_iota(jnp.int32, query_parts[0].shape, 1)
        grad_query_ref[:, cols] = (
            jnp.where(lane < lanes // 2, query_parts[0], query_parts[1]) * scale
        ).astype(LOW)
        for spot in range(2):
            rows = slice(spot * half, (spot + 1) * half)
            grad_key_ref[rows, cols] = (key_parts[spot][0] + key_parts[spot][1]).astype(LOW)
            grad_value_ref[rows, cols] = (value_parts[spot][0] + value_parts[spot][1]).astype(LOW)
    copies[0].wait()
    back, gain_grad = norm_grads(
        residual_ref[...], gain_ref[...], mul_cols(grad_query_ref[...], weight_buf[0])
    )
    gain_grad_ref[...] = gain_grad
    grad_one = grad_two_ref[...] + back
    grad_one_ref[...] = grad_one
    grad_one_low = grad_one.astype(LOW)
    grad_one_low_ref[...] = grad_one_low
    copies[1].wait()
    grad_mixed_one_ref[...] = mul_cols(grad_one_low, weight_buf[1]).astype(LOW)
    copies[2].wait()
    copies[3].wait()
    rows = half // 2
    for spot in (3, 2, 1, 0):
        part = slice(spot * rows, (spot + 1) * rows)
        grad = mul_cols(grad_key_ref[part], weight_buf[2]) + mul_cols(grad_value_ref[part], weight_buf[3])
        if spot == 0:
            grad_own_ref[...] = grad
        else:
            (grad_core_ref, grad_chip_ref, grad_far_ref)[spot - 1][...] = grad.astype(LOW)


def cross_backward(query, key_a, value_a, key_b, value_b, totals, grad_mixed, key_segment, query_segment, residual, gain, grad_two, query_w, key_w, value_w, output_w):
    tokens, width = query.shape
    heads = totals.shape[0]
    keys = 2 * key_a.shape[0]
    low, wide, tall = shape_of(tokens, width), shape_of(tokens, width, kind=WIDE), shape_of(keys, width)
    return pl.pallas_call(
        functools.partial(cross_backward_kernel, (width // heads) ** (-0.5), heads // 2),
        out_shape=[
            low, tall, tall, shape_of(keys // 4, width, kind=WIDE), *[shape_of(keys // 4, width)] * 3,
            wide, low, low, shape_of(1, width, kind=WIDE),
        ],
        in_specs=[WHOLE] * 12 + [HBM] * 4,
        out_specs=[WHOLE] * 11,
        scratch_shapes=[
            pltpu.VMEM((4, width, width), LOW),
            pltpu.VMEM((keys, tokens), WIDE),
            pltpu.SemaphoreType.DMA((4,)),
        ],
        compiler_params=params(),
        cost_estimate=cost(4 * keys * width * width + 20 * tokens * keys * width + 4 * tokens * width * width, 8 * width * width),
        name="cross_backward",
    )(query, key_a, value_a, key_b, value_b, totals, grad_mixed, key_segment, query_segment, residual, gain, grad_two, query_w, key_w, value_w, output_w)


def self_backward_kernel(
    scale, steps, pairs, block,
    query_ref, key_ref, value_ref, grad_mixed_ref, dec_ref, gain_ref, grad_one_ref, bucket_ref, bias_ref,
    query_w, key_w, value_w,
    grads_ref, result_ref, gain_grad_ref, bias_grad_ref,
    weight_buf, mask_ref, table_ref, semaphores,
):
    copies = load_all((query_w, key_w, value_w), [weight_buf.at[i] for i in range(3)], semaphores)
    bias_masks(bucket_ref, bias_ref, mask_ref, block, steps)
    for pair in range(pairs):
        table = jnp.zeros((steps, 2 * block), WIDE)
        for start in range(0, dec_ref.shape[0], block):
            rows, cols = slice(start, start + block), slice(pair * block, (pair + 1) * block)
            query, keys, values = query_ref[rows, cols], two_heads(key_ref[rows, cols]), two_heads(value_ref[rows, cols])
            grad = grad_mixed_ref[rows, cols]
            weights = pair_softmax(mul_cols(query, keys) * scale + mask_ref[pair], block)
            grad_weights = mul_cols(grad, values)
            product = weights * grad_weights
            grad_scores = jnp.concatenate(
                [
                    product[:, side * block : (side + 1) * block]
                    - weights[:, side * block : (side + 1) * block]
                    * jnp.sum(product[:, side * block : (side + 1) * block], axis=-1, keepdims=True)
                    for side in range(2)
                ],
                axis=1,
            ).astype(LOW)
            table += jnp.sum(grad_scores.astype(WIDE).reshape(block // steps, steps, 2 * block), axis=0)
            grads_ref[0, rows, cols] = (mul(grad_scores, keys) * scale).astype(LOW)
            key_parts = mul_rows(grad_scores, query)
            value_parts = mul_rows(weights.astype(LOW), grad)
            lane = lax.broadcasted_iota(jnp.int32, (block, block), 1) < block // 2
            grads_ref[1, rows, cols] = (
                jnp.where(lane, key_parts[:block], key_parts[block:]) * scale
            ).astype(LOW)
            grads_ref[2, rows, cols] = jnp.where(lane, value_parts[:block], value_parts[block:]).astype(LOW)
        table_ref[pair] = table
    spots = bucket_ref[...]
    for bucket in range(bias_ref.shape[0]):
        hit = jnp.concatenate([spots == bucket] * 2, axis=1)
        for pair in range(pairs):
            kept = jnp.sum(jnp.where(hit, table_ref[pair], 0.0), axis=0, keepdims=True)
            bias_grad_ref[2 * pair, bucket : bucket + 1, :] = kept[:, :block]
            bias_grad_ref[2 * pair + 1, bucket : bucket + 1, :] = kept[:, block:]
    upward = 0.0
    for spot in range(3):
        copies[spot].wait()
        upward += mul_cols(grads_ref[spot], weight_buf[spot])
    back, gain_grad = norm_grads(dec_ref[...].astype(WIDE), gain_ref[...], upward)
    gain_grad_ref[...] = gain_grad
    result_ref[...] = grad_one_ref[...] + back


def self_backward(query, key, value, grad_mixed, dec, gain, grad_one, bucket_tile, bias, query_w, key_w, value_w, steps):
    tokens, width = query.shape
    buckets, heads = bias.shape
    block = bucket_tile.shape[1]
    return pl.pallas_call(
        functools.partial(self_backward_kernel, (width // heads) ** (-0.5), steps, heads // 2, block),
        out_shape=[shape_of(3, tokens, width), shape_of(tokens, width, kind=WIDE), shape_of(1, width, kind=WIDE), shape_of(heads, buckets, block, kind=WIDE)],
        in_specs=[WHOLE] * 8 + [SCALARS] + [HBM] * 3,
        out_specs=[WHOLE] * 4,
        scratch_shapes=[
            pltpu.VMEM((3, width, width), LOW),
            pltpu.VMEM((heads // 2, block, 2 * block), WIDE),
            pltpu.VMEM((heads // 2, steps, 2 * block), WIDE),
            pltpu.SemaphoreType.DMA((3,)),
        ],
        compiler_params=params(),
        cost_estimate=cost(6 * tokens * width * width, 6 * width * width),
        name="self_backward",
    )(query, key, value, grad_mixed, dec, gain, grad_one, bucket_tile, bias, query_w, key_w, value_w)


def pack_kernel(count, core_ref, *refs):
    sources, others, mines = refs[:count], refs[count : 2 * count], refs[2 * count :]
    first = core_ref[0] == 0
    for source, other, mine in zip(sources, others, mines):
        quarter = source.shape[1] // 4
        parts = [source[:, spot * quarter : (spot + 1) * quarter] for spot in range(4)]
        for chip in range(2):
            even, odd = parts[2 * chip], parts[2 * chip + 1]
            mine[chip] = jnp.where(first, even, odd)
            other[chip] = jnp.where(first, odd, even)


def pack(core, sources):
    count = len(sources)
    shapes = [shape_of(2, source.shape[0], source.shape[1] // 4) for source in sources]
    results = pl.pallas_call(
        functools.partial(pack_kernel, count),
        out_shape=shapes * 2,
        in_specs=[SCALARS] + [WHOLE] * count,
        out_specs=[WHOLE] * (2 * count),
        compiler_params=params(),
        cost_estimate=cost(0, 4 * sum(source.size for source in sources)),
        name="pack",
    )(core, *sources)
    return results[:count], results[count:]


def weight_kernel(terms, sums, ends, pick_ref, *refs):
    total = 0.0
    for spot in range(terms):
        total += mul_rows(refs[2 * spot][0], refs[2 * spot + 1][0])
    for ref in refs[2 * terms : 2 * terms + sums]:
        total += ref[...].reshape(ref.shape[-2:]).astype(WIDE)
    outs = refs[2 * terms + sums :]
    total = total.astype(LOW)
    if ends == 1:
        outs[0][0, 0] = total
    else:
        for spot in range(2):

            @pl.when(pl.program_id(1) == spot)
            def _():
                outs[spot][0] = total


def weight_parts(pick, terms, sums, ends):
    arrays, specs = [], []
    for factors, grads, block in terms:
        if factors.ndim == 3:
            factors = factors[None]
        count, _, rows, size = factors.shape
        half = grads.shape[2] // 2
        arrays += [factors.reshape((-1,) + factors.shape[2:]), grads]
        single = count == 1
        specs += [
            pl.BlockSpec((1, rows, size), lambda w, j, p, single=single: ((0 if single else 2 * w) + p[3 * j], 0, 0)),
            pl.BlockSpec((1, rows, half), lambda w, j, p, block=block: (w, block, p[3 * j + 1])),
        ]
    weights = terms[0][1].shape[0]
    flops = sum(4 * weights * factors.shape[-1] * factors.shape[-2] * half for factors, _, _ in terms)
    for member in sums:
        arrays.append(member)
        if member.shape[-1] == half:
            specs.append(pl.BlockSpec((1, 1, size, half), lambda w, j, p: (w, p[3 * j + 2], 0, 0)))
        else:
            specs.append(pl.BlockSpec((1, 1, size, half), lambda w, j, p: (w, p[3 * j], 0, p[3 * j + 1])))
    if ends == 1:
        out_shape = [shape_of(weights, 2, size, half)]
        out_specs = [pl.BlockSpec((1, 1, size, half), lambda w, j, p: (w, j, 0, 0))]
    else:
        out_shape = [shape_of(weights, size, half)] * 2
        out_specs = [pl.BlockSpec((1, size, half), lambda w, j, p: (w, 0, 0))] * 2
    return pl.pallas_call(
        functools.partial(weight_kernel, len(terms), len(sums), ends),
        grid_spec=pltpu.PrefetchScalarGridSpec(
            num_scalar_prefetch=1, grid=(weights, 2), in_specs=specs, out_specs=out_specs
        ),
        out_shape=out_shape,
        compiler_params=params(),
        cost_estimate=cost(flops, 4 * weights * size * half),
        name="weight_parts",
    )(pick, *arrays)


def place_rows_kernel(head_ref, own_ref, core_ref, chip_ref, far_ref, out_ref):
    for spot, ref in enumerate((own_ref, core_ref, chip_ref, far_ref)):

        @pl.when(pl.program_id(0) == spot)
        def _():
            out_ref[0] = ref[...].astype(WIDE)


def place_rows(head, own, core, chip, far):
    rows, width = own.shape
    return pl.pallas_call(
        place_rows_kernel,
        grid_spec=pltpu.PrefetchScalarGridSpec(
            num_scalar_prefetch=1,
            grid=(4,),
            in_specs=[pl.BlockSpec((rows, width), lambda step, head: (0, 0))] * 4,
            out_specs=pl.BlockSpec((1, rows, width), lambda step, head: (head[0] ^ step, 0, 0)),
        ),
        out_shape=shape_of(4, rows, width, kind=WIDE),
        compiler_params=params(),
        cost_estimate=cost(0, 24 * rows * width),
        name="place_rows",
    )(head, own, core, chip, far)


def weight_whole_kernel(terms, *refs):
    total = 0.0
    for spot in range(terms):
        total += mul_rows(refs[2 * spot][0], refs[2 * spot + 1][0])
    refs[-1][0, 0] = total.astype(LOW)


def weight_whole(terms):
    arrays, specs = [], []
    for factors, grads, block in terms:
        _, rows, size = factors.shape
        weights, _, width = grads.shape
        arrays += [factors, grads]
        specs += [
            pl.BlockSpec((1, rows, size), lambda w, j: (j, 0, 0)),
            pl.BlockSpec((1, rows, width), lambda w, j, block=block: (w, block, 0)),
        ]
    return pl.pallas_call(
        functools.partial(weight_whole_kernel, len(terms)),
        grid=(weights, 2),
        in_specs=specs,
        out_specs=pl.BlockSpec((1, 1, size, width), lambda w, j: (w, j, 0, 0)),
        out_shape=shape_of(weights, 2, size, width),
        compiler_params=params(),
        cost_estimate=cost(len(terms) * 4 * weights * rows * size * width, 4 * weights * size * width),
        name="weight_whole",
    )(*arrays)


AXES = ("dp", "head")


def device_maps(dp_size, head_size):
    length = dp_size // 2
    half = length // 2

    def of(move):
        pairs = []
        for outer in range(dp_size):
            for inner in range(head_size):
                goal = move(outer // 2, outer % 2, inner)
                if goal is not None:
                    spot, side, place = goal
                    pairs.append(
                        (outer * head_size + inner, (2 * spot + side) * head_size + place)
                    )
        return pairs

    def along(first, first_goal):
        def step(spot, side, place):
            if spot == first:
                return (first_goal, side, place)
            if spot == length - 1 - first:
                return (length - 1 - first_goal, side, place)
            return None

        return of(step)

    return {
        "core": of(lambda spot, side, place: (spot, side, place ^ 1)),
        "chip": of(lambda spot, side, place: (spot, side, place ^ 2)),
        "far": of(lambda spot, side, place: (spot, side, place ^ 3)),
        "pair": of(lambda spot, side, place: (spot, 1 - side, place)),
        "middle_pair": of(
            lambda spot, side, place: (spot, 1 - side, place) if spot in (half - 1, half) else None
        ),
        "inward": [along(step, step + 1) for step in range(half - 1)],
        "middle": along(half - 1, half),
        "outward": [along(step + 1, step) for step in range(half - 1)],
    }


class Place:
    def __init__(self):
        dp_size, head_size = lax.axis_size("dp"), lax.axis_size("head")
        self.maps = device_maps(dp_size, head_size)
        self.length = dp_size // 2
        self.head = lax.axis_index("head")
        self.chip, self.core = self.head // 2, self.head % 2
        dp_index = lax.axis_index("dp")
        self.pair, self.line = dp_index % 2, dp_index // 2

    def move(self, array, name):
        return lax.ppermute(array, AXES, self.maps[name])

    def inward(self, part):
        for perm in self.maps["inward"]:
            part = add_low(part, lax.ppermute(part, AXES, perm))
        return part

    def outward(self, part):
        for step in range(len(self.maps["outward"]) - 1, -1, -1):
            came = lax.ppermute(part, AXES, self.maps["outward"][step])
            takes = (self.line == step) | (self.line == self.length - 1 - step)
            part = jnp.where(takes, came, part)
        return part


def add_low(first, second):
    kind = first.dtype
    return (first.astype(jnp.float32) + second.astype(jnp.float32)).astype(kind)


def picks(*values):
    return jnp.stack([jnp.asarray(value, jnp.int32) for value in values])


def finish(place, part):
    part = place.inward(part)
    part = add_low(part, place.move(part, "middle"))
    part = place.outward(part)
    came = place.move(part, "pair")
    first = jnp.where(place.pair == 0, part, came)
    second = jnp.where(place.pair == 0, came, part)
    return jnp.concatenate([first, second], axis=-1).astype(jnp.float32)


def finish_whole(place, parts):
    parts = place.inward(parts)
    left = place.line < place.length // 2
    mine = jnp.where(left, parts[:, 0], parts[:, 1])
    other = jnp.where(left, parts[:, 1], parts[:, 0])
    mine = add_low(mine, place.move(other, "middle"))
    mine = add_low(mine, place.move(mine, "middle_pair"))
    came = place.move(mine, "middle")
    parts = jnp.stack([jnp.where(left, mine, came), jnp.where(left, came, mine)], axis=1)
    parts = place.outward(parts)
    return jnp.concatenate([parts[:, 0], parts[:, 1]], axis=-1).astype(jnp.float32)


def reduce_weights(place, terms, sums, mode):
    chip, pair = place.chip, place.pair
    if mode == "chip":
        (sent,) = weight_parts(picks(1 - chip, 0, 0, 1 - chip, 1, 1), terms, sums, 1)
        came = place.move(sent, "chip")
        give, keep = weight_parts(
            picks(chip, 1 - pair, 1 - pair, chip, pair, pair), terms, sums + [came], 2
        )
        return finish(place, add_low(keep, place.move(give, "pair")))
    if mode == "pair":
        (sent,) = weight_parts(picks(0, 1 - pair, 0, 1, 1 - pair, 1), terms, sums, 1)
        came = place.move(sent, "pair")
        give, keep = weight_parts(
            picks(1 - chip, pair, 1 - chip, chip, pair, chip), terms, sums + [came], 2
        )
        return finish(place, add_low(keep, place.move(give, "chip")))
    (sent,) = weight_parts(picks(1 - chip, 0, 0, 1 - chip, 1, 1), terms, sums, 1)
    came = place.move(sent, "chip")
    (both,) = weight_parts(picks(chip, 0, 0, chip, 1, 1), terms, sums + [came], 1)
    return finish_whole(place, both)


def sum_everywhere(place, values):
    for name in ("core", "chip", "pair"):
        values = values + place.move(values, name)
    values = place.inward(values)
    values = values + place.move(values, "middle")
    return place.outward(values)


def body(
    decoder_in,
    encoder_out,
    encoder_segment,
    slot_segment,
    position_bucket,
    self_gain,
    self_query,
    self_key,
    self_value,
    self_output,
    position_bias,
    cross_gain,
    cross_query,
    cross_key,
    cross_value,
    cross_output,
    feed_gain,
    feed_in,
    feed_out,
    score_row,
    grad_hidden,
    grad_score,
):
    place = Place()
    model_width = decoder_in.shape[1]
    heads = position_bias.shape[1]
    steps = position_bucket.shape[0]
    head_index, core = place.head, place.core
    core_list = picks(core)

    blocks = [
        lax.dynamic_index_in_dim(encoder_out, head_index ^ near, 0, keepdims=False)
        for near in range(4)
    ]
    rows = [blocks[0]] + [
        place.move(blocks[near], name) for near, name in ((2, "chip"), (3, "far"), (1, "core"))
    ]
    rows = [rows[0], rows[3], rows[1], rows[2]]
    own_segment = lax.dynamic_index_in_dim(encoder_segment, head_index, 0, keepdims=False)
    own_segment = own_segment.reshape(4, -1)
    key_segment = jnp.concatenate(
        [lax.dynamic_index_in_dim(own_segment, head_index ^ near, 0) for near in range(4)], axis=1
    )
    own_slots = lax.dynamic_index_in_dim(slot_segment, head_index, 0, keepdims=False)
    query_segment = jnp.repeat(own_slots, steps)[None, :]
    bucket_tile = jnp.tile(position_bucket, (1, 128 // steps))
    row_wide = score_row.astype(jnp.float32)[None, :]
    scaled = grad_score[:, None] * model_width ** (-0.5)
    upstream_low = (grad_hidden + scaled * row_wide).astype(jnp.bfloat16)
    upstream_came = place.move(upstream_low, "core")

    act_one, query_one, key_one, value_one, mixed_one, residual_one, act_two, query_two = self_forward(
        decoder_in, self_gain[None], cross_gain[None], bucket_tile, position_bias,
        self_query, self_key, self_value, self_output, cross_query, steps,
    )
    key_a, value_a = key_value(rows[0], rows[1], cross_key, cross_value)
    early_other, early_mine = pack(core_list, [act_one, mixed_one, act_two])
    early_came = [place.move(member, "core") for member in early_other]
    key_b, value_b, mixed_two, totals, residual_two, act_three = cross_forward(
        query_two, key_a, value_a, rows[2], rows[3], key_segment, query_segment,
        residual_one, feed_gain[None], cross_key, cross_value, cross_output, heads,
    )
    (
        hidden_other, hidden_mine, grad_pre, hidden_out, ranking, row_grad, feed_gain_grad,
        grad_two, grad_two_low, grad_mixed,
    ) = feed(
        picks(1 - core, 3 - core, core, 2 + core),
        act_three, upstream_low, residual_two, grad_hidden, grad_score[:, None], row_wide,
        feed_gain[None], feed_in, feed_out, cross_output,
    )
    hidden_came = place.move(hidden_other, "core")
    grad_pre_came = place.move(grad_pre, "core")
    late_other, late_mine = pack(core_list, [act_three, mixed_two])
    late_came = [place.move(member, "core") for member in late_other]
    feed_out_grad = reduce_weights(
        place,
        [(hidden_mine, upstream_low[None], 0), (hidden_came, upstream_came[None], 0)],
        [],
        MODES["feed_out"],
    )[0]
    feed_in_grad = reduce_weights(
        place,
        [(late_mine[0], grad_pre[None], 0), (late_came[0], grad_pre_came[None], 0)],
        [],
        MODES["feed_in"],
    )[0]
    grad_two_came = place.move(grad_two_low, "core")
    cross_output_grad = reduce_weights(
        place,
        [(late_mine[1], grad_two_low[None], 0), (late_came[1], grad_two_came[None], 0)],
        [],
        MODES["cross_output"],
    )[0]
    (
        grad_query_two, grad_key_two, grad_value_two, row_own, row_core, row_chip, row_far,
        grad_one, grad_one_low, grad_mixed_one, cross_gain_grad,
    ) = cross_backward(
        query_two, key_a, value_a, key_b, value_b, totals, grad_mixed, key_segment, query_segment,
        residual_one, cross_gain[None], grad_two, cross_query, cross_key, cross_value, self_output,
    )
    encoder_grad = place_rows(
        picks(head_index),
        row_own,
        place.move(row_core, "core"),
        place.move(row_chip, "chip"),
        place.move(row_far, "far"),
    )
    query_out = jnp.stack([grad_query_two, grad_one_low])
    query_out_came = place.move(query_out, "core")
    cross_query_grad, self_output_grad = reduce_weights(
        place,
        [
            (jnp.stack([early_mine[2], early_mine[1]]), query_out, 0),
            (jnp.stack([early_came[2], early_came[1]]), query_out_came, 0),
        ],
        [],
        MODES["query_out"],
    )
    row_other, row_mine = pack(core_list, rows)
    key_value_grads = jnp.stack([grad_key_two, grad_value_two])
    key_value_part = weight_whole([(member, key_value_grads, spot) for spot, member in enumerate(row_other)])
    key_value_came = place.move(key_value_part, "core")
    cross_key_grad, cross_value_grad = reduce_weights(
        place,
        [(member, key_value_grads, spot) for spot, member in enumerate(row_mine)],
        [key_value_came],
        MODES["key_value"],
    )
    self_grads, decoder_grad, self_gain_grad, bias_grad = self_backward(
        query_one, key_one, value_one, grad_mixed_one, decoder_in, self_gain[None], grad_one,
        bucket_tile, position_bias, self_query, self_key, self_value, steps,
    )
    self_came = place.move(self_grads, "core")
    self_query_grad, self_key_grad, self_value_grad = reduce_weights(
        place,
        [(early_mine[0], self_grads, 0), (early_came[0], self_came, 0)],
        [],
        MODES["self"],
    )
    bias_grad = jnp.sum(bias_grad, axis=-1).T
    small = jnp.concatenate(
        [
            member.reshape(4, -1)
            for member in (self_gain_grad, bias_grad, cross_gain_grad, feed_gain_grad, row_grad)
        ],
        axis=1,
    )
    small = lax.dynamic_index_in_dim(sum_everywhere(place, small), head_index, 0, keepdims=False)
    width = model_width // 4
    rest = width + bias_grad.size // 4
    return (
        hidden_out,
        ranking[:, 0],
        decoder_grad,
        encoder_grad,
        small[:width],
        self_query_grad,
        self_key_grad,
        self_value_grad,
        self_output_grad,
        small[width:rest].reshape(-1, heads),
        small[rest : rest + width],
        cross_query_grad,
        cross_key_grad,
        cross_value_grad,
        cross_output_grad,
        small[rest + width : rest + 2 * width],
        feed_in_grad,
        feed_out_grad,
        small[rest + 2 * width :],
    )


MODES = {
    "feed_out": "whole",
    "feed_in": "pair",
    "cross_output": "chip",
    "query_out": "chip",
    "key_value": "whole",
    "self": "chip",
}


def solution(mesh):
    in_specs = (
        P(("dp", "head"), None),
        P("dp", "head", None),
        P("dp", None),
        P("dp", None),
        P(),
        P(),
        P(),
        P(),
        P(),
        P(),
        P(),
        P(),
        P(),
        P(),
        P(),
        P(),
        P(),
        P(),
        P(),
        P(),
        P(("dp", "head"), None),
        P(("dp", "head")),
    )
    out_specs = (
        P(("dp", "head"), None),
        P(("dp", "head")),
        P(("dp", "head"), None),
        P("dp", "head", None),
        P("head"),
        P("head", None),
        P("head", None),
        P("head", None),
        P("head", None),
        P("head", None),
        P("head"),
        P("head", None),
        P("head", None),
        P("head", None),
        P("head", None),
        P("head"),
        P("head", None),
        P("head", None),
        P("head"),
    )
    return jax.shard_map(body, mesh=mesh, in_specs=in_specs, out_specs=out_specs, check_vma=False)
```

```python
import functools
import jax
import jax.numpy as jnp
from jax import lax
from jax.experimental import pallas as pl
from jax.experimental.pallas import tpu as pltpu
from jax.sharding import PartitionSpec as P

EPSILON = 1e-06
MASKED = -1e30
HBM = pl.BlockSpec(memory_space=pl.ANY)
VMEM = pl.BlockSpec(memory_space=pltpu.VMEM)
SCALARS = pl.BlockSpec(memory_space=pltpu.SMEM)
LOW = jnp.bfloat16
BLOCK = 128
CHIP, PAIR, WHOLE, CORE, FAR, MIDDLE, MIDDLE_PAIR, INWARD, OUTWARD = range(9)
SECOND, SPLIT, ADD, JOIN, LINES, ADD_INWARD, ADD_MIDDLE, ADD_OUTWARD, TAKE, COLUMNS = range(10)
ADDS = (ADD_INWARD, ADD_MIDDLE, ADD_OUTWARD)
NAMES = {SPLIT: "combine_split", ADD: "combine_add", JOIN: "combine_join", LINES: "combine_rows"}
NAMES.update({TAKE: "combine_take", COLUMNS: "combine_columns"})
(
    OUT, IN, ASK, SELF, KEEP, BACK, SELF_PASS, SELF_COPY, ENCODER, KEEP_PASS, KEEP_COPY, NEED_KEEP, ASK_FIRST,
    SELF_FIRST, KEEP_FIRST, ROWS, ROWS_SEND, ROWS_PASS, ROWS_LAST,
) = range(19)
WIDE = jnp.float32


def shape_of(*dims, kind=LOW):
    return jax.ShapeDtypeStruct(dims, kind)


def params(megabytes=56):
    return pltpu.CompilerParams(vmem_limit_bytes=megabytes * 2**20)


def cost(flops, bytes_moved=0):
    return pl.CostEstimate(flops=flops, bytes_accessed=bytes_moved, transcendentals=0)


class Order:
    last = None

    def __init__(self):
        self.wanted = []

    def need(self, *arrays):
        self.wanted += arrays

    def run(self, kernel, args, out_shape, in_specs, out_specs, scratch_shapes, flops, moved, name, grid=None, prefetch=0, room=56):
        count = len(args)
        extra = ([] if self.last is None else [self.last]) + self.wanted
        self.wanted = []

        def ordered(*refs):
            kernel(*refs[:count], *refs[count + len(extra) :])

        specs = dict(in_specs=list(in_specs) + [HBM] * len(extra), out_specs=out_specs)
        if grid is None:
            specs["scratch_shapes"] = scratch_shapes
        else:
            specs = dict(
                grid_spec=pltpu.PrefetchScalarGridSpec(
                    num_scalar_prefetch=prefetch, grid=grid, scratch_shapes=scratch_shapes, **specs
                )
            )
        results = pl.pallas_call(
            ordered, out_shape=out_shape, compiler_params=params(room), cost_estimate=cost(1, 1), name=name, **specs
        )(*args, *extra)
        self.last = min(results, key=lambda result: result.size)
        return results


def mul(first, second):
    return jnp.dot(first, second, preferred_element_type=WIDE)


def mul_cols(first, second):
    return lax.dot_general(
        first, second, (((1,), (1,)), ((), ())), preferred_element_type=WIDE
    )


def mul_rows(first, second):
    return lax.dot_general(
        first, second, (((0,), (0,)), ((), ())), preferred_element_type=WIDE
    )


def inverse_root(hidden):
    return lax.rsqrt(jnp.mean(hidden * hidden, axis=-1, keepdims=True) + EPSILON)


def norm_grads(hidden, gain, upstream):
    inverse = inverse_root(hidden)
    scaled = hidden * inverse
    gain_grad = jnp.sum(upstream * scaled, axis=0, keepdims=True)
    weighted = upstream * gain
    dots = jnp.mean(weighted * scaled, axis=-1, keepdims=True)
    return inverse * (weighted - scaled * dots), gain_grad


def load_all(sources, buffers, semaphores):
    copies = [
        pltpu.make_async_copy(source, buffer, semaphores.at[spot])
        for spot, (source, buffer) in enumerate(zip(sources, buffers))
    ]
    for copy in copies:
        copy.start()
    return copies


def two_heads(pair):
    width = pair.shape[1] // 2
    lane = lax.broadcasted_iota(jnp.int32, pair.shape, 1)
    zero = jnp.zeros_like(pair)
    return jnp.concatenate(
        [jnp.where(lane < width, pair, zero), jnp.where(lane < width, zero, pair)], axis=0
    )


def hot(shape, allowed):
    row = lax.broadcasted_iota(jnp.int32, shape, 0)
    column = lax.broadcasted_iota(jnp.int32, shape, 1)
    return jnp.where(allowed(row, column), jnp.ones((), WIDE), jnp.zeros((), WIDE)).astype(LOW)


def bucket_columns(bucket_ref, block):
    steps = bucket_ref.shape[0]
    spread_out = hot((steps, block), lambda row, column: row == column % steps)
    return mul(bucket_ref[...].astype(WIDE).astype(LOW), spread_out)


def bias_masks(bucket_ref, bias_ref, mask_ref, block):
    buckets, heads = bias_ref.shape
    steps = bucket_ref.shape[0]
    spots = bucket_columns(bucket_ref, block)
    row = lax.broadcasted_iota(jnp.int32, (block, block), 0)
    column = lax.broadcasted_iota(jnp.int32, (block, block), 1)
    allowed = (row // steps == column // steps) & (row >= column)
    for head in range(heads):
        table = jnp.zeros(spots.shape, WIDE)
        for bucket in range(buckets):
            table = jnp.where(spots == bucket, bias_ref[bucket, head], table)
        tiled = jnp.concatenate([table] * (block // steps), axis=0)
        side = (head % 2) * block
        mask_ref[head // 2, :, side : side + block] = jnp.where(allowed, tiled, MASKED)


def pair_softmax(scores, block):
    parts = []
    for side in range(2):
        part = scores[:, side * block : (side + 1) * block]
        part = jnp.exp(part - jnp.max(part, axis=-1, keepdims=True))
        parts.append(part / jnp.sum(part, axis=-1, keepdims=True))
    return jnp.concatenate(parts, axis=1)


def line_of(ref):
    return ref[...].reshape(1, ref.shape[0])


def grad_of_token(score_ref, row_ref):
    row = line_of(row_ref).astype(WIDE)
    scores = jnp.broadcast_to(line_of(score_ref), (8, score_ref.shape[0])).T[:, :1]
    return scores * row.shape[1] ** (-0.5), row


def self_forward_kernel(
    scale, pairs, block,
    dec_ref, self_gain_ref, cross_gain_ref, score_ref, row_ref, grad_hidden_ref, bucket_ref, bias_ref,
    query_w, key_w, value_w, output_w, cross_w,
    act_one_ref, query_ref, key_ref, value_ref, mixed_ref, residual_ref, act_two_ref, query_two_ref, upstream_ref,
    weight_buf, mask_ref, semaphores,
):
    copies = load_all(
        (query_w, key_w, value_w, output_w, cross_w), [weight_buf.at[i] for i in range(5)], semaphores
    )
    tokens = dec_ref[...].astype(WIDE)
    act_one = (tokens * inverse_root(tokens) * line_of(self_gain_ref)).astype(LOW)
    act_one_ref[...] = act_one
    bias_masks(bucket_ref, bias_ref, mask_ref, block)
    scaled, row = grad_of_token(score_ref, row_ref)
    upstream_ref[...] = (grad_hidden_ref[...] + scaled * row).astype(LOW)
    for spot, ref in ((0, query_ref), (1, key_ref), (2, value_ref)):
        copies[spot].wait()
        ref[...] = mul(act_one, weight_buf[spot]).astype(LOW)
    for start in range(0, tokens.shape[0], block):
        for pair in range(pairs):
            rows, cols = slice(start, start + block), slice(pair * block, (pair + 1) * block)
            scores = mul_cols(query_ref[rows, cols], two_heads(key_ref[rows, cols])) * scale
            weights = pair_softmax(scores + mask_ref[pair], block).astype(LOW)
            mixed_ref[rows, cols] = mul(weights, two_heads(value_ref[rows, cols])).astype(LOW)
    copies[3].wait()
    residual = tokens + mul(mixed_ref[...], weight_buf[3])
    residual_ref[...] = residual
    act_two = (residual * inverse_root(residual) * line_of(cross_gain_ref)).astype(LOW)
    act_two_ref[...] = act_two
    copies[4].wait()
    query_two_ref[...] = mul(act_two, weight_buf[4]).astype(LOW)


def self_forward(order, dec, self_gain, cross_gain, score, row, grad_hidden, bucket, bias, query_w, key_w, value_w, output_w, cross_w):
    tokens, width = dec.shape
    heads = bias.shape[1]
    low = shape_of(tokens, width)
    return order.run(
        functools.partial(self_forward_kernel, (width // heads) ** (-0.5), heads // 2, BLOCK),
        (dec, self_gain, cross_gain, score, row, grad_hidden, bucket, bias, query_w, key_w, value_w, output_w, cross_w),
        [low] * 5 + [shape_of(tokens, width, kind=WIDE), low, low, low],
        [VMEM] * 7 + [SCALARS] + [HBM] * 5,
        [VMEM] * 9,
        [
            pltpu.VMEM((5, width, width), LOW),
            pltpu.VMEM((heads // 2, BLOCK, 2 * BLOCK), WIDE),
            pltpu.SemaphoreType.DMA((5,)),
        ],
        10 * tokens * width * width, 10 * width * width, "self_forward",
    )


def regroup_kernel(head_ref, rows_ref, chip_ref, far_ref, near_ref, own_ref):
    for near, ref in ((2, chip_ref), (3, far_ref), (1, near_ref), (0, own_ref)):
        ref[...] = rows_ref[head_ref[0] ^ near]


def regroup(order, head, rows):
    shape = shape_of(*rows.shape[1:])
    return order.run(regroup_kernel, (head, rows), [shape] * 4, [SCALARS, VMEM], [VMEM] * 4, [], 0, 0, "regroup")


def attend_mask(head_ref, key_segment_ref, slot_ref, mask_ref, spots):
    rows, length = key_segment_ref.shape
    slots = slot_ref.shape[1]
    head = head_ref[0]
    part = length // rows
    queries = mask_ref.shape[1]
    keys = jnp.concatenate(
        [
            key_segment_ref[pl.ds(head, 1), pl.ds(pl.multiple_of((head ^ spot) * part, part), part)]
            for spot in spots
        ],
        axis=1,
    )
    key_hot = hot((slots, keys.shape[1]), lambda row, column: row == keys)
    slot_segment = slot_ref[pl.ds(head, 1), :]
    slot_hot = hot((slots, slots), lambda row, column: row == slot_segment)
    ask_hot = mul(slot_hot, hot((slots, queries), lambda row, column: row == column // (queries // slots)))
    mask_ref[...] = jnp.where(mul_rows(key_hot, ask_hot.astype(LOW)) > 0.5, 0.0, MASKED)


def one_head(pair, side):
    width = pair.shape[1] // 2
    lane = lax.broadcasted_iota(jnp.int32, pair.shape, 1)
    return jnp.where((lane < width) == (side == 0), pair, jnp.zeros_like(pair))


def half_attention(pair, side, query, key_ref, value_t, mask_ref):
    lanes = BLOCK
    width = lanes // 2
    cols = slice(pair * lanes, (pair + 1) * lanes)
    spots = slice((2 * pair + side) * width, (2 * pair + side + 1) * width)
    scores = mul_cols(key_ref[:, cols], one_head(query, side)) + mask_ref[...]
    highest = jnp.max(scores, axis=0, keepdims=True)
    raised = jnp.exp(scores - highest)
    return highest, jnp.sum(raised, axis=0, keepdims=True), mul(value_t[spots], raised.astype(LOW)), spots


def cross_first_kernel(
    scale, pairs,
    head_ref, first_ref, second_ref, key_segment_ref, slot_ref, query_ref, key_w, value_w,
    key_ref, value_ref, mixed_ref, highest_ref, mass_ref,
    weight_buf, mask_ref, value_t, semaphores,
):
    copies = load_all((key_w, value_w), [weight_buf.at[0], weight_buf.at[1]], semaphores)
    attend_mask(head_ref, key_segment_ref, slot_ref, mask_ref, (0, 1))
    rows = first_ref.shape[0]
    for spot, ref in ((0, key_ref), (1, value_ref)):
        copies[spot].wait()
        ref[:rows] = mul(first_ref[...], weight_buf[spot]).astype(LOW)
        ref[rows:] = mul(second_ref[...], weight_buf[spot]).astype(LOW)
    value_t[...] = value_ref[...].T
    for pair in range(pairs):
        query = query_ref[:, pair * BLOCK : (pair + 1) * BLOCK] * scale
        for side in range(2):
            head = 2 * pair + side
            highest, mass, mixed, spots = half_attention(pair, side, query, key_ref, value_t, mask_ref)
            highest_ref[head : head + 1, :] = highest
            mass_ref[head : head + 1, :] = mass
            mixed_ref[spots] = mixed


def cross_first(order, head, first, second, key_segment, slots, query, key_w, value_w, heads):
    rows, width = first.shape
    tokens = query.shape[0]
    stat = shape_of(heads, tokens, kind=WIDE)
    return order.run(
        functools.partial(cross_first_kernel, (width // heads) ** (-0.5), heads // 2),
        (head, first, second, key_segment, slots, query, key_w, value_w),
        [shape_of(2 * rows, width)] * 2 + [shape_of(width, tokens, kind=WIDE), stat, stat],
        [SCALARS] + [VMEM] * 5 + [HBM] * 2,
        [VMEM] * 5,
        [
            pltpu.VMEM((2, width, width), LOW), pltpu.VMEM((2 * rows, tokens), WIDE),
            pltpu.VMEM((width, 2 * rows), LOW), pltpu.SemaphoreType.DMA((2,)),
        ],
        0, 0, "cross_first",
    )


def cross_last_kernel(
    scale, pairs,
    head_ref, third_ref, fourth_ref, key_segment_ref, slot_ref, query_ref,
    mixed_a_ref, highest_a_ref, mass_a_ref, residual_ref, gain_ref, key_w, value_w, output_w,
    key_ref, value_ref, mixed_ref, totals_ref, residual_two_ref, act_ref,
    weight_buf, mask_ref, value_t, semaphores,
):
    copies = load_all(
        (key_w, value_w, output_w), [weight_buf.at[i] for i in range(3)], semaphores
    )
    attend_mask(head_ref, key_segment_ref, slot_ref, mask_ref, (2, 3))
    rows = third_ref.shape[0]
    for spot, ref in ((0, key_ref), (1, value_ref)):
        copies[spot].wait()
        ref[:rows] = mul(third_ref[...], weight_buf[spot]).astype(LOW)
        ref[rows:] = mul(fourth_ref[...], weight_buf[spot]).astype(LOW)
    value_t[...] = value_ref[...].T
    for pair in range(pairs):
        query = query_ref[:, pair * BLOCK : (pair + 1) * BLOCK] * scale
        for side in range(2):
            head = 2 * pair + side
            line = slice(head, head + 1)
            highest, mass, mixed, spots = half_attention(pair, side, query, key_ref, value_t, mask_ref)
            top = jnp.maximum(highest, highest_a_ref[line, :])
            here, there = jnp.exp(highest - top), jnp.exp(highest_a_ref[line, :] - top)
            mass = mass * here + mass_a_ref[line, :] * there
            totals_ref[line, :] = top + jnp.log(mass)
            inverse = 1.0 / mass
            mixed_ref[spots] = (mixed * (here * inverse) + mixed_a_ref[spots] * (there * inverse)).astype(LOW)
    copies[2].wait()
    residual = residual_ref[...] + mul(mixed_ref[...].T, weight_buf[2])
    residual_two_ref[...] = residual
    act_ref[...] = (residual * inverse_root(residual) * line_of(gain_ref)).astype(LOW)


def cross_last(order, head, third, fourth, key_segment, slots, query, mixed, highest, mass, residual, gain, key_w, value_w, output_w, heads):
    tokens, width = query.shape
    rows = third.shape[0]
    tall = shape_of(2 * rows, width)
    return order.run(
        functools.partial(cross_last_kernel, (width // heads) ** (-0.5), heads // 2),
        (head, third, fourth, key_segment, slots, query, mixed, highest, mass, residual, gain, key_w, value_w, output_w),
        [
            tall, tall, shape_of(width, tokens), shape_of(heads, tokens, kind=WIDE),
            shape_of(tokens, width, kind=WIDE), shape_of(tokens, width),
        ],
        [SCALARS] + [VMEM] * 10 + [HBM] * 3,
        [VMEM] * 6,
        [
            pltpu.VMEM((3, width, width), LOW), pltpu.VMEM((2 * rows, tokens), WIDE),
            pltpu.VMEM((width, 2 * rows), LOW), pltpu.SemaphoreType.DMA((3,)),
        ],
        0, 0, "cross_last",
    )


def gelu_parts(pre):
    root = 0.7978845608028654
    square = pre * pre
    curve = jnp.tanh(root * (pre + 0.044715 * (square * pre)))
    ahead = 0.5 * (1.0 + curve)
    slope = ahead + (0.5 * root) * pre * (1.0 - curve * curve) * (1.0 + (3 * 0.044715) * square)
    return (pre * ahead).astype(LOW), slope


def spread_quarters(core, turned, other_ref, at, mine_ref, spot):
    quarter = turned.shape[0] // 4
    first = core == 0
    for chip in range(2):
        even = turned[2 * chip * quarter : (2 * chip + 1) * quarter]
        odd = turned[(2 * chip + 1) * quarter : (2 * chip + 2) * quarter]
        mine_ref[spot + chip] = jnp.where(first, even, odd)
        other_ref[at + chip * quarter : at + (chip + 1) * quarter] = jnp.where(first, odd, even)


def feed_first_kernel(
    order_ref, act_ref, upstream_low_ref, act_one_ref, mixed_one_ref, act_two_ref, mixed_ref, in_ref, out_ref,
    other_ref, grad_pre_ref, total_ref, upward_ref, mine_ref,
):
    step = pl.program_id(0)
    part, width = in_ref.shape[1], in_ref.shape[0]

    @pl.when(step == 0)
    def _():
        sources = (act_ref[...].T, mixed_ref[...], act_one_ref[...].T, mixed_one_ref[...].T, act_two_ref[...].T)
        for spot, turned in enumerate(sources):
            spread_quarters(order_ref[2], turned, other_ref, 2 * part + spot * width // 2, mine_ref, 2 * spot)
        other_ref[2 * part + len(sources) * width // 2 :] = upstream_low_ref[...].T
        total_ref[...] = jnp.zeros_like(total_ref)
        upward_ref[...] = jnp.zeros_like(upward_ref)

    hidden, slope = gelu_parts(mul(act_ref[...], in_ref[...]))
    other_ref[pl.ds(pl.multiple_of(step * part, part), part)] = hidden.T
    grad_pre = (mul_cols(upstream_low_ref[...], out_ref[...]) * slope).astype(LOW)
    grad_pre_ref[0] = grad_pre
    total_ref[...] += mul(hidden, out_ref[...])
    upward_ref[...] += mul_cols(grad_pre, in_ref[...])


def feed_last_kernel(
    order_ref,
    act_ref, upstream_low_ref, in_total_ref, in_upward_ref, residual_ref, grad_hidden_ref, score_ref, row_ref, gain_ref,
    in_ref, out_ref, cross_w,
    hidden_ref, grad_pre_ref,
    result_ref, ranking_ref, row_grad_ref, gain_grad_ref, grad_two_ref, grad_two_low_ref, grad_mixed_ref,
    total, upward, cross_buf, semaphore,
):
    step = pl.program_id(0)
    copy = pltpu.make_async_copy(cross_w, cross_buf, semaphore)

    @pl.when(step == 0)
    def _():
        copy.start()
        total[...] = in_total_ref[...]
        upward[...] = in_upward_ref[...]

    hidden, slope = gelu_parts(mul(act_ref[...], in_ref[...]))
    hidden_ref[0] = hidden.T
    grad_pre = (mul_cols(upstream_low_ref[...], out_ref[...]) * slope).astype(LOW)
    grad_pre_ref[0] = grad_pre
    total[...] += mul(hidden, out_ref[...])
    upward[...] += mul_cols(grad_pre, in_ref[...])

    @pl.when(step == pl.num_programs(0) - 1)
    def _():
        residual = residual_ref[...]
        scaled, row = grad_of_token(score_ref, row_ref)
        final = residual + total[...]
        result_ref[...] = final.astype(LOW)
        ranking = jnp.sum(final * row, axis=-1, keepdims=True) * row.shape[1] ** (-0.5)
        ranking_ref[...] = jnp.broadcast_to(ranking, (ranking.shape[0], BLOCK)).T[:1]
        row_grad_ref[...] = jnp.sum(scaled * final, axis=0, keepdims=True)
        back, gain_grad = norm_grads(residual, line_of(gain_ref), upward[...])
        gain_grad_ref[...] = gain_grad
        grad_two = grad_hidden_ref[...] + scaled * row + back
        grad_two_ref[...] = grad_two
        grad_two_low = grad_two.astype(LOW)
        grad_two_low_ref[...] = grad_two_low
        copy.wait()
        grad_mixed_ref[...] = mul_cols(grad_two_low, cross_buf[...]).astype(LOW)


def feed_specs(tokens, width, part, first):
    whole = lambda *dims: pl.BlockSpec(dims, lambda step, order: (0,) * len(dims))
    weights = [
        pl.BlockSpec((width, part), lambda step, order: (0, order[first + step])),
        pl.BlockSpec((part, width), lambda step, order: (order[first + step], 0)),
    ]
    return whole, weights, pl.BlockSpec((1, tokens, part), lambda step, order: (step, 0, 0))


def feed_first(order, parts, act, upstream_low, act_one, mixed_one, act_two, mixed, feed_in, feed_out):
    tokens, width = act.shape
    part = feed_in.shape[1] // 4
    whole, weights, result = feed_specs(tokens, width, part, 0)
    full = whole(tokens, width)
    height = 2 * part + 5 * width // 2 + width
    return order.run(
        feed_first_kernel,
        (parts, act, upstream_low, act_one, mixed_one, act_two, mixed, feed_in, feed_out),
        [shape_of(height, tokens), shape_of(2, tokens, part)]
        + [shape_of(tokens, width, kind=WIDE)] * 2
        + [shape_of(10, width // 4, tokens)],
        [full] * 5 + [whole(width, tokens)] + weights,
        [whole(height, tokens), result] + [full] * 2 + [whole(10, width // 4, tokens)],
        [],
        0, 0, "feed_first", grid=(2,), prefetch=1,
    )


def feed_last(order, parts, act, upstream_low, total, upward, residual, grad_hidden, score, row, gain, feed_in, feed_out, cross_output):
    tokens, width = act.shape
    part = feed_in.shape[1] // 4
    whole, weights, result = feed_specs(tokens, width, part, 2)
    full, line = whole(tokens, width), whole(1, width)
    return order.run(
        feed_last_kernel,
        (parts, act, upstream_low, total, upward, residual, grad_hidden, score, row, gain, feed_in, feed_out, cross_output),
        [
            shape_of(2, part, tokens), shape_of(2, tokens, part),
            shape_of(tokens, width), shape_of(1, tokens, kind=WIDE), shape_of(1, width, kind=WIDE),
            shape_of(1, width, kind=WIDE), shape_of(tokens, width, kind=WIDE), shape_of(tokens, width), shape_of(tokens, width),
        ],
        [full] * 6 + [whole(tokens), whole(width), whole(width)] + weights + [HBM],
        [
            pl.BlockSpec((1, part, tokens), lambda step, order: (step, 0, 0)), result,
            full, whole(1, tokens), line, line, full, full, full,
        ],
        [
            pltpu.VMEM((tokens, width), WIDE),
            pltpu.VMEM((tokens, width), WIDE),
            pltpu.VMEM((width, width), LOW),
            pltpu.SemaphoreType.DMA,
        ],
        0, 0, "feed_last", grid=(2,), prefetch=1,
    )


def cross_backward_kernel(
    scale, pairs,
    head_ref, query_ref, key_a_ref, value_a_ref, key_b_ref, value_b_ref, totals_ref, grad_mixed_ref,
    key_segment_ref, slot_ref, residual_ref, gain_ref, grad_two_ref, query_w, output_w,
    asked_ref, kept_ref,
    grad_one_ref, grad_mixed_one_ref, gain_grad_ref,
    weight_buf, mask_ref, key_t, query_t, semaphores,
):
    copies = load_all(
        (query_w, output_w), [weight_buf.at[i] for i in range(2)], semaphores
    )
    attend_mask(head_ref, key_segment_ref, slot_ref, mask_ref, (0, 1, 2, 3))
    half = key_a_ref.shape[0]
    lanes = 128
    key_t[:, :half] = key_a_ref[...].T
    key_t[:, half:] = key_b_ref[...].T
    for pair in range(pairs):
        cols = slice(pair * lanes, (pair + 1) * lanes)
        query = query_ref[:, cols] * scale
        keys = (key_a_ref, key_b_ref)
        values = (value_a_ref, value_b_ref)
        key_parts = [[], []]
        value_parts = [[], []]
        for side in range(2):
            ask = one_head(query, side)
            grad = one_head(grad_mixed_ref[:, cols], side)
            head = 2 * pair + side
            total = totals_ref[head : head + 1, :]
            weights, grad_weights = [], []
            for spot in range(2):
                rows = slice(spot * half, (spot + 1) * half)
                scores = mul_cols(keys[spot][:, cols], ask) + mask_ref[rows]
                weights.append(jnp.exp(scores - total))
                grad_weights.append(mul_cols(values[spot][:, cols], grad))
            dots = sum(
                jnp.sum(one * other, axis=0, keepdims=True) for one, other in zip(weights, grad_weights)
            )
            spots = slice(head * (lanes // 2), (head + 1) * (lanes // 2))
            part = 0.0
            for spot in range(2):
                grad_scores = (weights[spot] * (grad_weights[spot] - dots)).astype(LOW)
                part += mul(key_t[spots, spot * half : (spot + 1) * half], grad_scores)
                key_parts[spot].append(mul(grad_scores, ask))
                value_parts[spot].append(mul(weights[spot].astype(LOW), grad))
            query_t[spots] = (part * scale).astype(LOW)
        for spot in range(2):
            rows = slice(spot * half, (spot + 1) * half)
            kept_ref[0, rows, cols] = (key_parts[spot][0] + key_parts[spot][1]).astype(LOW)
            kept_ref[1, rows, cols] = (value_parts[spot][0] + value_parts[spot][1]).astype(LOW)
    asked_ref[0] = query_t[...].T
    copies[0].wait()
    back, gain_grad = norm_grads(
        residual_ref[...], line_of(gain_ref), mul_cols(asked_ref[0], weight_buf[0])
    )
    gain_grad_ref[...] = gain_grad
    grad_one = grad_two_ref[...] + back
    grad_one_ref[...] = grad_one
    grad_one_low = grad_one.astype(LOW)
    asked_ref[1] = grad_one_low
    copies[1].wait()
    grad_mixed_one_ref[...] = mul_cols(grad_one_low, weight_buf[1]).astype(LOW)


def cross_backward(order, head, query, key_a, value_a, key_b, value_b, totals, grad_mixed, key_segment, slots, residual, gain, grad_two, query_w, output_w):
    tokens, width = query.shape
    heads = totals.shape[0]
    keys = 2 * key_a.shape[0]
    return order.run(
        functools.partial(cross_backward_kernel, (width // heads) ** (-0.5), heads // 2),
        (head, query, key_a, value_a, key_b, value_b, totals, grad_mixed, key_segment, slots, residual, gain, grad_two, query_w, output_w),
        [
            shape_of(2, tokens, width), shape_of(2, keys, width),
            shape_of(tokens, width, kind=WIDE), shape_of(tokens, width), shape_of(1, width, kind=WIDE),
        ],
        [SCALARS] + [VMEM] * 12 + [HBM] * 2,
        [VMEM] * 5,
        [
            pltpu.VMEM((2, width, width), LOW),
            pltpu.VMEM((keys, tokens), WIDE),
            pltpu.VMEM((width, keys), LOW),
            pltpu.VMEM((width, tokens), LOW),
            pltpu.SemaphoreType.DMA((2,)),
        ],
        4 * keys * width * width + 20 * tokens * keys * width + 4 * tokens * width * width, 8 * width * width,
        "cross_backward",
    )


def self_backward_kernel(
    scale, pairs, block,
    query_ref, key_ref, value_ref, grad_mixed_ref, dec_ref, gain_ref, grad_one_ref, bucket_ref,
    asked_ref, cross_gain_ref, feed_gain_ref, row_grad_ref, bias_ref, query_w, key_w, value_w,
    pack_ref, ask_ref, result_ref,
    weight_buf, mask_ref, table_ref, bias_grad, small, semaphores,
):
    tokens = dec_ref.shape[0]
    copies = load_all((query_w, key_w, value_w), [weight_buf.at[i] for i in range(3)], semaphores)
    steps = bucket_ref.shape[0]
    bias_masks(bucket_ref, bias_ref, mask_ref, block)
    for pair in range(pairs):
        table = jnp.zeros((steps, 2 * block), WIDE)
        for start in range(0, dec_ref.shape[0], block):
            rows, cols = slice(start, start + block), slice(pair * block, (pair + 1) * block)
            query, keys, values = query_ref[rows, cols], two_heads(key_ref[rows, cols]), two_heads(value_ref[rows, cols])
            grad = grad_mixed_ref[rows, cols]
            weights = pair_softmax(mul_cols(query, keys) * scale + mask_ref[pair], block)
            grad_weights = mul_cols(grad, values)
            product = weights * grad_weights
            grad_scores = jnp.concatenate(
                [
                    product[:, side * block : (side + 1) * block]
                    - weights[:, side * block : (side + 1) * block]
                    * jnp.sum(product[:, side * block : (side + 1) * block], axis=-1, keepdims=True)
                    for side in range(2)
                ],
                axis=1,
            ).astype(LOW)
            table += jnp.sum(grad_scores.astype(WIDE).reshape(block // steps, steps, 2 * block), axis=0)
            pack_ref[0 * tokens + start : 0 * tokens + start + block, cols] = (mul(grad_scores, keys) * scale).astype(LOW)
            key_parts = mul_rows(grad_scores, query)
            value_parts = mul_rows(weights.astype(LOW), grad)
            lane = lax.broadcasted_iota(jnp.int32, (block, block), 1) < block // 2
            pack_ref[1 * tokens + start : 1 * tokens + start + block, cols] = (
                jnp.where(lane, key_parts[:block], key_parts[block:]) * scale
            ).astype(LOW)
            pack_ref[2 * tokens + start : 2 * tokens + start + block, cols] = jnp.where(lane, value_parts[:block], value_parts[block:]).astype(LOW)
        table_ref[pair] = table
    spots = bucket_columns(bucket_ref, block)
    for bucket in range(bias_ref.shape[0]):
        hit = jnp.concatenate([spots == bucket] * 2, axis=1)
        for pair in range(pairs):
            kept = jnp.sum(jnp.where(hit, table_ref[pair], 0.0), axis=0, keepdims=True)
            bias_grad[2 * pair, bucket : bucket + 1, :] = kept[:, :block]
            bias_grad[2 * pair + 1, bucket : bucket + 1, :] = kept[:, block:]
    upward = 0.0
    for spot in range(3):
        copies[spot].wait()
        upward += mul_cols(pack_ref[spot * tokens : (spot + 1) * tokens], weight_buf[spot])
    back, gain_grad = norm_grads(dec_ref[...].astype(WIDE), line_of(gain_ref), upward)
    small[...] = jnp.zeros_like(small)
    for row, value in enumerate((gain_grad, cross_gain_ref[...], feed_gain_ref[...], row_grad_ref[...])):
        small[row : row + 1, :] = value
    heads, buckets, _ = bias_grad.shape
    small[4 : 4 + heads, :buckets] = jnp.sum(bias_grad[...], axis=-1)
    ask_ref[:tokens] = asked_ref[0]
    ask_ref[tokens : 2 * tokens] = asked_ref[1]
    ask_ref[2 * tokens :] = small[...].astype(LOW)
    result_ref[...] = grad_one_ref[...] + back


def self_backward(order, query, key, value, grad_mixed, dec, gain, grad_one, bucket, asked, cross_gain_grad, feed_gain_grad, row_grad, bias, query_w, key_w, value_w):
    tokens, width = query.shape
    buckets, heads = bias.shape
    small = -(-(4 + heads) // 16) * 16
    steps = bucket.shape[0]
    return order.run(
        functools.partial(self_backward_kernel, (width // heads) ** (-0.5), heads // 2, BLOCK),
        (query, key, value, grad_mixed, dec, gain, grad_one, bucket, asked, cross_gain_grad, feed_gain_grad, row_grad, bias, query_w, key_w, value_w),
        [shape_of(3 * tokens, width), shape_of(2 * tokens + small, width), shape_of(tokens, width, kind=WIDE)],
        [VMEM] * 12 + [SCALARS] + [HBM] * 3,
        [VMEM] * 3,
        [
            pltpu.VMEM((3, width, width), LOW),
            pltpu.VMEM((heads // 2, BLOCK, 2 * BLOCK), WIDE),
            pltpu.VMEM((heads // 2, steps, 2 * BLOCK), WIDE),
            pltpu.VMEM((heads, buckets, BLOCK), WIDE),
            pltpu.VMEM((small, width), WIDE),
            pltpu.SemaphoreType.DMA((3,)),
        ],
        0, 0, "self_backward",
    )


def encoder_weights_kernel(core_ref, first_ref, second_ref, third_ref, fourth_ref, grads_ref, other_ref, mine_ref, turned, whole):
    for spot, ref in enumerate((first_ref, second_ref, third_ref, fourth_ref)):
        rows = ref.shape[0]
        turned[:, spot * rows : (spot + 1) * rows] = ref[...].T
    quarter = whole.shape[0] // 4
    core = core_ref[0]
    for weight in range(2):
        whole[...] = mul(turned[...], grads_ref[weight]).astype(LOW)
        for chip in range(2):
            at = lambda side: pl.ds(pl.multiple_of((2 * chip + side) * quarter, quarter), quarter)
            mine_ref[weight, chip] = whole[at(core)]
            other_ref[weight, chip] = whole[at(1 - core)]


def encoder_weights(order, core, rows, grads):
    count, width = rows[0].shape
    shape = shape_of(2, 2, width // 4, width)
    return order.run(
        encoder_weights_kernel,
        (core, *rows, grads),
        [shape] * 2,
        [SCALARS] + [VMEM] * 5,
        [VMEM] * 2,
        [pltpu.VMEM((width, 4 * count), LOW), pltpu.VMEM((width, width), LOW)],
        16 * count * width * width, 8 * width * width, "encoder_weights",
    )


def encoder_rows_kernel(grads_ref, key_w, value_w, own_ref, near_ref, chip_ref, weight_buf, semaphores):
    copies = load_all((key_w, value_w), [weight_buf.at[0], weight_buf.at[1]], semaphores)
    for copy in copies:
        copy.wait()
    rows = own_ref.shape[0]
    for ref, start in ((own_ref, 0), (near_ref, rows), (chip_ref, 2 * rows)):
        part = slice(start, start + ref.shape[0])
        grad = mul_cols(grads_ref[0, part], weight_buf[0]) + mul_cols(grads_ref[1, part], weight_buf[1])
        ref[...] = grad.astype(ref.dtype)


def encoder_rows(order, grads, key_w, value_w):
    rows, width = grads.shape[1] // 4, grads.shape[2]
    return order.run(
        encoder_rows_kernel,
        (grads, key_w, value_w),
        [shape_of(rows, width, kind=WIDE), shape_of(rows, width), shape_of(2 * rows, width)],
        [VMEM] + [HBM] * 2,
        [VMEM] * 3,
        [pltpu.VMEM((2, width, width), LOW), pltpu.SemaphoreType.DMA((2,))],
        16 * rows * width * width, 8 * width * width, "encoder_rows",
    )


def stage_kernel(mode, weights, rows, extra, count, place_ref, *refs):
    stage, way = mode
    chip, pair = place_ref[0], place_ref[1]
    inputs, outs = refs[:count], refs[count:]

    def columns(matrix, side):
        if side is None:
            return matrix
        half = matrix.shape[1] // 2
        return jnp.where((pair == 0) == (side == 0), matrix[:, :half], matrix[:, half:])

    def value(weight, quarter, side):
        if len(weight) == 3:
            here, came, row = weight
            return columns(inputs[here][row:].astype(WIDE) + inputs[came][row:].astype(WIDE), side)
        if len(weight) == 4:
            here, spot, came, other = weight
            return columns(
                inputs[here][spot, quarter].astype(WIDE) + inputs[came][other, quarter].astype(WIDE), side
            )
        here, base, came, at, grads, grads_came, row = weight
        size, tokens = inputs[here].shape[1:]
        there = inputs[came][pl.ds(pl.multiple_of(at + quarter * size, 64), size)]
        if grads_came == came:
            near, far = inputs[grads][...], columns(mul_cols(there, inputs[came][row:]), side)
        else:
            spots = slice(row, row + tokens)
            near, far = inputs[grads][spots], mul(there, columns(inputs[grads_came][spots], side))
        return mul(inputs[here][base + quarter], columns(near, side)) + far

    at = 0
    for weight in list(weights) + ([] if extra is None else [extra]):
        if way == PAIR:
            totals = [value(weight, quarter, 1 if stage == 0 else 0) for quarter in range(2)]
        else:
            total = value(weight, (1 - chip) if stage == 0 else chip, None)
            half = total.shape[1] // 2
            totals = [total[:, :half], total[:, half:]]
        spots = slice(at, at + totals[0].shape[0])
        at = spots.stop
        if stage == 1:
            totals = [total + inputs[-1][part, spots].astype(WIDE) for part, total in enumerate(totals)]
        totals = [total.astype(LOW) for total in totals]
        if stage == 0 or way == WHOLE:
            outs[0][0, spots] = totals[0]
            outs[0][1, spots] = totals[1]
        else:
            low = (chip if way == PAIR else pair) == 0
            outs[0][spots] = jnp.where(low, totals[1], totals[0])
            outs[1][spots] = jnp.where(low, totals[0], totals[1])


def stage(order, spots, mode, weights, extra=None, came=None):
    arrays, described = [], []

    def spot_of(array):
        for spot, known in enumerate(arrays):
            if known is array:
                return spot
        arrays.append(array)
        return len(arrays) - 1

    for weight in weights:
        if len(weight) == 4:
            here, spot, other, member = weight
            described.append((spot_of(here), spot, spot_of(other), member))
            rows, columns = here.shape[-2:]
        else:
            here, base, other, at, grads, grads_came, row = weight
            described.append((spot_of(here), base, spot_of(other), at, spot_of(grads), spot_of(grads_came), row))
            rows, columns = here.shape[1], grads.shape[1]
    height = rows * len(weights)
    if extra is not None:
        height += extra[0].shape[0] - extra[2]
        extra = (spot_of(extra[0]), spot_of(extra[1]), extra[2])
    if came is not None:
        arrays.append(came)
    if mode[0] == 0 or mode[1] == WHOLE:
        shapes = [shape_of(2, height, columns // 2)]
    else:
        shapes = [shape_of(height, columns // 2)] * 2
    return order.run(
        functools.partial(stage_kernel, mode, described, rows, extra, len(arrays)),
        (spots, *arrays),
        shapes,
        [SCALARS] + [VMEM] * len(arrays),
        [VMEM] * len(shapes),
        [],
        0, 0, "stage", room=20,
    )


def feed_in_kernel(stage_index, place_ref, here_ref, came_ref, first_ref, last_ref, first_came_ref, last_came_ref, *refs):
    chip, pair, core = place_ref[0], place_ref[1], place_ref[2]
    half = pair if stage_index else 1 - pair
    part = last_ref.shape[2]
    low = chip == 0
    for side, (own, other) in enumerate(((last_ref, first_came_ref), (first_ref, last_came_ref))):
        block = core if side == 0 else 1 - core
        columns = pl.ds(pl.multiple_of(block * part, part), part)
        totals = []
        for quarter in range(2):
            size = here_ref.shape[1]
            start = 2 * part + quarter * size
            total = mul(here_ref[quarter], own[half]) + mul(came_ref[start : start + size], other[half])
            if stage_index:
                total += refs[0][quarter, :, columns].astype(WIDE)
            totals.append(total.astype(LOW))
        if stage_index:
            refs[1][:, columns] = jnp.where(low, totals[1], totals[0])
            refs[2][:, columns] = jnp.where(low, totals[0], totals[1])
        else:
            refs[0][0, :, columns] = totals[0]
            refs[0][1, :, columns] = totals[1]


def feed_in_stage(order, spots, stage_index, here, came, first, last, first_came, last_came, arrived=None):
    arrays = [here, came, first, last, first_came, last_came] + ([] if arrived is None else [arrived])
    rows = here.shape[1]
    half = 2 * first.shape[2]
    shapes = [shape_of(rows, half)] * 2 if stage_index else [shape_of(2, rows, half)]
    return order.run(
        functools.partial(feed_in_kernel, stage_index),
        (spots, *arrays),
        shapes,
        [SCALARS] + [VMEM] * len(arrays),
        [VMEM] * len(shapes),
        [],
        0, 0, "feed_in_stage", room=20,
    )


def combine_kernel(way, heights, place_ref, *refs):
    line, length = place_ref[3], place_ref[4]
    left = line < length // 2
    takes = (line == 0) | (line == length - 1)

    def add(first, second):
        return (first.astype(WIDE) + second.astype(WIDE)).astype(LOW)

    if way == ADD:
        refs[2][...] = add(refs[0][...], refs[1][...])
    elif way == SPLIT:
        sums = [add(refs[0][part], refs[1][part]) for part in range(2)]
        refs[2][...] = jnp.where(left, sums[0], sums[1])
        refs[3][...] = jnp.where(left, sums[1], sums[0])
    elif way == JOIN:
        refs[2][0] = jnp.where(left, refs[0][...], refs[1][...])
        refs[2][1] = jnp.where(left, refs[1][...], refs[0][...])
    elif way == TAKE:
        refs[2][...] = jnp.where(takes, refs[1][...], refs[0][...])
    else:
        at = 0
        for index, height in enumerate(heights):
            spots = slice(at, at + height)
            at += height
            if way == COLUMNS:
                first = place_ref[1] == 0
                mine, came = refs[0][spots], refs[1][spots]
                parts = (jnp.where(first, mine, came), jnp.where(first, came, mine))
            else:
                parts = [jnp.where(takes, refs[1][part, spots], refs[0][part, spots]) for part in range(2)]
            half = parts[0].shape[1]
            refs[2 + index][:, :half] = parts[0].astype(WIDE)
            refs[2 + index][:, half:] = parts[1].astype(WIDE)


def combine(order, spots, way, mine, came, heights):
    if way == SPLIT:
        shapes = [shape_of(*mine.shape[1:])] * 2
    elif way == JOIN:
        shapes = [shape_of(2, *mine.shape)]
    elif way in (ADD, TAKE):
        shapes = [shape_of(*mine.shape)]
    else:
        shapes = [shape_of(height, 2 * mine.shape[-1], kind=WIDE) for height in heights]
    results = order.run(
        functools.partial(combine_kernel, way, heights),
        (spots, mine, came),
        shapes,
        [SCALARS] + [VMEM] * 2,
        [VMEM] * len(shapes),
        [],
        0, 0, NAMES[way], room=12,
    )
    return results[0] if way in (ADD, TAKE, JOIN) else results


def hand_on_kernel(*refs):
    for source, target in zip(refs[: len(refs) // 2], refs[len(refs) // 2 :]):
        target[...] = source[...]


def hand_on(order, *arrays):
    shapes = [shape_of(*array.shape, kind=array.dtype) for array in arrays]
    return order.run(
        hand_on_kernel, arrays, shapes, [VMEM] * len(arrays), [VMEM] * len(arrays), [], 0, 0, "hand_on", room=16
    )


def place_rows_kernel(head_ref, own_ref, core_ref, chip_ref, far_ref, out_ref):
    for spot, ref in enumerate((own_ref, core_ref, chip_ref, far_ref)):

        @pl.when(pl.program_id(0) == spot)
        def _():
            out_ref[0] = ref[...].astype(WIDE)


def place_rows(order, head, own, core, chip, far):
    rows, width = own.shape
    return order.run(
        place_rows_kernel,
        (head, own, core, chip, far),
        [shape_of(4, rows, width, kind=WIDE)],
        [pl.BlockSpec((rows, width), lambda step, head: (0, 0))] * 4,
        [pl.BlockSpec((1, rows, width), lambda step, head: (head[0] ^ step, 0, 0))],
        [],
        0, 24 * rows * width, "place_rows", grid=(4,), prefetch=1,
    )[0]


AXES = ("dp", "head")


def device_maps(dp_size, head_size):
    length = dp_size // 2
    half = length // 2

    def of(move):
        pairs = []
        for outer in range(dp_size):
            for inner in range(head_size):
                goal = move(outer // 2, outer % 2, inner)
                if goal is not None:
                    spot, side, place = goal
                    pairs.append(
                        (outer * head_size + inner, (2 * spot + side) * head_size + place)
                    )
        return pairs

    def along(first, first_goal):
        def step(spot, side, place):
            if spot == first:
                return (first_goal, side, place)
            if spot == length - 1 - first:
                return (length - 1 - first_goal, side, place)
            return None

        return of(step)

    return {
        CORE: of(lambda spot, side, place: (spot, side, place ^ 1)),
        CHIP: of(lambda spot, side, place: (spot, side, place ^ 2)),
        FAR: of(lambda spot, side, place: (spot, side, place ^ 3)),
        PAIR: of(lambda spot, side, place: (spot, 1 - side, place)),
        MIDDLE_PAIR: of(
            lambda spot, side, place: (spot, 1 - side, place) if spot in (half - 1, half) else None
        ),
        INWARD: [along(step, step + 1) for step in range(half - 1)],
        MIDDLE: along(half - 1, half),
        OUTWARD: [along(step + 1, step) for step in range(half - 1)],
    }


class Made:
    pass


class Place:
    def __init__(self):
        dp_size, head_size = lax.axis_size("dp"), lax.axis_size("head")
        self.maps = device_maps(dp_size, head_size)
        self.length = dp_size // 2
        self.head = lax.axis_index("head")
        self.chip, self.core = self.head // 2, self.head % 2
        dp_index = lax.axis_index("dp")
        self.pair, self.line = dp_index % 2, dp_index // 2

    def move(self, array, name):
        return lax.ppermute(array, AXES, self.maps[name])

    def inward(self, part):
        perms = self.maps[INWARD]
        for perm in perms[:-1]:
            part = add_low(part, lax.ppermute(part, AXES, perm))
        return part, lax.ppermute(part, AXES, perms[-1])

    def outward(self, part):
        perms = self.maps[OUTWARD]
        for step in range(len(perms) - 1, 0, -1):
            came = lax.ppermute(part, AXES, perms[step])
            part = jnp.where(self.takes(step), came, part)
        return part, lax.ppermute(part, AXES, perms[0])

    def takes(self, step):
        return (self.line == step) | (self.line == self.length - 1 - step)


def add_low(first, second):
    kind = first.dtype
    return (first.astype(jnp.float32) + second.astype(jnp.float32)).astype(kind)


def picks(*values):
    return jnp.stack([jnp.asarray(value, jnp.int32) for value in values])


class Group:
    def __init__(self, place, order, spots, mode):
        self.place, self.order, self.spots, self.mode = place, order, spots, mode
        self.steps = [SECOND] + (
            [SPLIT, ADD, ADD, JOIN, LINES]
            if mode == WHOLE
            else [ADD_INWARD, ADD_MIDDLE, ADD_OUTWARD, TAKE, COLUMNS]
        )

    def first(self, weights, extra=None):
        self.weights, self.extra = weights, extra
        (sent,) = stage(self.order, self.spots, (0, self.mode), weights, extra)
        rows = 0 if extra is None else extra[0].shape[0] - extra[2]
        self.heights = [(sent.shape[1] - rows) // len(weights)] * len(weights) + [rows] * (rows > 0)
        self.came = self.place.move(sent, PAIR if self.mode == PAIR else CHIP)

    def first_feed_in(self, parts):
        self.parts, self.weights = parts, None
        (sent,) = feed_in_stage(self.order, self.spots, 0, *parts)
        self.heights = [sent.shape[1]]
        self.came = self.place.move(sent, PAIR)

    def step(self):
        place = self.place
        way = self.steps.pop(0)
        if way == SECOND:
            if self.weights is None:
                results = feed_in_stage(self.order, self.spots, 1, *self.parts, self.came)
            else:
                results = stage(self.order, self.spots, (1, self.mode), self.weights, self.extra, self.came)
            if self.mode == WHOLE:
                self.part, self.came = place.inward(results[0])
            else:
                self.part = results[1]
                self.came = place.move(results[0], CHIP if self.mode == PAIR else PAIR)
            return
        result = combine(self.order, self.spots, ADD if way in ADDS else way, self.part, self.came, self.heights)
        if way == SPLIT:
            self.part, other = result
            self.came = place.move(other, MIDDLE)
        elif way == ADD:
            self.part = result
            self.came = place.move(result, MIDDLE_PAIR if self.steps[0] == ADD else MIDDLE)
        elif way in (JOIN, ADD_OUTWARD):
            self.part, self.came = place.outward(result)
        elif way == ADD_INWARD:
            self.part, self.came = place.inward(result)
        elif way == ADD_MIDDLE:
            self.part, self.came = result, place.move(result, MIDDLE)
        elif way == TAKE:
            self.part, self.came = result, place.move(result, PAIR)
        else:
            self.result = result


MODES = {OUT: CHIP, IN: PAIR, SELF: PAIR, ASK: CHIP, KEEP: CHIP}
SEQUENCE = (
    BACK, SELF_PASS, OUT, ENCODER, IN, SELF_FIRST, ASK_FIRST, KEEP_PASS, OUT, IN, KEEP_FIRST, OUT, ROWS, SELF, ASK,
    IN, SELF, OUT, ASK, KEEP, IN, SELF, OUT, KEEP, ASK, SELF, IN, OUT, ROWS_SEND, ASK, KEEP, SELF, KEEP, IN, ASK,
    SELF, KEEP, ROWS_PASS, ASK, ROWS_LAST, KEEP,
)


def body(
    decoder_in,
    encoder_out,
    encoder_segment,
    slot_segment,
    position_bucket,
    self_gain,
    self_query,
    self_key,
    self_value,
    self_output,
    position_bias,
    cross_gain,
    cross_query,
    cross_key,
    cross_value,
    cross_output,
    feed_gain,
    feed_in,
    feed_out,
    score_row,
    grad_hidden,
    grad_score,
):
    place = Place()
    model_width = decoder_in.shape[1]
    heads = position_bias.shape[1]
    tokens = decoder_in.shape[0]
    head_index, core = place.head, place.core
    core_list, head_list = picks(core), picks(head_index)
    spots = picks(place.chip, place.pair, core, place.line, place.length)
    order = Order()
    to_chip, to_far, to_near, own_rows = regroup(order, head_list, encoder_out)
    from_chip, from_far, from_near = place.move(to_chip, CHIP), place.move(to_far, FAR), place.move(to_near, CORE)
    rows = [own_rows, from_near, from_chip, from_far]
    act_one, query_one, key_one, value_one, mixed_one, residual_one, act_two, query_two, upstream_low = self_forward(
        order, decoder_in, self_gain, cross_gain, grad_score, score_row, grad_hidden, position_bucket, position_bias,
        self_query, self_key, self_value, self_output, cross_query,
    )
    key_a, value_a, mixed_a, highest, mass = cross_first(
        order, head_list, own_rows, from_near, encoder_segment, slot_segment, query_two, cross_key, cross_value, heads
    )
    key_b, value_b, mixed_two, totals, residual_two, act_three = cross_last(
        order, head_list, from_chip, from_far, encoder_segment, slot_segment, query_two, mixed_a, highest, mass,
        residual_one, feed_gain, cross_key, cross_value, cross_output, heads,
    )
    feed_parts = picks(1 - core, 3 - core, core, 2 + core)
    feed_other, pre_first, total, upward, mine = feed_first(
        order, feed_parts, act_three, upstream_low, act_one, mixed_one, act_two, mixed_two, feed_in, feed_out
    )
    feed_came, pre_first_came = place.move(feed_other, CORE), place.move(pre_first, CORE)
    (
        hidden_mine, pre_last, hidden_out, ranking, row_grad, feed_gain_grad, grad_two, grad_two_low, grad_mixed,
    ) = feed_last(
        order, feed_parts, act_three, upstream_low, total, upward, residual_two, grad_hidden, grad_score, score_row,
        feed_gain, feed_in, feed_out, cross_output,
    )
    pre_last_came, grad_two_came = place.move(pre_last, CORE), place.move(grad_two_low, CORE)
    groups = {name: Group(place, order, spots, MODES[name]) for name in MODES}
    half = model_width // 2
    acts = feed_out.shape[0] // 2
    groups[OUT].first([(hidden_mine, 0, feed_came, 0, upstream_low, feed_came, acts + 5 * half)])
    order.need(grad_two_came)
    groups[IN].first_feed_in((mine, feed_came, pre_first, pre_last, pre_first_came, pre_last_came))
    asked, kept, grad_one, grad_mixed_one, cross_gain_grad = cross_backward(
        order, head_list, query_two, key_a, value_a, key_b, value_b, totals, grad_mixed, encoder_segment, slot_segment,
        residual_one, cross_gain, grad_two, cross_query, self_output,
    )
    made = Made()

    def back():
        made.grads, made.asked, made.decoder = self_backward(
            order, query_one, key_one, value_one, grad_mixed_one, decoder_in, self_gain, grad_one, position_bucket, asked,
            cross_gain_grad, feed_gain_grad, row_grad, position_bias, self_query, self_key, self_value,
        )

    def self_pass():
        made.asked_came, made.grads_came = place.move(made.asked, CORE), place.move(made.grads, CORE)

    def self_copy():
        copies = hand_on(order, made.asked, made.grads)
        made.asked_came, made.grads_came = [place.move(copy, CORE) for copy in copies]

    def keep_copy():
        (other,) = hand_on(order, made.other)
        made.came = place.move(other, CORE)

    def keep_pass():
        made.came = place.move(made.other, CORE)

    def self_first():
        grads = made.grads
        groups[SELF].first(
            [(mine, 4, feed_came, acts + 2 * half, grads, made.grads_came, spot * tokens) for spot in range(3)]
        )

    def ask_first():
        asked, asked_came = made.asked, made.asked_came
        groups[ASK].first(
            [
                (mine, 2, feed_came, acts + half, grad_two_low, grad_two_came, 0),
                (mine, 8, feed_came, acts + 4 * half, asked, asked_came, 0),
                (mine, 6, feed_came, acts + 3 * half, asked, asked_came, tokens),
            ],
            (asked, asked_came, 2 * tokens),
        )

    def encoder_step():
        made.other, made.mine = encoder_weights(order, core_list, rows, kept)

    def keep_first():
        groups[KEEP].first([(made.mine, spot, made.came, spot) for spot in range(2)])

    def rows_step():
        made.own, made.to_near, made.to_chip = encoder_rows(order, kept, cross_key, cross_value)

    def rows_send():
        near, chip = hand_on(order, made.to_near, made.to_chip)
        made.chip, made.near = place.move(chip, CHIP), place.move(near, CORE)

    def rows_pass():
        count = made.chip.shape[0] // 2
        order.need(made.near)
        made.far = place.move(made.chip[count:], CORE)

    def rows_last():
        made.rows = place_rows(order, head_list, made.own, made.near, made.chip, made.far)

    tasks = {
        ASK_FIRST: ask_first,
        SELF_FIRST: self_first,
        SELF_PASS: self_pass,
        BACK: back,
        KEEP_PASS: keep_pass,
        SELF_COPY: self_copy,
        KEEP_COPY: keep_copy,
        ROWS_SEND: rows_send,
        KEEP_FIRST: keep_first,
        ENCODER: encoder_step,
        ROWS: rows_step,
        ROWS_PASS: rows_pass,
        ROWS_LAST: rows_last,
        NEED_KEEP: lambda: order.need(made.came),
    }
    for name in SEQUENCE:
        tasks.get(name, lambda: groups[name].step())()
    feed_out_grad, feed_in_grad = groups[OUT].result[0], groups[IN].result[0]
    self_query_grad, self_key_grad, self_value_grad = groups[SELF].result
    cross_output_grad, cross_query_grad, self_output_grad, small = groups[ASK].result
    cross_key_grad, cross_value_grad = groups[KEEP].result
    encoder_grad = made.rows
    width = model_width // 4
    gains = lax.dynamic_slice_in_dim(small[:4], head_index * width, width, axis=1)
    buckets = position_bias.shape[0] // 4
    bias_grad = lax.dynamic_slice_in_dim(small[4 : 4 + heads], head_index * buckets, buckets, axis=1).T
    return (
        hidden_out,
        ranking[0],
        made.decoder,
        encoder_grad,
        gains[0],
        self_query_grad,
        self_key_grad,
        self_value_grad,
        self_output_grad,
        bias_grad,
        gains[1],
        cross_query_grad,
        cross_key_grad,
        cross_value_grad,
        cross_output_grad,
        gains[2],
        feed_in_grad,
        feed_out_grad,
        gains[3],
    )


def solution(mesh):
    in_specs = (
        P(("dp", "head"), None),
        P("dp", "head", None),
        P("dp", None),
        P("dp", None),
        P(),
        P(),
        P(),
        P(),
        P(),
        P(),
        P(),
        P(),
        P(),
        P(),
        P(),
        P(),
        P(),
        P(),
        P(),
        P(),
        P(("dp", "head"), None),
        P(("dp", "head")),
    )
    out_specs = (
        P(("dp", "head"), None),
        P(("dp", "head")),
        P(("dp", "head"), None),
        P("dp", "head", None),
        P("head"),
        P("head", None),
        P("head", None),
        P("head", None),
        P("head", None),
        P("head", None),
        P("head"),
        P("head", None),
        P("head", None),
        P("head", None),
        P("head", None),
        P("head"),
        P("head", None),
        P("head", None),
        P("head"),
    )
    return jax.shard_map(body, mesh=mesh, in_specs=in_specs, out_specs=out_specs, check_vma=False)
```

```python
import functools
import jax
import jax.numpy as jnp
from jax import lax
from jax.experimental import pallas as pl
from jax.experimental.pallas import tpu as pltpu
from jax.sharding import PartitionSpec as P

EPSILON = 1e-06
MASKED = -1e30
HBM = pl.BlockSpec(memory_space=pl.ANY)
VMEM = pl.BlockSpec(memory_space=pltpu.VMEM)
SCALARS = pl.BlockSpec(memory_space=pltpu.SMEM)
LOW = jnp.bfloat16
BLOCK = 128
CHIP, PAIR, WHOLE, CORE, FAR, MIDDLE, MIDDLE_PAIR, INWARD, OUTWARD = range(9)
SECOND, SPLIT, ADD, JOIN, LINES, ADD_INWARD, ADD_MIDDLE, ADD_OUTWARD, TAKE, COLUMNS = range(10)
ADDS = (ADD_INWARD, ADD_MIDDLE, ADD_OUTWARD)
NAMES = {SPLIT: "combine_split", ADD: "combine_add", JOIN: "combine_join", LINES: "combine_rows"}
NAMES.update({TAKE: "combine_take", COLUMNS: "combine_columns"})
(
    OUT, IN, ASK, SELF, KEEP, BACK, SELF_PASS, SELF_COPY, ENCODER, KEEP_PASS, KEEP_COPY, NEED_KEEP, ASK_FIRST,
    SELF_FIRST, KEEP_FIRST, ROWS, ROWS_SEND, ROWS_PASS, ROWS_LAST,
) = range(19)
WIDE = jnp.float32


def shape_of(*dims, kind=LOW):
    return jax.ShapeDtypeStruct(dims, kind)


def params(megabytes=56):
    return pltpu.CompilerParams(vmem_limit_bytes=megabytes * 2**20)


def cost(flops, bytes_moved=0):
    return pl.CostEstimate(flops=flops, bytes_accessed=bytes_moved, transcendentals=0)


class Order:
    last = None

    def __init__(self):
        self.wanted = []

    def need(self, *arrays):
        self.wanted += arrays

    def run(self, kernel, args, out_shape, in_specs, out_specs, scratch_shapes, flops, moved, name, grid=None, prefetch=0, room=56):
        count = len(args)
        extra = ([] if self.last is None else [self.last]) + self.wanted
        self.wanted = []

        def ordered(*refs):
            kernel(*refs[:count], *refs[count + len(extra) :])

        specs = dict(in_specs=list(in_specs) + [HBM] * len(extra), out_specs=out_specs)
        if grid is None:
            specs["scratch_shapes"] = scratch_shapes
        else:
            specs = dict(
                grid_spec=pltpu.PrefetchScalarGridSpec(
                    num_scalar_prefetch=prefetch, grid=grid, scratch_shapes=scratch_shapes, **specs
                )
            )
        results = pl.pallas_call(
            ordered, out_shape=out_shape, compiler_params=params(room), cost_estimate=cost(1, 1), name=name, **specs
        )(*args, *extra)
        self.last = min(results, key=lambda result: result.size)
        return results


def mul(first, second):
    return jnp.dot(first, second, preferred_element_type=WIDE)


def mul_cols(first, second):
    return lax.dot_general(
        first, second, (((1,), (1,)), ((), ())), preferred_element_type=WIDE
    )


def mul_rows(first, second):
    return lax.dot_general(
        first, second, (((0,), (0,)), ((), ())), preferred_element_type=WIDE
    )


def inverse_root(hidden):
    return lax.rsqrt(jnp.mean(hidden * hidden, axis=-1, keepdims=True) + EPSILON)


def norm_grads(hidden, gain, upstream):
    inverse = inverse_root(hidden)
    scaled = hidden * inverse
    gain_grad = jnp.sum(upstream * scaled, axis=0, keepdims=True)
    weighted = upstream * gain
    dots = jnp.mean(weighted * scaled, axis=-1, keepdims=True)
    return inverse * (weighted - scaled * dots), gain_grad


def load_all(sources, buffers, semaphores):
    copies = [
        pltpu.make_async_copy(source, buffer, semaphores.at[spot])
        for spot, (source, buffer) in enumerate(zip(sources, buffers))
    ]
    for copy in copies:
        copy.start()
    return copies


def two_heads(pair):
    width = pair.shape[1] // 2
    lane = lax.broadcasted_iota(jnp.int32, pair.shape, 1)
    zero = jnp.zeros_like(pair)
    return jnp.concatenate(
        [jnp.where(lane < width, pair, zero), jnp.where(lane < width, zero, pair)], axis=0
    )


def hot(shape, allowed):
    row = lax.broadcasted_iota(jnp.int32, shape, 0)
    column = lax.broadcasted_iota(jnp.int32, shape, 1)
    return jnp.where(allowed(row, column), jnp.ones((), WIDE), jnp.zeros((), WIDE)).astype(LOW)


def bucket_columns(bucket_ref, block):
    steps = bucket_ref.shape[0]
    spread_out = hot((steps, block), lambda row, column: row == column % steps)
    return mul(bucket_ref[...].astype(WIDE).astype(LOW), spread_out)


def bias_masks(bucket_ref, bias_ref, mask_ref, block):
    buckets, heads = bias_ref.shape
    steps = bucket_ref.shape[0]
    spots = bucket_columns(bucket_ref, block)
    row = lax.broadcasted_iota(jnp.int32, (block, block), 0)
    column = lax.broadcasted_iota(jnp.int32, (block, block), 1)
    allowed = (row // steps == column // steps) & (row >= column)
    for head in range(heads):
        table = jnp.zeros(spots.shape, WIDE)
        for bucket in range(buckets):
            table = jnp.where(spots == bucket, bias_ref[bucket, head], table)
        tiled = jnp.concatenate([table] * (block // steps), axis=0)
        side = (head % 2) * block
        mask_ref[head // 2, :, side : side + block] = jnp.where(allowed, tiled, MASKED)


def pair_softmax(scores, block):
    parts = []
    for side in range(2):
        part = scores[:, side * block : (side + 1) * block]
        part = jnp.exp(part - jnp.max(part, axis=-1, keepdims=True))
        parts.append(part / jnp.sum(part, axis=-1, keepdims=True))
    return jnp.concatenate(parts, axis=1)


def line_of(ref):
    return ref[...].reshape(1, ref.shape[0])


def grad_of_token(score_ref, row_ref):
    row = line_of(row_ref).astype(WIDE)
    scores = jnp.broadcast_to(line_of(score_ref), (8, score_ref.shape[0])).T[:, :1]
    return scores * row.shape[1] ** (-0.5), row


def self_forward_part(
    scale, pairs, block, copies,
    dec_ref, self_gain_ref, cross_gain_ref, score_ref, row_ref, grad_hidden_ref, bucket_ref, bias_ref,
    act_one_ref, query_ref, key_ref, value_ref, mixed_ref, residual_ref, act_two_ref, query_two_ref, upstream_ref,
    weight_buf, mask_ref,
):
    tokens = dec_ref[...].astype(WIDE)
    act_one = (tokens * inverse_root(tokens) * line_of(self_gain_ref)).astype(LOW)
    act_one_ref[...] = act_one
    bias_masks(bucket_ref, bias_ref, mask_ref, block)
    scaled, row = grad_of_token(score_ref, row_ref)
    upstream_ref[...] = (grad_hidden_ref[...] + scaled * row).astype(LOW)
    for spot, ref in ((0, query_ref), (1, key_ref), (2, value_ref)):
        copies[spot].wait()
        ref[...] = mul(act_one, weight_buf[spot]).astype(LOW)
    for start in range(0, tokens.shape[0], block):
        for pair in range(pairs):
            rows, cols = slice(start, start + block), slice(pair * block, (pair + 1) * block)
            scores = mul_cols(query_ref[rows, cols], two_heads(key_ref[rows, cols])) * scale
            weights = pair_softmax(scores + mask_ref[pair], block).astype(LOW)
            mixed_ref[rows, cols] = mul(weights, two_heads(value_ref[rows, cols])).astype(LOW)
    copies[3].wait()
    residual = tokens + mul(mixed_ref[...], weight_buf[3])
    residual_ref[...] = residual
    act_two = (residual * inverse_root(residual) * line_of(cross_gain_ref)).astype(LOW)
    act_two_ref[...] = act_two
    copies[4].wait()
    query_two_ref[...] = mul(act_two, weight_buf[4]).astype(LOW)


def regroup_kernel(head_ref, rows_ref, chip_ref, far_ref, near_ref, own_ref):
    for near, ref in ((2, chip_ref), (3, far_ref), (1, near_ref), (0, own_ref)):
        ref[...] = rows_ref[head_ref[0] ^ near]


def regroup(order, head, rows):
    shape = shape_of(*rows.shape[1:])
    return order.run(regroup_kernel, (head, rows), [shape] * 4, [SCALARS, VMEM], [VMEM] * 4, [], 0, 0, "regroup")


def attend_mask(head_ref, key_segment_ref, slot_ref, mask_ref, spots):
    rows, length = key_segment_ref.shape
    slots = slot_ref.shape[1]
    head = head_ref[0]
    part = length // rows
    queries = mask_ref.shape[1]
    keys = jnp.concatenate(
        [
            key_segment_ref[pl.ds(head, 1), pl.ds(pl.multiple_of((head ^ spot) * part, part), part)]
            for spot in spots
        ],
        axis=1,
    )
    key_hot = hot((slots, keys.shape[1]), lambda row, column: row == keys)
    slot_segment = slot_ref[pl.ds(head, 1), :]
    slot_hot = hot((slots, slots), lambda row, column: row == slot_segment)
    ask_hot = mul(slot_hot, hot((slots, queries), lambda row, column: row == column // (queries // slots)))
    mask_ref[...] = jnp.where(mul_rows(key_hot, ask_hot.astype(LOW)) > 0.5, 0.0, MASKED)


def one_head(pair, side):
    width = pair.shape[1] // 2
    lane = lax.broadcasted_iota(jnp.int32, pair.shape, 1)
    return jnp.where((lane < width) == (side == 0), pair, jnp.zeros_like(pair))


def half_attention(pair, side, query, key_ref, value_t, mask_ref):
    lanes = BLOCK
    width = lanes // 2
    cols = slice(pair * lanes, (pair + 1) * lanes)
    spots = slice((2 * pair + side) * width, (2 * pair + side + 1) * width)
    scores = mul_cols(key_ref[:, cols], one_head(query, side)) + mask_ref[...]
    highest = jnp.max(scores, axis=0, keepdims=True)
    raised = jnp.exp(scores - highest)
    return highest, jnp.sum(raised, axis=0, keepdims=True), mul(value_t[spots], raised.astype(LOW)), spots


def cross_first_part(
    scale, pairs, copies,
    head_ref, first_ref, second_ref, key_segment_ref, slot_ref, query_ref,
    key_ref, value_ref, mixed_ref, highest_ref, mass_ref,
    weight_buf, mask_ref, value_t,
):
    attend_mask(head_ref, key_segment_ref, slot_ref, mask_ref, (0, 1))
    rows = first_ref.shape[0]
    for spot, ref in ((0, key_ref), (1, value_ref)):
        copies[spot].wait()
        ref[:rows] = mul(first_ref[...], weight_buf[spot]).astype(LOW)
        ref[rows:] = mul(second_ref[...], weight_buf[spot]).astype(LOW)
    value_t[...] = value_ref[...].T
    for pair in range(pairs):
        query = query_ref[:, pair * BLOCK : (pair + 1) * BLOCK] * scale
        for side in range(2):
            head = 2 * pair + side
            highest, mass, mixed, spots = half_attention(pair, side, query, key_ref, value_t, mask_ref)
            highest_ref[head : head + 1, :] = highest
            mass_ref[head : head + 1, :] = mass
            mixed_ref[spots] = mixed


def self_cross_kernel(
    scale, pairs,
    dec_ref, self_gain_ref, cross_gain_ref, score_ref, row_ref, grad_hidden_ref, bucket_ref, bias_ref,
    head_ref, first_ref, second_ref, key_segment_ref, slot_ref,
    query_w, key_w, value_w, output_w, cross_w, cross_key_w, cross_value_w,
    act_one_ref, query_ref, key_ref, value_ref, mixed_one_ref, residual_ref, act_two_ref, query_two_ref, upstream_ref,
    key_two_ref, value_two_ref, mixed_ref, highest_ref, mass_ref,
    weight_buf, bias_mask_ref, mask_ref, value_t, semaphores,
):
    sources = (query_w, key_w, value_w, output_w, cross_w, cross_key_w, cross_value_w)
    copies = load_all(sources, [weight_buf.at[i] for i in range(len(sources))], semaphores)
    self_forward_part(
        scale, pairs, BLOCK, copies,
        dec_ref, self_gain_ref, cross_gain_ref, score_ref, row_ref, grad_hidden_ref, bucket_ref, bias_ref,
        act_one_ref, query_ref, key_ref, value_ref, mixed_one_ref, residual_ref, act_two_ref, query_two_ref, upstream_ref,
        weight_buf, bias_mask_ref,
    )
    cross_first_part(
        scale, pairs, copies[5:],
        head_ref, first_ref, second_ref, key_segment_ref, slot_ref, query_two_ref,
        key_two_ref, value_two_ref, mixed_ref, highest_ref, mass_ref,
        weight_buf.at[5:], mask_ref, value_t,
    )


def self_cross(order, dec, self_gain, cross_gain, score, row, grad_hidden, bucket, bias, head, first, second, key_segment, slots, *weights):
    tokens, width = dec.shape
    heads = bias.shape[1]
    rows = first.shape[0]
    low, stat = shape_of(tokens, width), shape_of(heads, tokens, kind=WIDE)
    return order.run(
        functools.partial(self_cross_kernel, (width // heads) ** (-0.5), heads // 2),
        (dec, self_gain, cross_gain, score, row, grad_hidden, bucket, bias, head, first, second, key_segment, slots, *weights),
        [low] * 5 + [shape_of(tokens, width, kind=WIDE), low, low, low]
        + [shape_of(2 * rows, width)] * 2 + [shape_of(width, tokens, kind=WIDE), stat, stat],
        [VMEM] * 7 + [SCALARS] * 2 + [VMEM] * 4 + [HBM] * 7,
        [VMEM] * 14,
        [
            pltpu.VMEM((7, width, width), LOW),
            pltpu.VMEM((heads // 2, BLOCK, 2 * BLOCK), WIDE),
            pltpu.VMEM((2 * rows, tokens), WIDE),
            pltpu.VMEM((width, 2 * rows), LOW),
            pltpu.SemaphoreType.DMA((7,)),
        ],
        0, 0, "self_cross",
    )


def cross_last_part(
    scale, pairs, copies,
    head_ref, third_ref, fourth_ref, key_segment_ref, slot_ref, query_ref,
    mixed_a_ref, highest_a_ref, mass_a_ref, residual_ref, gain_ref,
    key_ref, value_ref, mixed_ref, totals_ref, residual_two_ref, act_ref,
    weight_buf, mask_ref, value_t,
):
    attend_mask(head_ref, key_segment_ref, slot_ref, mask_ref, (2, 3))
    rows = third_ref.shape[0]
    for spot, ref in ((0, key_ref), (1, value_ref)):
        copies[spot].wait()
        ref[:rows] = mul(third_ref[...], weight_buf[spot]).astype(LOW)
        ref[rows:] = mul(fourth_ref[...], weight_buf[spot]).astype(LOW)
    value_t[...] = value_ref[...].T
    for pair in range(pairs):
        query = query_ref[:, pair * BLOCK : (pair + 1) * BLOCK] * scale
        for side in range(2):
            head = 2 * pair + side
            line = slice(head, head + 1)
            highest, mass, mixed, spots = half_attention(pair, side, query, key_ref, value_t, mask_ref)
            top = jnp.maximum(highest, highest_a_ref[line, :])
            here, there = jnp.exp(highest - top), jnp.exp(highest_a_ref[line, :] - top)
            mass = mass * here + mass_a_ref[line, :] * there
            totals_ref[line, :] = top + jnp.log(mass)
            inverse = 1.0 / mass
            mixed_ref[spots] = (mixed * (here * inverse) + mixed_a_ref[spots] * (there * inverse)).astype(LOW)
    copies[2].wait()
    residual = residual_ref[...] + mul(mixed_ref[...].T, weight_buf[2])
    residual_two_ref[...] = residual
    act_ref[...] = (residual * inverse_root(residual) * line_of(gain_ref)).astype(LOW)


def gelu_parts(pre):
    root = 0.7978845608028654
    square = pre * pre
    curve = jnp.tanh(root * (pre + 0.044715 * (square * pre)))
    ahead = 0.5 * (1.0 + curve)
    slope = ahead + (0.5 * root) * pre * (1.0 - curve * curve) * (1.0 + (3 * 0.044715) * square)
    return (pre * ahead).astype(LOW), slope


def spread_quarters(core, turned, other_ref, at, mine_ref, spot):
    quarter = turned.shape[0] // 4
    first = core == 0
    for chip in range(2):
        even = turned[2 * chip * quarter : (2 * chip + 1) * quarter]
        odd = turned[(2 * chip + 1) * quarter : (2 * chip + 2) * quarter]
        mine_ref[spot + chip] = jnp.where(first, even, odd)
        other_ref[at + chip * quarter : at + (chip + 1) * quarter] = jnp.where(first, odd, even)


def cross_feed_kernel(
    scale, pairs,
    parts_ref, head_ref, third_ref, fourth_ref, key_segment_ref, slot_ref, query_ref,
    mixed_a_ref, highest_a_ref, mass_a_ref, residual_ref, gain_ref,
    upstream_low_ref, act_one_ref, mixed_one_ref, act_two_ref,
    key_w, value_w, output_w, feed_in, feed_out,
    key_ref, value_ref, totals_ref, residual_two_ref, act_ref,
    other_ref, grad_pre_ref, total_ref, upward_ref, mine_ref,
    weight_buf, mask_ref, value_t, mixed_ref, semaphores,
):
    part, width = grad_pre_ref.shape[2], act_ref.shape[1]
    columns = [pl.ds(pl.multiple_of(parts_ref[step] * part, part), part) for step in range(2)]
    sources = [key_w, value_w, output_w]
    for spot in columns:
        sources += [feed_in.at[:, spot], feed_out.at[spot]]
    copies = load_all(sources, [weight_buf.at[i] for i in range(len(sources))], semaphores)
    cross_last_part(
        scale, pairs, copies,
        head_ref, third_ref, fourth_ref, key_segment_ref, slot_ref, query_ref,
        mixed_a_ref, highest_a_ref, mass_a_ref, residual_ref, gain_ref,
        key_ref, value_ref, mixed_ref, totals_ref, residual_two_ref, act_ref,
        weight_buf, mask_ref, value_t,
    )
    turned = (act_ref[...].T, mixed_ref[...], act_one_ref[...].T, mixed_one_ref[...].T, act_two_ref[...].T)
    for spot, source in enumerate(turned):
        spread_quarters(parts_ref[2], source, other_ref, 2 * part + spot * width // 2, mine_ref, 2 * spot)
    other_ref[2 * part + len(turned) * width // 2 :] = upstream_low_ref[...].T
    for step in range(2):
        copies[3 + 2 * step].wait()
        copies[4 + 2 * step].wait()
        in_ref, out_ref = weight_buf.at[3 + 2 * step], weight_buf.at[4 + 2 * step]
        hidden, slope = gelu_parts(mul(act_ref[...], in_ref[...]))
        other_ref[step * part : (step + 1) * part] = hidden.T
        grad_pre = (mul_cols(upstream_low_ref[...], out_ref[...]) * slope).astype(LOW)
        grad_pre_ref[step] = grad_pre
        total, upward = mul(hidden, out_ref[...]), mul_cols(grad_pre, in_ref[...])
        if step == 0:
            total_ref[...], upward_ref[...] = total, upward
        else:
            total_ref[...] += total
            upward_ref[...] += upward


def cross_feed(order, parts, head, third, fourth, key_segment, slots, query, mixed, highest, mass, residual, gain, upstream_low, act_one, mixed_one, act_two, key_w, value_w, output_w, feed_in, feed_out, heads):
    tokens, width = query.shape
    rows = third.shape[0]
    part = feed_in.shape[1] // 4
    height = 2 * part + 5 * width // 2 + width
    tall, wide = shape_of(2 * rows, width), shape_of(tokens, width, kind=WIDE)
    return order.run(
        functools.partial(cross_feed_kernel, (width // heads) ** (-0.5), heads // 2),
        (
            parts, head, third, fourth, key_segment, slots, query, mixed, highest, mass, residual, gain,
            upstream_low, act_one, mixed_one, act_two, key_w, value_w, output_w, feed_in, feed_out,
        ),
        [
            tall, tall, shape_of(heads, tokens, kind=WIDE), wide, shape_of(tokens, width),
            shape_of(height, tokens), shape_of(2, tokens, part), wide, wide, shape_of(10, width // 4, tokens),
        ],
        [SCALARS] * 2 + [VMEM] * 14 + [HBM] * 5,
        [VMEM] * 10,
        [
            pltpu.VMEM((7, width, width), LOW), pltpu.VMEM((2 * rows, tokens), WIDE),
            pltpu.VMEM((width, 2 * rows), LOW), pltpu.VMEM((width, tokens), LOW), pltpu.SemaphoreType.DMA((7,)),
        ],
        0, 0, "cross_feed",
    )


def feed_last_kernel(
    parts_ref,
    act_ref, upstream_low_ref, in_total_ref, in_upward_ref, score_ref, row_ref, gain_ref,
    residual_hbm, grad_hidden_hbm, feed_in, feed_out, cross_w,
    hidden_ref, grad_pre_ref,
    result_ref, ranking_ref, row_grad_ref, gain_grad_ref, grad_two_ref, grad_two_low_ref, grad_mixed_ref,
    weight_buf, wide_buf, semaphores,
):
    part = grad_pre_ref.shape[2]
    columns = [pl.ds(pl.multiple_of(parts_ref[2 + step] * part, part), part) for step in range(2)]
    sources = []
    for spot in columns:
        sources += [feed_in.at[:, spot], feed_out.at[spot]]
    copies = load_all(
        sources + [residual_hbm, grad_hidden_hbm, cross_w],
        [weight_buf.at[i] for i in range(4)] + [wide_buf.at[0], wide_buf.at[1], weight_buf.at[4]],
        semaphores,
    )
    total, upward = in_total_ref[...], in_upward_ref[...]
    for step in range(2):
        copies[2 * step].wait()
        copies[2 * step + 1].wait()
        in_ref, out_ref = weight_buf.at[2 * step], weight_buf.at[2 * step + 1]
        hidden, slope = gelu_parts(mul(act_ref[...], in_ref[...]))
        hidden_ref[step] = hidden.T
        grad_pre = (mul_cols(upstream_low_ref[...], out_ref[...]) * slope).astype(LOW)
        grad_pre_ref[step] = grad_pre
        total = total + mul(hidden, out_ref[...])
        upward = upward + mul_cols(grad_pre, in_ref[...])
    copies[4].wait()
    copies[5].wait()
    residual = wide_buf[0]
    scaled, row = grad_of_token(score_ref, row_ref)
    final = residual + total
    result_ref[...] = final.astype(LOW)
    ranking = jnp.sum(final * row, axis=-1, keepdims=True) * row.shape[1] ** (-0.5)
    ranking_ref[...] = jnp.broadcast_to(ranking, (ranking.shape[0], BLOCK)).T[:1]
    row_grad_ref[...] = jnp.sum(scaled * final, axis=0, keepdims=True)
    back, gain_grad = norm_grads(residual, line_of(gain_ref), upward)
    gain_grad_ref[...] = gain_grad
    grad_two = wide_buf[1] + scaled * row + back
    grad_two_ref[...] = grad_two
    grad_two_low = grad_two.astype(LOW)
    grad_two_low_ref[...] = grad_two_low
    copies[6].wait()
    grad_mixed_ref[...] = mul_cols(grad_two_low, weight_buf[4]).astype(LOW)


def feed_last(order, parts, act, upstream_low, total, upward, residual, grad_hidden, score, row, gain, feed_in, feed_out, cross_output):
    tokens, width = act.shape
    part = feed_in.shape[1] // 4
    low, line = shape_of(tokens, width), shape_of(1, width, kind=WIDE)
    return order.run(
        feed_last_kernel,
        (parts, act, upstream_low, total, upward, score, row, gain, residual, grad_hidden, feed_in, feed_out, cross_output),
        [
            shape_of(2, part, tokens), shape_of(2, tokens, part),
            low, shape_of(1, tokens, kind=WIDE), line, line, shape_of(tokens, width, kind=WIDE), low, low,
        ],
        [SCALARS] + [VMEM] * 7 + [HBM] * 5,
        [VMEM] * 9,
        [pltpu.VMEM((5, width, part), LOW), pltpu.VMEM((2, tokens, width), WIDE), pltpu.SemaphoreType.DMA((7,))],
        0, 0, "feed_last",
    )


def cross_backward_part(
    scale, pairs, copies,
    head_ref, query_ref, key_a_ref, value_a_ref, key_b_ref, value_b_ref, totals_ref, grad_mixed_ref,
    key_segment_ref, slot_ref, residual_ref, gain_ref, grad_two_ref,
    asked_ref, kept_ref,
    grad_one_ref, grad_mixed_one_ref, gain_grad_ref,
    weight_buf, mask_ref, key_t, query_t,
):
    attend_mask(head_ref, key_segment_ref, slot_ref, mask_ref, (0, 1, 2, 3))
    half = key_a_ref.shape[0]
    lanes = 128
    key_t[:, :half] = key_a_ref[...].T
    key_t[:, half:] = key_b_ref[...].T
    for pair in range(pairs):
        cols = slice(pair * lanes, (pair + 1) * lanes)
        query = query_ref[:, cols] * scale
        keys = (key_a_ref, key_b_ref)
        values = (value_a_ref, value_b_ref)
        key_parts = [[], []]
        value_parts = [[], []]
        for side in range(2):
            ask = one_head(query, side)
            grad = one_head(grad_mixed_ref[:, cols], side)
            head = 2 * pair + side
            total = totals_ref[head : head + 1, :]
            weights, grad_weights = [], []
            for spot in range(2):
                rows = slice(spot * half, (spot + 1) * half)
                scores = mul_cols(keys[spot][:, cols], ask) + mask_ref[rows]
                weights.append(jnp.exp(scores - total))
                grad_weights.append(mul_cols(values[spot][:, cols], grad))
            dots = sum(
                jnp.sum(one * other, axis=0, keepdims=True) for one, other in zip(weights, grad_weights)
            )
            spots = slice(head * (lanes // 2), (head + 1) * (lanes // 2))
            part = 0.0
            for spot in range(2):
                grad_scores = (weights[spot] * (grad_weights[spot] - dots)).astype(LOW)
                part += mul(key_t[spots, spot * half : (spot + 1) * half], grad_scores)
                key_parts[spot].append(mul(grad_scores, ask))
                value_parts[spot].append(mul(weights[spot].astype(LOW), grad))
            query_t[spots] = (part * scale).astype(LOW)
        for spot in range(2):
            rows = slice(spot * half, (spot + 1) * half)
            kept_ref[0, rows, cols] = (key_parts[spot][0] + key_parts[spot][1]).astype(LOW)
            kept_ref[1, rows, cols] = (value_parts[spot][0] + value_parts[spot][1]).astype(LOW)
    asked_ref[0] = query_t[...].T
    copies[0].wait()
    back, gain_grad = norm_grads(
        residual_ref[...], line_of(gain_ref), mul_cols(asked_ref[0], weight_buf[0])
    )
    gain_grad_ref[...] = gain_grad
    grad_one = grad_two_ref[...] + back
    grad_one_ref[...] = grad_one
    grad_one_low = grad_one.astype(LOW)
    asked_ref[1] = grad_one_low
    copies[1].wait()
    grad_mixed_one_ref[...] = mul_cols(grad_one_low, weight_buf[1]).astype(LOW)


def self_backward_part(
    scale, pairs, block, copies,
    query_ref, key_ref, value_ref, grad_mixed_ref, dec_ref, gain_ref, grad_one_ref, bucket_ref,
    asked_ref, cross_gain_ref, feed_gain_ref, row_grad_ref, bias_ref,
    pack_ref, ask_ref, result_ref,
    weight_buf, mask_ref, table_ref, bias_grad, small,
):
    tokens = dec_ref.shape[0]
    steps = bucket_ref.shape[0]
    bias_masks(bucket_ref, bias_ref, mask_ref, block)
    for pair in range(pairs):
        table = jnp.zeros((steps, 2 * block), WIDE)
        for start in range(0, dec_ref.shape[0], block):
            rows, cols = slice(start, start + block), slice(pair * block, (pair + 1) * block)
            query, keys, values = query_ref[rows, cols], two_heads(key_ref[rows, cols]), two_heads(value_ref[rows, cols])
            grad = grad_mixed_ref[rows, cols]
            weights = pair_softmax(mul_cols(query, keys) * scale + mask_ref[pair], block)
            grad_weights = mul_cols(grad, values)
            product = weights * grad_weights
            grad_scores = jnp.concatenate(
                [
                    product[:, side * block : (side + 1) * block]
                    - weights[:, side * block : (side + 1) * block]
                    * jnp.sum(product[:, side * block : (side + 1) * block], axis=-1, keepdims=True)
                    for side in range(2)
                ],
                axis=1,
            ).astype(LOW)
            table += jnp.sum(grad_scores.astype(WIDE).reshape(block // steps, steps, 2 * block), axis=0)
            pack_ref[0 * tokens + start : 0 * tokens + start + block, cols] = (mul(grad_scores, keys) * scale).astype(LOW)
            key_parts = mul_rows(grad_scores, query)
            value_parts = mul_rows(weights.astype(LOW), grad)
            lane = lax.broadcasted_iota(jnp.int32, (block, block), 1) < block // 2
            pack_ref[1 * tokens + start : 1 * tokens + start + block, cols] = (
                jnp.where(lane, key_parts[:block], key_parts[block:]) * scale
            ).astype(LOW)
            pack_ref[2 * tokens + start : 2 * tokens + start + block, cols] = jnp.where(lane, value_parts[:block], value_parts[block:]).astype(LOW)
        table_ref[pair] = table
    spots = bucket_columns(bucket_ref, block)
    for bucket in range(bias_ref.shape[0]):
        hit = jnp.concatenate([spots == bucket] * 2, axis=1)
        for pair in range(pairs):
            kept = jnp.sum(jnp.where(hit, table_ref[pair], 0.0), axis=0, keepdims=True)
            bias_grad[2 * pair, bucket : bucket + 1, :] = kept[:, :block]
            bias_grad[2 * pair + 1, bucket : bucket + 1, :] = kept[:, block:]
    upward = 0.0
    for spot in range(3):
        copies[spot].wait()
        upward += mul_cols(pack_ref[spot * tokens : (spot + 1) * tokens], weight_buf[spot])
    back, gain_grad = norm_grads(dec_ref[...].astype(WIDE), line_of(gain_ref), upward)
    small[...] = jnp.zeros_like(small)
    for row, value in enumerate((gain_grad, cross_gain_ref[...], feed_gain_ref[...], row_grad_ref[...])):
        small[row : row + 1, :] = value
    heads, buckets, _ = bias_grad.shape
    small[4 : 4 + heads, :buckets] = jnp.sum(bias_grad[...], axis=-1)
    ask_ref[:tokens] = asked_ref[0]
    ask_ref[tokens : 2 * tokens] = asked_ref[1]
    ask_ref[2 * tokens :] = small[...].astype(LOW)
    result_ref[...] = grad_one_ref[...] + back


def backward_kernel(
    scale, pairs,
    head_ref, query_two_ref, key_a_ref, value_a_ref, key_b_ref, value_b_ref, totals_ref, grad_mixed_ref,
    key_segment_ref, slot_ref, residual_ref, cross_gain_ref, grad_two_ref,
    query_ref, key_ref, value_ref, dec_ref, self_gain_ref, bucket_ref, feed_gain_grad_ref, row_grad_ref, bias_ref,
    cross_query_w, output_w, query_w, key_w, value_w,
    kept_ref, pack_ref, ask_ref, result_ref,
    weight_buf, mask_ref, key_t, query_t, asked, grad_one, grad_mixed_one, gain_grad,
    bias_mask_ref, table_ref, bias_grad, small, semaphores,
):
    sources = (cross_query_w, output_w, query_w, key_w, value_w)
    copies = load_all(sources, [weight_buf.at[i] for i in range(len(sources))], semaphores)
    cross_backward_part(
        scale, pairs, copies,
        head_ref, query_two_ref, key_a_ref, value_a_ref, key_b_ref, value_b_ref, totals_ref, grad_mixed_ref,
        key_segment_ref, slot_ref, residual_ref, cross_gain_ref, grad_two_ref,
        asked, kept_ref, grad_one, grad_mixed_one, gain_grad,
        weight_buf, mask_ref, key_t, query_t,
    )
    self_backward_part(
        scale, pairs, BLOCK, copies[2:],
        query_ref, key_ref, value_ref, grad_mixed_one, dec_ref, self_gain_ref, grad_one, bucket_ref,
        asked, gain_grad, feed_gain_grad_ref, row_grad_ref, bias_ref,
        pack_ref, ask_ref, result_ref,
        weight_buf.at[2:], bias_mask_ref, table_ref, bias_grad, small,
    )


def backward(order, head, query_two, key_a, value_a, key_b, value_b, totals, grad_mixed, key_segment, slots, residual, cross_gain, grad_two, query, key, value, dec, self_gain, bucket, feed_gain_grad, row_grad, bias, *weights):
    tokens, width = query.shape
    buckets, heads = bias.shape
    keys = 2 * key_a.shape[0]
    rest = -(-(4 + heads) // 16) * 16
    return order.run(
        functools.partial(backward_kernel, (width // heads) ** (-0.5), heads // 2),
        (
            head, query_two, key_a, value_a, key_b, value_b, totals, grad_mixed, key_segment, slots, residual, cross_gain,
            grad_two, query, key, value, dec, self_gain, bucket, feed_gain_grad, row_grad, bias, *weights,
        ),
        [
            shape_of(2, keys, width), shape_of(3 * tokens, width), shape_of(2 * tokens + rest, width),
            shape_of(tokens, width, kind=WIDE),
        ],
        [SCALARS] + [VMEM] * 20 + [SCALARS] + [HBM] * 5,
        [VMEM] * 4,
        [
            pltpu.VMEM((5, width, width), LOW),
            pltpu.VMEM((keys, tokens), WIDE),
            pltpu.VMEM((width, keys), LOW),
            pltpu.VMEM((width, tokens), LOW),
            pltpu.VMEM((2, tokens, width), LOW),
            pltpu.VMEM((tokens, width), WIDE),
            pltpu.VMEM((tokens, width), LOW),
            pltpu.VMEM((1, width), WIDE),
            pltpu.VMEM((heads // 2, BLOCK, 2 * BLOCK), WIDE),
            pltpu.VMEM((heads // 2, bucket.shape[0], 2 * BLOCK), WIDE),
            pltpu.VMEM((heads, buckets, BLOCK), WIDE),
            pltpu.VMEM((rest, width), WIDE),
            pltpu.SemaphoreType.DMA((5,)),
        ],
        0, 0, "backward",
    )


def encoder_weights_kernel(core_ref, first_ref, second_ref, third_ref, fourth_ref, grads_ref, other_ref, mine_ref, turned, whole):
    for spot, ref in enumerate((first_ref, second_ref, third_ref, fourth_ref)):
        rows = ref.shape[0]
        turned[:, spot * rows : (spot + 1) * rows] = ref[...].T
    quarter = whole.shape[0] // 4
    core = core_ref[0]
    for weight in range(2):
        whole[...] = mul(turned[...], grads_ref[weight]).astype(LOW)
        for chip in range(2):
            at = lambda side: pl.ds(pl.multiple_of((2 * chip + side) * quarter, quarter), quarter)
            mine_ref[weight, chip] = whole[at(core)]
            other_ref[weight, chip] = whole[at(1 - core)]


def encoder_weights(order, core, rows, grads):
    count, width = rows[0].shape
    shape = shape_of(2, 2, width // 4, width)
    return order.run(
        encoder_weights_kernel,
        (core, *rows, grads),
        [shape] * 2,
        [SCALARS] + [VMEM] * 5,
        [VMEM] * 2,
        [pltpu.VMEM((width, 4 * count), LOW), pltpu.VMEM((width, width), LOW)],
        16 * count * width * width, 8 * width * width, "encoder_weights",
    )


def encoder_rows_kernel(grads_ref, key_w, value_w, own_ref, near_ref, chip_ref, weight_buf, semaphores):
    copies = load_all((key_w, value_w), [weight_buf.at[0], weight_buf.at[1]], semaphores)
    for copy in copies:
        copy.wait()
    rows = own_ref.shape[0]
    for ref, start in ((own_ref, 0), (near_ref, rows), (chip_ref, 2 * rows)):
        part = slice(start, start + ref.shape[0])
        grad = mul_cols(grads_ref[0, part], weight_buf[0]) + mul_cols(grads_ref[1, part], weight_buf[1])
        ref[...] = grad.astype(ref.dtype)


def encoder_rows(order, grads, key_w, value_w):
    rows, width = grads.shape[1] // 4, grads.shape[2]
    return order.run(
        encoder_rows_kernel,
        (grads, key_w, value_w),
        [shape_of(rows, width, kind=WIDE), shape_of(rows, width), shape_of(2 * rows, width)],
        [VMEM] + [HBM] * 2,
        [VMEM] * 3,
        [pltpu.VMEM((2, width, width), LOW), pltpu.SemaphoreType.DMA((2,))],
        16 * rows * width * width, 8 * width * width, "encoder_rows",
    )


def stage_kernel(mode, weights, rows, extra, count, place_ref, *refs):
    stage, way = mode
    chip, pair = place_ref[0], place_ref[1]
    inputs, outs = refs[:count], refs[count:]

    def columns(matrix, side):
        if side is None:
            return matrix
        half = matrix.shape[1] // 2
        return jnp.where((pair == 0) == (side == 0), matrix[:, :half], matrix[:, half:])

    def value(weight, quarter, side):
        if len(weight) == 3:
            here, came, row = weight
            return columns(inputs[here][row:].astype(WIDE) + inputs[came][row:].astype(WIDE), side)
        if len(weight) == 4:
            here, spot, came, other = weight
            return columns(
                inputs[here][spot, quarter].astype(WIDE) + inputs[came][other, quarter].astype(WIDE), side
            )
        here, base, came, at, grads, grads_came, row = weight
        size, tokens = inputs[here].shape[1:]
        there = inputs[came][pl.ds(pl.multiple_of(at + quarter * size, 64), size)]
        if grads_came == came:
            near, far = inputs[grads][...], columns(mul_cols(there, inputs[came][row:]), side)
        else:
            spots = slice(row, row + tokens)
            near, far = inputs[grads][spots], mul(there, columns(inputs[grads_came][spots], side))
        return mul(inputs[here][base + quarter], columns(near, side)) + far

    at = 0
    for weight in list(weights) + ([] if extra is None else [extra]):
        if way == PAIR:
            totals = [value(weight, quarter, 1 if stage == 0 else 0) for quarter in range(2)]
        else:
            total = value(weight, (1 - chip) if stage == 0 else chip, None)
            half = total.shape[1] // 2
            totals = [total[:, :half], total[:, half:]]
        spots = slice(at, at + totals[0].shape[0])
        at = spots.stop
        if stage == 1:
            totals = [total + inputs[-1][part, spots].astype(WIDE) for part, total in enumerate(totals)]
        totals = [total.astype(LOW) for total in totals]
        if stage == 0 or way == WHOLE:
            outs[0][0, spots] = totals[0]
            outs[0][1, spots] = totals[1]
        else:
            low = (chip if way == PAIR else pair) == 0
            outs[0][spots] = jnp.where(low, totals[1], totals[0])
            outs[1][spots] = jnp.where(low, totals[0], totals[1])


def stage(order, spots, mode, weights, extra=None, came=None):
    arrays, described = [], []

    def spot_of(array):
        for spot, known in enumerate(arrays):
            if known is array:
                return spot
        arrays.append(array)
        return len(arrays) - 1

    for weight in weights:
        if len(weight) == 4:
            here, spot, other, member = weight
            described.append((spot_of(here), spot, spot_of(other), member))
            rows, columns = here.shape[-2:]
        else:
            here, base, other, at, grads, grads_came, row = weight
            described.append((spot_of(here), base, spot_of(other), at, spot_of(grads), spot_of(grads_came), row))
            rows, columns = here.shape[1], grads.shape[1]
    height = rows * len(weights)
    if extra is not None:
        height += extra[0].shape[0] - extra[2]
        extra = (spot_of(extra[0]), spot_of(extra[1]), extra[2])
    if came is not None:
        arrays.append(came)
    if mode[0] == 0 or mode[1] == WHOLE:
        shapes = [shape_of(2, height, columns // 2)]
    else:
        shapes = [shape_of(height, columns // 2)] * 2
    return order.run(
        functools.partial(stage_kernel, mode, described, rows, extra, len(arrays)),
        (spots, *arrays),
        shapes,
        [SCALARS] + [VMEM] * len(arrays),
        [VMEM] * len(shapes),
        [],
        0, 0, "stage", room=20,
    )


def feed_in_kernel(stage_index, place_ref, here_ref, came_ref, first_ref, last_ref, first_came_ref, last_came_ref, *refs):
    chip, pair, core = place_ref[0], place_ref[1], place_ref[2]
    half = pair if stage_index else 1 - pair
    part = last_ref.shape[2]
    low = chip == 0
    for side, (own, other) in enumerate(((last_ref, first_came_ref), (first_ref, last_came_ref))):
        block = core if side == 0 else 1 - core
        columns = pl.ds(pl.multiple_of(block * part, part), part)
        totals = []
        for quarter in range(2):
            size = here_ref.shape[1]
            start = 2 * part + quarter * size
            total = mul(here_ref[quarter], own[half]) + mul(came_ref[start : start + size], other[half])
            if stage_index:
                total += refs[0][quarter, :, columns].astype(WIDE)
            totals.append(total.astype(LOW))
        if stage_index:
            refs[1][:, columns] = jnp.where(low, totals[1], totals[0])
            refs[2][:, columns] = jnp.where(low, totals[0], totals[1])
        else:
            refs[0][0, :, columns] = totals[0]
            refs[0][1, :, columns] = totals[1]


def feed_in_stage(order, spots, stage_index, here, came, first, last, first_came, last_came, arrived=None):
    arrays = [here, came, first, last, first_came, last_came] + ([] if arrived is None else [arrived])
    rows = here.shape[1]
    half = 2 * first.shape[2]
    shapes = [shape_of(rows, half)] * 2 if stage_index else [shape_of(2, rows, half)]
    return order.run(
        functools.partial(feed_in_kernel, stage_index),
        (spots, *arrays),
        shapes,
        [SCALARS] + [VMEM] * len(arrays),
        [VMEM] * len(shapes),
        [],
        0, 0, "feed_in_stage", room=20,
    )


def combine_kernel(way, heights, place_ref, *refs):
    line, length = place_ref[3], place_ref[4]
    left = line < length // 2
    takes = (line == 0) | (line == length - 1)

    def add(first, second):
        return (first.astype(WIDE) + second.astype(WIDE)).astype(LOW)

    if way == ADD:
        refs[2][...] = add(refs[0][...], refs[1][...])
    elif way == SPLIT:
        sums = [add(refs[0][part], refs[1][part]) for part in range(2)]
        refs[2][...] = jnp.where(left, sums[0], sums[1])
        refs[3][...] = jnp.where(left, sums[1], sums[0])
    elif way == JOIN:
        refs[2][0] = jnp.where(left, refs[0][...], refs[1][...])
        refs[2][1] = jnp.where(left, refs[1][...], refs[0][...])
    elif way == TAKE:
        refs[2][...] = jnp.where(takes, refs[1][...], refs[0][...])
    else:
        at = 0
        for index, height in enumerate(heights):
            spots = slice(at, at + height)
            at += height
            if way == COLUMNS:
                first = place_ref[1] == 0
                mine, came = refs[0][spots], refs[1][spots]
                parts = (jnp.where(first, mine, came), jnp.where(first, came, mine))
            else:
                parts = [jnp.where(takes, refs[1][part, spots], refs[0][part, spots]) for part in range(2)]
            half = parts[0].shape[1]
            refs[2 + index][:, :half] = parts[0].astype(WIDE)
            refs[2 + index][:, half:] = parts[1].astype(WIDE)


def combine(order, spots, way, mine, came, heights):
    if way == SPLIT:
        shapes = [shape_of(*mine.shape[1:])] * 2
    elif way == JOIN:
        shapes = [shape_of(2, *mine.shape)]
    elif way in (ADD, TAKE):
        shapes = [shape_of(*mine.shape)]
    else:
        shapes = [shape_of(height, 2 * mine.shape[-1], kind=WIDE) for height in heights]
    results = order.run(
        functools.partial(combine_kernel, way, heights),
        (spots, mine, came),
        shapes,
        [SCALARS] + [VMEM] * 2,
        [VMEM] * len(shapes),
        [],
        0, 0, NAMES[way], room=12,
    )
    return results[0] if way in (ADD, TAKE, JOIN) else results


def hand_on_kernel(*refs):
    for source, target in zip(refs[: len(refs) // 2], refs[len(refs) // 2 :]):
        target[...] = source[...]


def hand_on(order, *arrays):
    shapes = [shape_of(*array.shape, kind=array.dtype) for array in arrays]
    return order.run(
        hand_on_kernel, arrays, shapes, [VMEM] * len(arrays), [VMEM] * len(arrays), [], 0, 0, "hand_on", room=16
    )


def place_rows_kernel(head_ref, own_ref, core_ref, chip_ref, far_ref, out_ref):
    for spot, ref in enumerate((own_ref, core_ref, chip_ref, far_ref)):

        @pl.when(pl.program_id(0) == spot)
        def _():
            out_ref[0] = ref[...].astype(WIDE)


def place_rows(order, head, own, core, chip, far):
    rows, width = own.shape
    return order.run(
        place_rows_kernel,
        (head, own, core, chip, far),
        [shape_of(4, rows, width, kind=WIDE)],
        [pl.BlockSpec((rows, width), lambda step, head: (0, 0))] * 4,
        [pl.BlockSpec((1, rows, width), lambda step, head: (head[0] ^ step, 0, 0))],
        [],
        0, 24 * rows * width, "place_rows", grid=(4,), prefetch=1,
    )[0]


AXES = ("dp", "head")


def device_maps(dp_size, head_size):
    length = dp_size // 2
    half = length // 2

    def of(move):
        pairs = []
        for outer in range(dp_size):
            for inner in range(head_size):
                goal = move(outer // 2, outer % 2, inner)
                if goal is not None:
                    spot, side, place = goal
                    pairs.append(
                        (outer * head_size + inner, (2 * spot + side) * head_size + place)
                    )
        return pairs

    def along(first, first_goal):
        def step(spot, side, place):
            if spot == first:
                return (first_goal, side, place)
            if spot == length - 1 - first:
                return (length - 1 - first_goal, side, place)
            return None

        return of(step)

    return {
        CORE: of(lambda spot, side, place: (spot, side, place ^ 1)),
        CHIP: of(lambda spot, side, place: (spot, side, place ^ 2)),
        FAR: of(lambda spot, side, place: (spot, side, place ^ 3)),
        PAIR: of(lambda spot, side, place: (spot, 1 - side, place)),
        MIDDLE_PAIR: of(
            lambda spot, side, place: (spot, 1 - side, place) if spot in (half - 1, half) else None
        ),
        INWARD: [along(step, step + 1) for step in range(half - 1)],
        MIDDLE: along(half - 1, half),
        OUTWARD: [along(step + 1, step) for step in range(half - 1)],
    }


class Made:
    pass


class Place:
    def __init__(self):
        dp_size, head_size = lax.axis_size("dp"), lax.axis_size("head")
        self.maps = device_maps(dp_size, head_size)
        self.length = dp_size // 2
        self.head = lax.axis_index("head")
        self.chip, self.core = self.head // 2, self.head % 2
        dp_index = lax.axis_index("dp")
        self.pair, self.line = dp_index % 2, dp_index // 2

    def move(self, array, name):
        return lax.ppermute(array, AXES, self.maps[name])

    def inward(self, part):
        perms = self.maps[INWARD]
        for perm in perms[:-1]:
            part = add_low(part, lax.ppermute(part, AXES, perm))
        return part, lax.ppermute(part, AXES, perms[-1])

    def outward(self, part):
        perms = self.maps[OUTWARD]
        for step in range(len(perms) - 1, 0, -1):
            came = lax.ppermute(part, AXES, perms[step])
            part = jnp.where(self.takes(step), came, part)
        return part, lax.ppermute(part, AXES, perms[0])

    def takes(self, step):
        return (self.line == step) | (self.line == self.length - 1 - step)


def add_low(first, second):
    kind = first.dtype
    return (first.astype(jnp.float32) + second.astype(jnp.float32)).astype(kind)


def picks(*values):
    return jnp.stack([jnp.asarray(value, jnp.int32) for value in values])


class Group:
    def __init__(self, place, order, spots, mode):
        self.place, self.order, self.spots, self.mode = place, order, spots, mode
        self.steps = [SECOND] + (
            [SPLIT, ADD, ADD, JOIN, LINES]
            if mode == WHOLE
            else [ADD_INWARD, ADD_MIDDLE, ADD_OUTWARD, TAKE, COLUMNS]
        )

    def first(self, weights, extra=None):
        self.weights, self.extra = weights, extra
        (sent,) = stage(self.order, self.spots, (0, self.mode), weights, extra)
        rows = 0 if extra is None else extra[0].shape[0] - extra[2]
        self.heights = [(sent.shape[1] - rows) // len(weights)] * len(weights) + [rows] * (rows > 0)
        self.came = self.place.move(sent, PAIR if self.mode == PAIR else CHIP)

    def first_feed_in(self, parts):
        self.parts, self.weights = parts, None
        (sent,) = feed_in_stage(self.order, self.spots, 0, *parts)
        self.heights = [sent.shape[1]]
        self.came = self.place.move(sent, PAIR)

    def step(self):
        place = self.place
        way = self.steps.pop(0)
        if way == SECOND:
            if self.weights is None:
                results = feed_in_stage(self.order, self.spots, 1, *self.parts, self.came)
            else:
                results = stage(self.order, self.spots, (1, self.mode), self.weights, self.extra, self.came)
            if self.mode == WHOLE:
                self.part, self.came = place.inward(results[0])
            else:
                self.part = results[1]
                self.came = place.move(results[0], CHIP if self.mode == PAIR else PAIR)
            return
        result = combine(self.order, self.spots, ADD if way in ADDS else way, self.part, self.came, self.heights)
        if way == SPLIT:
            self.part, other = result
            self.came = place.move(other, MIDDLE)
        elif way == ADD:
            self.part = result
            self.came = place.move(result, MIDDLE_PAIR if self.steps[0] == ADD else MIDDLE)
        elif way in (JOIN, ADD_OUTWARD):
            self.part, self.came = place.outward(result)
        elif way == ADD_INWARD:
            self.part, self.came = place.inward(result)
        elif way == ADD_MIDDLE:
            self.part, self.came = result, place.move(result, MIDDLE)
        elif way == TAKE:
            self.part, self.came = result, place.move(result, PAIR)
        else:
            self.result = result


MODES = {OUT: CHIP, IN: PAIR, SELF: PAIR, ASK: CHIP, KEEP: CHIP}
SEQUENCE = (
    BACK, SELF_PASS, OUT, ENCODER, IN, SELF_FIRST, ASK_FIRST, KEEP_PASS, OUT, IN, KEEP_FIRST, OUT, SELF, ASK, SELF,
    IN, OUT, ASK, ROWS, KEEP, SELF, IN, OUT, KEEP, ASK, SELF, IN, OUT, ROWS_SEND, ASK, SELF, KEEP, IN, ASK, KEEP,
    SELF, KEEP, ASK, ROWS_PASS, KEEP, ROWS_LAST,
)


def body(
    decoder_in,
    encoder_out,
    encoder_segment,
    slot_segment,
    position_bucket,
    self_gain,
    self_query,
    self_key,
    self_value,
    self_output,
    position_bias,
    cross_gain,
    cross_query,
    cross_key,
    cross_value,
    cross_output,
    feed_gain,
    feed_in,
    feed_out,
    score_row,
    grad_hidden,
    grad_score,
):
    place = Place()
    model_width = decoder_in.shape[1]
    heads = position_bias.shape[1]
    tokens = decoder_in.shape[0]
    head_index, core = place.head, place.core
    core_list, head_list = picks(core), picks(head_index)
    spots = picks(place.chip, place.pair, core, place.line, place.length)
    order = Order()
    to_chip, to_far, to_near, own_rows = regroup(order, head_list, encoder_out)
    from_chip, from_far, from_near = place.move(to_chip, CHIP), place.move(to_far, FAR), place.move(to_near, CORE)
    rows = [own_rows, from_near, from_chip, from_far]
    (
        act_one, query_one, key_one, value_one, mixed_one, residual_one, act_two, query_two, upstream_low,
        key_a, value_a, mixed_a, highest, mass,
    ) = self_cross(
        order, decoder_in, self_gain, cross_gain, grad_score, score_row, grad_hidden, position_bucket, position_bias,
        head_list, own_rows, from_near, encoder_segment, slot_segment,
        self_query, self_key, self_value, self_output, cross_query, cross_key, cross_value,
    )
    feed_parts = picks(1 - core, 3 - core, core, 2 + core)
    key_b, value_b, totals, residual_two, act_three, feed_other, pre_first, total, upward, mine = cross_feed(
        order, feed_parts, head_list, from_chip, from_far, encoder_segment, slot_segment, query_two, mixed_a, highest,
        mass, residual_one, feed_gain, upstream_low, act_one, mixed_one, act_two,
        cross_key, cross_value, cross_output, feed_in, feed_out, heads,
    )
    feed_came, pre_first_came = place.move(feed_other, CORE), place.move(pre_first, CORE)
    (
        hidden_mine, pre_last, hidden_out, ranking, row_grad, feed_gain_grad, grad_two, grad_two_low, grad_mixed,
    ) = feed_last(
        order, feed_parts, act_three, upstream_low, total, upward, residual_two, grad_hidden, grad_score, score_row,
        feed_gain, feed_in, feed_out, cross_output,
    )
    pre_last_came, grad_two_came = place.move(pre_last, CORE), place.move(grad_two_low, CORE)
    groups = {name: Group(place, order, spots, MODES[name]) for name in MODES}
    half = model_width // 2
    acts = feed_out.shape[0] // 2
    groups[OUT].first([(hidden_mine, 0, feed_came, 0, upstream_low, feed_came, acts + 5 * half)])
    order.need(grad_two_came)
    groups[IN].first_feed_in((mine, feed_came, pre_first, pre_last, pre_first_came, pre_last_came))
    made = Made()

    def back():
        made.kept, made.grads, made.asked, made.decoder = backward(
            order, head_list, query_two, key_a, value_a, key_b, value_b, totals, grad_mixed, encoder_segment, slot_segment,
            residual_one, cross_gain, grad_two, query_one, key_one, value_one, decoder_in, self_gain, position_bucket,
            feed_gain_grad, row_grad, position_bias, cross_query, self_output, self_query, self_key, self_value,
        )

    def self_pass():
        made.asked_came, made.grads_came = place.move(made.asked, CORE), place.move(made.grads, CORE)

    def self_copy():
        copies = hand_on(order, made.asked, made.grads)
        made.asked_came, made.grads_came = [place.move(copy, CORE) for copy in copies]

    def keep_copy():
        (other,) = hand_on(order, made.other)
        made.came = place.move(other, CORE)

    def keep_pass():
        made.came = place.move(made.other, CORE)

    def self_first():
        grads = made.grads
        groups[SELF].first(
            [(mine, 4, feed_came, acts + 2 * half, grads, made.grads_came, spot * tokens) for spot in range(3)]
        )

    def ask_first():
        asked, asked_came = made.asked, made.asked_came
        groups[ASK].first(
            [
                (mine, 2, feed_came, acts + half, grad_two_low, grad_two_came, 0),
                (mine, 8, feed_came, acts + 4 * half, asked, asked_came, 0),
                (mine, 6, feed_came, acts + 3 * half, asked, asked_came, tokens),
            ],
            (asked, asked_came, 2 * tokens),
        )

    def encoder_step():
        made.other, made.mine = encoder_weights(order, core_list, rows, made.kept)

    def keep_first():
        groups[KEEP].first([(made.mine, spot, made.came, spot) for spot in range(2)])

    def rows_step():
        made.own, made.to_near, made.to_chip = encoder_rows(order, made.kept, cross_key, cross_value)

    def rows_send():
        near, chip = hand_on(order, made.to_near, made.to_chip)
        made.chip, made.near = place.move(chip, CHIP), place.move(near, CORE)

    def rows_pass():
        count = made.chip.shape[0] // 2
        order.need(made.near)
        made.far = place.move(made.chip[count:], CORE)

    def rows_last():
        made.rows = place_rows(order, head_list, made.own, made.near, made.chip, made.far)

    tasks = {
        ASK_FIRST: ask_first,
        SELF_FIRST: self_first,
        SELF_PASS: self_pass,
        BACK: back,
        KEEP_PASS: keep_pass,
        SELF_COPY: self_copy,
        KEEP_COPY: keep_copy,
        ROWS_SEND: rows_send,
        KEEP_FIRST: keep_first,
        ENCODER: encoder_step,
        ROWS: rows_step,
        ROWS_PASS: rows_pass,
        ROWS_LAST: rows_last,
        NEED_KEEP: lambda: order.need(made.came),
    }
    for name in SEQUENCE:
        tasks.get(name, lambda: groups[name].step())()
    feed_out_grad, feed_in_grad = groups[OUT].result[0], groups[IN].result[0]
    self_query_grad, self_key_grad, self_value_grad = groups[SELF].result
    cross_output_grad, cross_query_grad, self_output_grad, small = groups[ASK].result
    cross_key_grad, cross_value_grad = groups[KEEP].result
    encoder_grad = made.rows
    width = model_width // 4
    gains = lax.dynamic_slice_in_dim(small[:4], head_index * width, width, axis=1)
    buckets = position_bias.shape[0] // 4
    bias_grad = lax.dynamic_slice_in_dim(small[4 : 4 + heads], head_index * buckets, buckets, axis=1).T
    return (
        hidden_out,
        ranking[0],
        made.decoder,
        encoder_grad,
        gains[0],
        self_query_grad,
        self_key_grad,
        self_value_grad,
        self_output_grad,
        bias_grad,
        gains[1],
        cross_query_grad,
        cross_key_grad,
        cross_value_grad,
        cross_output_grad,
        gains[2],
        feed_in_grad,
        feed_out_grad,
        gains[3],
    )


def solution(mesh):
    in_specs = (
        P(("dp", "head"), None),
        P("dp", "head", None),
        P("dp", None),
        P("dp", None),
        P(),
        P(),
        P(),
        P(),
        P(),
        P(),
        P(),
        P(),
        P(),
        P(),
        P(),
        P(),
        P(),
        P(),
        P(),
        P(),
        P(("dp", "head"), None),
        P(("dp", "head")),
    )
    out_specs = (
        P(("dp", "head"), None),
        P(("dp", "head")),
        P(("dp", "head"), None),
        P("dp", "head", None),
        P("head"),
        P("head", None),
        P("head", None),
        P("head", None),
        P("head", None),
        P("head", None),
        P("head"),
        P("head", None),
        P("head", None),
        P("head", None),
        P("head", None),
        P("head"),
        P("head", None),
        P("head", None),
        P("head"),
    )
    return jax.shard_map(body, mesh=mesh, in_specs=in_specs, out_specs=out_specs, check_vma=False)
```

```python
import functools
import jax
import jax.numpy as jnp
from jax import lax
from jax.experimental import pallas as pl
from jax.experimental.pallas import tpu as pltpu
from jax.sharding import PartitionSpec as P

EPSILON = 1e-06
MASKED = -1e30
HBM = pl.BlockSpec(memory_space=pl.ANY)
VMEM = pl.BlockSpec(memory_space=pltpu.VMEM)
SCALARS = pl.BlockSpec(memory_space=pltpu.SMEM)
LOW = jnp.bfloat16
BLOCK = 128
CHIP, PAIR, WHOLE, CORE, FAR, MIDDLE, MIDDLE_PAIR, INWARD, OUTWARD = range(9)
SECOND, SPLIT, ADD, JOIN, LINES, ADD_INWARD, ADD_MIDDLE, ADD_OUTWARD, TAKE, COLUMNS = range(10)
ADDS = (ADD_INWARD, ADD_MIDDLE, ADD_OUTWARD)
NAMES = {SPLIT: "combine_split", ADD: "combine_add", JOIN: "combine_join", LINES: "combine_rows"}
NAMES.update({TAKE: "combine_take", COLUMNS: "combine_columns"})
(
    OUT, IN, ASK, SELF, KEEP, BACK, SELF_PASS, SELF_COPY, ENCODER, KEEP_PASS, KEEP_COPY, NEED_KEEP, ASK_FIRST,
    SELF_FIRST, KEEP_FIRST, ROWS, ROWS_SEND, ROWS_PASS, ROWS_LAST,
) = range(19)
WIDE = jnp.float32


def shape_of(*dims, kind=LOW):
    return jax.ShapeDtypeStruct(dims, kind)


def params(megabytes=56):
    return pltpu.CompilerParams(vmem_limit_bytes=megabytes * 2**20)


def cost(flops, bytes_moved=0):
    return pl.CostEstimate(flops=flops, bytes_accessed=bytes_moved, transcendentals=0)


class Order:
    last = None

    def __init__(self):
        self.wanted = []

    def need(self, *arrays):
        self.wanted += arrays

    def run(self, kernel, args, out_shape, in_specs, out_specs, scratch_shapes, flops, moved, name, grid=None, prefetch=0, room=56):
        count = len(args)
        extra = ([] if self.last is None else [self.last]) + self.wanted
        self.wanted = []

        def ordered(*refs):
            kernel(*refs[:count], *refs[count + len(extra) :])

        specs = dict(in_specs=list(in_specs) + [HBM] * len(extra), out_specs=out_specs)
        if grid is None:
            specs["scratch_shapes"] = scratch_shapes
        else:
            specs = dict(
                grid_spec=pltpu.PrefetchScalarGridSpec(
                    num_scalar_prefetch=prefetch, grid=grid, scratch_shapes=scratch_shapes, **specs
                )
            )
        results = pl.pallas_call(
            ordered, out_shape=out_shape, compiler_params=params(room), cost_estimate=cost(1, 1), name=name, **specs
        )(*args, *extra)
        self.last = min(results, key=lambda result: result.size)
        return results


def mul(first, second):
    return jnp.dot(first, second, preferred_element_type=WIDE)


def mul_cols(first, second):
    return lax.dot_general(
        first, second, (((1,), (1,)), ((), ())), preferred_element_type=WIDE
    )


def mul_rows(first, second):
    return lax.dot_general(
        first, second, (((0,), (0,)), ((), ())), preferred_element_type=WIDE
    )


def inverse_root(hidden):
    return lax.rsqrt(jnp.mean(hidden * hidden, axis=-1, keepdims=True) + EPSILON)


def norm_grads(hidden, gain, upstream):
    inverse = inverse_root(hidden)
    scaled = hidden * inverse
    gain_grad = jnp.sum(upstream * scaled, axis=0, keepdims=True)
    weighted = upstream * gain
    dots = jnp.mean(weighted * scaled, axis=-1, keepdims=True)
    return inverse * (weighted - scaled * dots), gain_grad


def load_all(sources, buffers, semaphores):
    copies = [
        pltpu.make_async_copy(source, buffer, semaphores.at[spot])
        for spot, (source, buffer) in enumerate(zip(sources, buffers))
    ]
    for copy in copies:
        copy.start()
    return copies


def two_heads(pair):
    width = pair.shape[1] // 2
    lane = lax.broadcasted_iota(jnp.int32, pair.shape, 1)
    zero = jnp.zeros_like(pair)
    return jnp.concatenate(
        [jnp.where(lane < width, pair, zero), jnp.where(lane < width, zero, pair)], axis=0
    )


def hot(shape, allowed):
    row = lax.broadcasted_iota(jnp.int32, shape, 0)
    column = lax.broadcasted_iota(jnp.int32, shape, 1)
    return jnp.where(allowed(row, column), jnp.ones((), WIDE), jnp.zeros((), WIDE)).astype(LOW)


def bucket_columns(bucket_ref, block):
    steps = bucket_ref.shape[0]
    spread_out = hot((steps, block), lambda row, column: row == column % steps)
    return mul(bucket_ref[...].astype(WIDE).astype(LOW), spread_out)


def bias_masks(bucket_ref, bias_ref, mask_ref, block):
    buckets, heads = bias_ref.shape
    steps = bucket_ref.shape[0]
    spots = bucket_columns(bucket_ref, block)
    row = lax.broadcasted_iota(jnp.int32, (block, block), 0)
    column = lax.broadcasted_iota(jnp.int32, (block, block), 1)
    allowed = (row // steps == column // steps) & (row >= column)
    for head in range(heads):
        table = jnp.zeros(spots.shape, WIDE)
        for bucket in range(buckets):
            table = jnp.where(spots == bucket, bias_ref[bucket, head], table)
        tiled = jnp.concatenate([table] * (block // steps), axis=0)
        side = (head % 2) * block
        mask_ref[head // 2, :, side : side + block] = jnp.where(allowed, tiled, MASKED)


def pair_softmax(scores, block):
    parts = []
    for side in range(2):
        part = scores[:, side * block : (side + 1) * block]
        part = jnp.exp(part - jnp.max(part, axis=-1, keepdims=True))
        parts.append(part / jnp.sum(part, axis=-1, keepdims=True))
    return jnp.concatenate(parts, axis=1)


def line_of(ref):
    return ref[...].reshape(1, ref.shape[0])


def grad_of_token(score_ref, row_ref):
    row = line_of(row_ref).astype(WIDE)
    scores = jnp.broadcast_to(line_of(score_ref), (8, score_ref.shape[0])).T[:, :1]
    return scores * row.shape[1] ** (-0.5), row


def self_forward_part(
    scale, pairs, block, copies,
    dec_ref, self_gain_ref, cross_gain_ref, score_ref, row_ref, grad_hidden_ref, bucket_ref, bias_ref,
    act_one_ref, query_ref, key_ref, value_ref, mixed_ref, residual_ref, act_two_ref, query_two_ref, upstream_ref,
    weight_buf, mask_ref,
):
    tokens = dec_ref[...].astype(WIDE)
    act_one = (tokens * inverse_root(tokens) * line_of(self_gain_ref)).astype(LOW)
    act_one_ref[...] = act_one
    bias_masks(bucket_ref, bias_ref, mask_ref, block)
    scaled, row = grad_of_token(score_ref, row_ref)
    upstream_ref[...] = (grad_hidden_ref[...] + scaled * row).astype(LOW)
    for spot, ref in ((0, query_ref), (1, key_ref), (2, value_ref)):
        copies[spot].wait()
        ref[...] = mul(act_one, weight_buf[spot]).astype(LOW)
    for start in range(0, tokens.shape[0], block):
        for pair in range(pairs):
            rows, cols = slice(start, start + block), slice(pair * block, (pair + 1) * block)
            scores = mul_cols(query_ref[rows, cols], two_heads(key_ref[rows, cols])) * scale
            weights = pair_softmax(scores + mask_ref[pair], block).astype(LOW)
            mixed_ref[rows, cols] = mul(weights, two_heads(value_ref[rows, cols])).astype(LOW)
    copies[3].wait()
    residual = tokens + mul(mixed_ref[...], weight_buf[3])
    residual_ref[...] = residual
    act_two = (residual * inverse_root(residual) * line_of(cross_gain_ref)).astype(LOW)
    act_two_ref[...] = act_two
    copies[4].wait()
    query_two_ref[...] = mul(act_two, weight_buf[4]).astype(LOW)


def regroup_kernel(head_ref, rows_ref, chip_ref, far_ref, near_ref, own_ref):
    for near, ref in ((2, chip_ref), (3, far_ref), (1, near_ref), (0, own_ref)):
        ref[...] = rows_ref[head_ref[0] ^ near]


def regroup(order, head, rows):
    shape = shape_of(*rows.shape[1:])
    return order.run(regroup_kernel, (head, rows), [shape] * 4, [SCALARS, VMEM], [VMEM] * 4, [], 0, 0, "regroup")


def attend_mask(head_ref, key_segment_ref, slot_ref, mask_ref, spots):
    rows, length = key_segment_ref.shape
    slots = slot_ref.shape[1]
    head = head_ref[0]
    part = length // rows
    queries = mask_ref.shape[1]
    keys = jnp.concatenate(
        [
            key_segment_ref[pl.ds(head, 1), pl.ds(pl.multiple_of((head ^ spot) * part, part), part)]
            for spot in spots
        ],
        axis=1,
    )
    key_hot = hot((slots, keys.shape[1]), lambda row, column: row == keys)
    slot_segment = slot_ref[pl.ds(head, 1), :]
    slot_hot = hot((slots, slots), lambda row, column: row == slot_segment)
    ask_hot = mul(slot_hot, hot((slots, queries), lambda row, column: row == column // (queries // slots)))
    mask_ref[...] = jnp.where(mul_rows(key_hot, ask_hot.astype(LOW)) > 0.5, 0.0, MASKED)


def one_head(pair, side):
    width = pair.shape[1] // 2
    lane = lax.broadcasted_iota(jnp.int32, pair.shape, 1)
    return jnp.where((lane < width) == (side == 0), pair, jnp.zeros_like(pair))


def half_attention(pair, side, query, key_ref, value_t, mask_ref):
    lanes = BLOCK
    width = lanes // 2
    cols = slice(pair * lanes, (pair + 1) * lanes)
    spots = slice((2 * pair + side) * width, (2 * pair + side + 1) * width)
    scores = mul_cols(key_ref[:, cols], one_head(query, side)) + mask_ref[...]
    highest = jnp.max(scores, axis=0, keepdims=True)
    raised = jnp.exp(scores - highest)
    return highest, jnp.sum(raised, axis=0, keepdims=True), mul(value_t[spots], raised.astype(LOW)), spots


def cross_first_part(
    scale, pairs, copies,
    head_ref, first_ref, second_ref, key_segment_ref, slot_ref, query_ref,
    key_ref, value_ref, mixed_ref, highest_ref, mass_ref,
    weight_buf, mask_ref, value_t,
):
    attend_mask(head_ref, key_segment_ref, slot_ref, mask_ref, (0, 1))
    rows = first_ref.shape[0]
    for spot, ref in ((0, key_ref), (1, value_ref)):
        copies[spot].wait()
        ref[:rows] = mul(first_ref[...], weight_buf[spot]).astype(LOW)
        ref[rows:] = mul(second_ref[...], weight_buf[spot]).astype(LOW)
    value_t[...] = value_ref[...].T
    for pair in range(pairs):
        query = query_ref[:, pair * BLOCK : (pair + 1) * BLOCK] * scale
        for side in range(2):
            head = 2 * pair + side
            highest, mass, mixed, spots = half_attention(pair, side, query, key_ref, value_t, mask_ref)
            highest_ref[head : head + 1, :] = highest
            mass_ref[head : head + 1, :] = mass
            mixed_ref[spots] = mixed


def self_cross_kernel(
    scale, pairs,
    dec_ref, self_gain_ref, cross_gain_ref, score_ref, row_ref, grad_hidden_ref, bucket_ref, bias_ref,
    head_ref, first_ref, second_ref, key_segment_ref, slot_ref,
    query_w, key_w, value_w, output_w, cross_w, cross_key_w, cross_value_w,
    act_one_ref, query_ref, key_ref, value_ref, mixed_one_ref, residual_ref, act_two_ref, query_two_ref, upstream_ref,
    key_two_ref, value_two_ref, mixed_ref, highest_ref, mass_ref,
    weight_buf, bias_mask_ref, mask_ref, value_t, semaphores,
):
    sources = (query_w, key_w, value_w, output_w, cross_w, cross_key_w, cross_value_w)
    copies = load_all(sources, [weight_buf.at[i] for i in range(len(sources))], semaphores)
    self_forward_part(
        scale, pairs, BLOCK, copies,
        dec_ref, self_gain_ref, cross_gain_ref, score_ref, row_ref, grad_hidden_ref, bucket_ref, bias_ref,
        act_one_ref, query_ref, key_ref, value_ref, mixed_one_ref, residual_ref, act_two_ref, query_two_ref, upstream_ref,
        weight_buf, bias_mask_ref,
    )
    cross_first_part(
        scale, pairs, copies[5:],
        head_ref, first_ref, second_ref, key_segment_ref, slot_ref, query_two_ref,
        key_two_ref, value_two_ref, mixed_ref, highest_ref, mass_ref,
        weight_buf.at[5:], mask_ref, value_t,
    )


def self_cross(order, dec, self_gain, cross_gain, score, row, grad_hidden, bucket, bias, head, first, second, key_segment, slots, *weights):
    tokens, width = dec.shape
    heads = bias.shape[1]
    rows = first.shape[0]
    low, stat = shape_of(tokens, width), shape_of(heads, tokens, kind=WIDE)
    return order.run(
        functools.partial(self_cross_kernel, (width // heads) ** (-0.5), heads // 2),
        (dec, self_gain, cross_gain, score, row, grad_hidden, bucket, bias, head, first, second, key_segment, slots, *weights),
        [low] * 5 + [shape_of(tokens, width, kind=WIDE), low, low, low]
        + [shape_of(2 * rows, width)] * 2 + [shape_of(width, tokens, kind=WIDE), stat, stat],
        [VMEM] * 7 + [SCALARS] * 2 + [VMEM] * 4 + [HBM] * 7,
        [VMEM] * 14,
        [
            pltpu.VMEM((7, width, width), LOW),
            pltpu.VMEM((heads // 2, BLOCK, 2 * BLOCK), WIDE),
            pltpu.VMEM((2 * rows, tokens), WIDE),
            pltpu.VMEM((width, 2 * rows), LOW),
            pltpu.SemaphoreType.DMA((7,)),
        ],
        0, 0, "self_cross",
    )


def cross_last_part(
    scale, pairs, copies,
    head_ref, third_ref, fourth_ref, key_segment_ref, slot_ref, query_ref,
    mixed_a_ref, highest_a_ref, mass_a_ref, residual_ref, gain_ref,
    key_ref, value_ref, mixed_ref, totals_ref, residual_two_ref, act_ref,
    weight_buf, mask_ref, value_t,
):
    attend_mask(head_ref, key_segment_ref, slot_ref, mask_ref, (2, 3))
    rows = third_ref.shape[0]
    for spot, ref in ((0, key_ref), (1, value_ref)):
        copies[spot].wait()
        ref[:rows] = mul(third_ref[...], weight_buf[spot]).astype(LOW)
        ref[rows:] = mul(fourth_ref[...], weight_buf[spot]).astype(LOW)
    value_t[...] = value_ref[...].T
    for pair in range(pairs):
        query = query_ref[:, pair * BLOCK : (pair + 1) * BLOCK] * scale
        for side in range(2):
            head = 2 * pair + side
            line = slice(head, head + 1)
            highest, mass, mixed, spots = half_attention(pair, side, query, key_ref, value_t, mask_ref)
            top = jnp.maximum(highest, highest_a_ref[line, :])
            here, there = jnp.exp(highest - top), jnp.exp(highest_a_ref[line, :] - top)
            mass = mass * here + mass_a_ref[line, :] * there
            totals_ref[line, :] = top + jnp.log(mass)
            inverse = 1.0 / mass
            mixed_ref[spots] = (mixed * (here * inverse) + mixed_a_ref[spots] * (there * inverse)).astype(LOW)
    copies[2].wait()
    residual = residual_ref[...] + mul(mixed_ref[...].T, weight_buf[2])
    residual_two_ref[...] = residual
    act_ref[...] = (residual * inverse_root(residual) * line_of(gain_ref)).astype(LOW)


def gelu_parts(pre):
    root = 0.7978845608028654
    square = pre * pre
    curve = jnp.tanh(root * (pre + 0.044715 * (square * pre)))
    ahead = 0.5 * (1.0 + curve)
    slope = ahead + (0.5 * root) * pre * (1.0 - curve * curve) * (1.0 + (3 * 0.044715) * square)
    return (pre * ahead).astype(LOW), slope


def spread_quarters(core, turned, other_ref, at, mine_ref, spot):
    quarter = turned.shape[0] // 4
    first = core == 0
    for chip in range(2):
        even = turned[2 * chip * quarter : (2 * chip + 1) * quarter]
        odd = turned[(2 * chip + 1) * quarter : (2 * chip + 2) * quarter]
        mine_ref[spot + chip] = jnp.where(first, even, odd)
        other_ref[at + chip * quarter : at + (chip + 1) * quarter] = jnp.where(first, odd, even)


def cross_feed_kernel(
    scale, pairs,
    parts_ref, head_ref, third_ref, fourth_ref, key_segment_ref, slot_ref, query_ref,
    mixed_a_ref, highest_a_ref, mass_a_ref, residual_ref, gain_ref,
    upstream_low_ref, act_one_ref, mixed_one_ref, act_two_ref,
    key_w, value_w, output_w, feed_in, feed_out,
    key_ref, value_ref, totals_ref, residual_two_ref, act_ref,
    other_ref, grad_pre_ref, total_ref, upward_ref, mine_ref,
    weight_buf, mask_ref, value_t, mixed_ref, semaphores,
):
    part, width = grad_pre_ref.shape[2], act_ref.shape[1]
    columns = [pl.ds(pl.multiple_of(parts_ref[step] * part, part), part) for step in range(2)]
    sources = [key_w, value_w, output_w]
    for spot in columns:
        sources += [feed_in.at[:, spot], feed_out.at[spot]]
    copies = load_all(sources, [weight_buf.at[i] for i in range(len(sources))], semaphores)
    cross_last_part(
        scale, pairs, copies,
        head_ref, third_ref, fourth_ref, key_segment_ref, slot_ref, query_ref,
        mixed_a_ref, highest_a_ref, mass_a_ref, residual_ref, gain_ref,
        key_ref, value_ref, mixed_ref, totals_ref, residual_two_ref, act_ref,
        weight_buf, mask_ref, value_t,
    )
    turned = (act_ref[...].T, mixed_ref[...], act_one_ref[...].T, mixed_one_ref[...].T, act_two_ref[...].T)
    for spot, source in enumerate(turned):
        spread_quarters(parts_ref[2], source, other_ref, 2 * part + spot * width // 2, mine_ref, 2 * spot)
    other_ref[2 * part + len(turned) * width // 2 :] = upstream_low_ref[...].T
    for step in range(2):
        copies[3 + 2 * step].wait()
        copies[4 + 2 * step].wait()
        in_ref, out_ref = weight_buf.at[3 + 2 * step], weight_buf.at[4 + 2 * step]
        hidden, slope = gelu_parts(mul(act_ref[...], in_ref[...]))
        other_ref[step * part : (step + 1) * part] = hidden.T
        grad_pre = (mul_cols(upstream_low_ref[...], out_ref[...]) * slope).astype(LOW)
        grad_pre_ref[step] = grad_pre
        total, upward = mul(hidden, out_ref[...]), mul_cols(grad_pre, in_ref[...])
        if step == 0:
            total_ref[...], upward_ref[...] = total, upward
        else:
            total_ref[...] += total
            upward_ref[...] += upward


def cross_feed(order, parts, head, third, fourth, key_segment, slots, query, mixed, highest, mass, residual, gain, upstream_low, act_one, mixed_one, act_two, key_w, value_w, output_w, feed_in, feed_out, heads):
    tokens, width = query.shape
    rows = third.shape[0]
    part = feed_in.shape[1] // 4
    height = 2 * part + 5 * width // 2 + width
    tall, wide = shape_of(2 * rows, width), shape_of(tokens, width, kind=WIDE)
    return order.run(
        functools.partial(cross_feed_kernel, (width // heads) ** (-0.5), heads // 2),
        (
            parts, head, third, fourth, key_segment, slots, query, mixed, highest, mass, residual, gain,
            upstream_low, act_one, mixed_one, act_two, key_w, value_w, output_w, feed_in, feed_out,
        ),
        [
            tall, tall, shape_of(heads, tokens, kind=WIDE), wide, shape_of(tokens, width),
            shape_of(height, tokens), shape_of(2, tokens, part), wide, wide, shape_of(10, width // 4, tokens),
        ],
        [SCALARS] * 2 + [VMEM] * 14 + [HBM] * 5,
        [VMEM] * 10,
        [
            pltpu.VMEM((7, width, width), LOW), pltpu.VMEM((2 * rows, tokens), WIDE),
            pltpu.VMEM((width, 2 * rows), LOW), pltpu.VMEM((width, tokens), LOW), pltpu.SemaphoreType.DMA((7,)),
        ],
        0, 0, "cross_feed",
    )


def feed_last_kernel(
    parts_ref,
    act_ref, upstream_low_ref, in_total_ref, in_upward_ref, score_ref, row_ref, gain_ref,
    residual_hbm, grad_hidden_hbm, feed_in, feed_out, cross_w,
    hidden_ref, grad_pre_ref,
    result_ref, ranking_ref, row_grad_ref, gain_grad_ref, grad_two_ref, grad_two_low_ref, grad_mixed_ref,
    weight_buf, wide_buf, semaphores,
):
    part = grad_pre_ref.shape[2]
    columns = [pl.ds(pl.multiple_of(parts_ref[2 + step] * part, part), part) for step in range(2)]
    sources = []
    for spot in columns:
        sources += [feed_in.at[:, spot], feed_out.at[spot]]
    copies = load_all(
        sources + [residual_hbm, grad_hidden_hbm, cross_w],
        [weight_buf.at[i] for i in range(4)] + [wide_buf.at[0], wide_buf.at[1], weight_buf.at[4]],
        semaphores,
    )
    total, upward = in_total_ref[...], in_upward_ref[...]
    for step in range(2):
        copies[2 * step].wait()
        copies[2 * step + 1].wait()
        in_ref, out_ref = weight_buf.at[2 * step], weight_buf.at[2 * step + 1]
        hidden, slope = gelu_parts(mul(act_ref[...], in_ref[...]))
        hidden_ref[step] = hidden.T
        grad_pre = (mul_cols(upstream_low_ref[...], out_ref[...]) * slope).astype(LOW)
        grad_pre_ref[step] = grad_pre
        total = total + mul(hidden, out_ref[...])
        upward = upward + mul_cols(grad_pre, in_ref[...])
    copies[4].wait()
    copies[5].wait()
    residual = wide_buf[0]
    scaled, row = grad_of_token(score_ref, row_ref)
    final = residual + total
    result_ref[...] = final.astype(LOW)
    ranking = jnp.sum(final * row, axis=-1, keepdims=True) * row.shape[1] ** (-0.5)
    ranking_ref[...] = jnp.broadcast_to(ranking, (ranking.shape[0], BLOCK)).T[:1]
    row_grad_ref[...] = jnp.sum(scaled * final, axis=0, keepdims=True)
    back, gain_grad = norm_grads(residual, line_of(gain_ref), upward)
    gain_grad_ref[...] = gain_grad
    grad_two = wide_buf[1] + scaled * row + back
    grad_two_ref[...] = grad_two
    grad_two_low = grad_two.astype(LOW)
    grad_two_low_ref[...] = grad_two_low
    copies[6].wait()
    grad_mixed_ref[...] = mul_cols(grad_two_low, weight_buf[4]).astype(LOW)


def feed_last(order, parts, act, upstream_low, total, upward, residual, grad_hidden, score, row, gain, feed_in, feed_out, cross_output):
    tokens, width = act.shape
    part = feed_in.shape[1] // 4
    low, line = shape_of(tokens, width), shape_of(1, width, kind=WIDE)
    return order.run(
        feed_last_kernel,
        (parts, act, upstream_low, total, upward, score, row, gain, residual, grad_hidden, feed_in, feed_out, cross_output),
        [
            shape_of(2, part, tokens), shape_of(2, tokens, part),
            low, shape_of(1, tokens, kind=WIDE), line, line, shape_of(tokens, width, kind=WIDE), low, low,
        ],
        [SCALARS] + [VMEM] * 7 + [HBM] * 5,
        [VMEM] * 9,
        [pltpu.VMEM((5, width, part), LOW), pltpu.VMEM((2, tokens, width), WIDE), pltpu.SemaphoreType.DMA((7,))],
        0, 0, "feed_last",
    )


def cross_backward_part(
    scale, pairs, copies,
    head_ref, query_ref, key_a_ref, value_a_ref, key_b_ref, value_b_ref, totals_ref, grad_mixed_ref,
    key_segment_ref, slot_ref, residual_ref, gain_ref, grad_two_ref,
    asked_ref, kept_ref,
    grad_one_ref, grad_mixed_one_ref, gain_grad_ref,
    weight_buf, mask_ref, key_t, query_t,
):
    attend_mask(head_ref, key_segment_ref, slot_ref, mask_ref, (0, 1, 2, 3))
    half = key_a_ref.shape[0]
    lanes = 128
    key_t[:, :half] = key_a_ref[...].T
    key_t[:, half:] = key_b_ref[...].T
    for pair in range(pairs):
        cols = slice(pair * lanes, (pair + 1) * lanes)
        query = query_ref[:, cols] * scale
        keys = (key_a_ref, key_b_ref)
        values = (value_a_ref, value_b_ref)
        key_parts = [[], []]
        value_parts = [[], []]
        for side in range(2):
            ask = one_head(query, side)
            grad = one_head(grad_mixed_ref[:, cols], side)
            head = 2 * pair + side
            total = totals_ref[head : head + 1, :]
            weights, grad_weights = [], []
            for spot in range(2):
                rows = slice(spot * half, (spot + 1) * half)
                scores = mul_cols(keys[spot][:, cols], ask) + mask_ref[rows]
                weights.append(jnp.exp(scores - total))
                grad_weights.append(mul_cols(values[spot][:, cols], grad))
            dots = sum(
                jnp.sum(one * other, axis=0, keepdims=True) for one, other in zip(weights, grad_weights)
            )
            spots = slice(head * (lanes // 2), (head + 1) * (lanes // 2))
            part = 0.0
            for spot in range(2):
                grad_scores = (weights[spot] * (grad_weights[spot] - dots)).astype(LOW)
                part += mul(key_t[spots, spot * half : (spot + 1) * half], grad_scores)
                key_parts[spot].append(mul(grad_scores, ask))
                value_parts[spot].append(mul(weights[spot].astype(LOW), grad))
            query_t[spots] = (part * scale).astype(LOW)
        for spot in range(2):
            rows = slice(spot * half, (spot + 1) * half)
            kept_ref[0, rows, cols] = (key_parts[spot][0] + key_parts[spot][1]).astype(LOW)
            kept_ref[1, rows, cols] = (value_parts[spot][0] + value_parts[spot][1]).astype(LOW)
    asked_ref[0] = query_t[...].T
    copies[0].wait()
    back, gain_grad = norm_grads(
        residual_ref[...], line_of(gain_ref), mul_cols(asked_ref[0], weight_buf[0])
    )
    gain_grad_ref[...] = gain_grad
    grad_one = grad_two_ref[...] + back
    grad_one_ref[...] = grad_one
    grad_one_low = grad_one.astype(LOW)
    asked_ref[1] = grad_one_low
    copies[1].wait()
    grad_mixed_one_ref[...] = mul_cols(grad_one_low, weight_buf[1]).astype(LOW)


def self_backward_part(
    scale, pairs, block, copies,
    query_ref, key_ref, value_ref, grad_mixed_ref, dec_ref, gain_ref, grad_one_ref, bucket_ref,
    asked_ref, cross_gain_ref, feed_gain_ref, row_grad_ref, bias_ref,
    pack_ref, ask_ref, result_ref,
    weight_buf, mask_ref, table_ref, bias_grad, small,
):
    tokens = dec_ref.shape[0]
    steps = bucket_ref.shape[0]
    bias_masks(bucket_ref, bias_ref, mask_ref, block)
    for pair in range(pairs):
        table = jnp.zeros((steps, 2 * block), WIDE)
        for start in range(0, dec_ref.shape[0], block):
            rows, cols = slice(start, start + block), slice(pair * block, (pair + 1) * block)
            query, keys, values = query_ref[rows, cols], two_heads(key_ref[rows, cols]), two_heads(value_ref[rows, cols])
            grad = grad_mixed_ref[rows, cols]
            weights = pair_softmax(mul_cols(query, keys) * scale + mask_ref[pair], block)
            grad_weights = mul_cols(grad, values)
            product = weights * grad_weights
            grad_scores = jnp.concatenate(
                [
                    product[:, side * block : (side + 1) * block]
                    - weights[:, side * block : (side + 1) * block]
                    * jnp.sum(product[:, side * block : (side + 1) * block], axis=-1, keepdims=True)
                    for side in range(2)
                ],
                axis=1,
            ).astype(LOW)
            table += jnp.sum(grad_scores.astype(WIDE).reshape(block // steps, steps, 2 * block), axis=0)
            pack_ref[0 * tokens + start : 0 * tokens + start + block, cols] = (mul(grad_scores, keys) * scale).astype(LOW)
            key_parts = mul_rows(grad_scores, query)
            value_parts = mul_rows(weights.astype(LOW), grad)
            lane = lax.broadcasted_iota(jnp.int32, (block, block), 1) < block // 2
            pack_ref[1 * tokens + start : 1 * tokens + start + block, cols] = (
                jnp.where(lane, key_parts[:block], key_parts[block:]) * scale
            ).astype(LOW)
            pack_ref[2 * tokens + start : 2 * tokens + start + block, cols] = jnp.where(lane, value_parts[:block], value_parts[block:]).astype(LOW)
        table_ref[pair] = table
    spots = bucket_columns(bucket_ref, block)
    for bucket in range(bias_ref.shape[0]):
        hit = jnp.concatenate([spots == bucket] * 2, axis=1)
        for pair in range(pairs):
            kept = jnp.sum(jnp.where(hit, table_ref[pair], 0.0), axis=0, keepdims=True)
            bias_grad[2 * pair, bucket : bucket + 1, :] = kept[:, :block]
            bias_grad[2 * pair + 1, bucket : bucket + 1, :] = kept[:, block:]
    upward = 0.0
    for spot in range(3):
        copies[spot].wait()
        upward += mul_cols(pack_ref[spot * tokens : (spot + 1) * tokens], weight_buf[spot])
    back, gain_grad = norm_grads(dec_ref[...].astype(WIDE), line_of(gain_ref), upward)
    small[...] = jnp.zeros_like(small)
    for row, value in enumerate((gain_grad, cross_gain_ref[...], feed_gain_ref[...], row_grad_ref[...])):
        small[row : row + 1, :] = value
    heads, buckets, _ = bias_grad.shape
    small[4 : 4 + heads, :buckets] = jnp.sum(bias_grad[...], axis=-1)
    ask_ref[:tokens] = asked_ref[0]
    ask_ref[tokens : 2 * tokens] = asked_ref[1]
    ask_ref[2 * tokens :] = small[...].astype(LOW)
    result_ref[...] = grad_one_ref[...] + back


def backward_kernel(
    scale, pairs,
    head_ref, query_two_ref, key_a_ref, value_a_ref, key_b_ref, value_b_ref, totals_ref, grad_mixed_ref,
    key_segment_ref, slot_ref, residual_ref, cross_gain_ref, grad_two_ref,
    query_ref, key_ref, value_ref, dec_ref, self_gain_ref, bucket_ref, feed_gain_grad_ref, row_grad_ref, bias_ref,
    cross_query_w, output_w, query_w, key_w, value_w,
    kept_ref, pack_ref, ask_ref, result_ref,
    weight_buf, mask_ref, key_t, query_t, asked, grad_one, grad_mixed_one, gain_grad,
    bias_mask_ref, table_ref, bias_grad, small, semaphores,
):
    sources = (cross_query_w, output_w, query_w, key_w, value_w)
    copies = load_all(sources, [weight_buf.at[i] for i in range(len(sources))], semaphores)
    cross_backward_part(
        scale, pairs, copies,
        head_ref, query_two_ref, key_a_ref, value_a_ref, key_b_ref, value_b_ref, totals_ref, grad_mixed_ref,
        key_segment_ref, slot_ref, residual_ref, cross_gain_ref, grad_two_ref,
        asked, kept_ref, grad_one, grad_mixed_one, gain_grad,
        weight_buf, mask_ref, key_t, query_t,
    )
    self_backward_part(
        scale, pairs, BLOCK, copies[2:],
        query_ref, key_ref, value_ref, grad_mixed_one, dec_ref, self_gain_ref, grad_one, bucket_ref,
        asked, gain_grad, feed_gain_grad_ref, row_grad_ref, bias_ref,
        pack_ref, ask_ref, result_ref,
        weight_buf.at[2:], bias_mask_ref, table_ref, bias_grad, small,
    )


def backward(order, head, query_two, key_a, value_a, key_b, value_b, totals, grad_mixed, key_segment, slots, residual, cross_gain, grad_two, query, key, value, dec, self_gain, bucket, feed_gain_grad, row_grad, bias, *weights):
    tokens, width = query.shape
    buckets, heads = bias.shape
    keys = 2 * key_a.shape[0]
    rest = -(-(4 + heads) // 16) * 16
    return order.run(
        functools.partial(backward_kernel, (width // heads) ** (-0.5), heads // 2),
        (
            head, query_two, key_a, value_a, key_b, value_b, totals, grad_mixed, key_segment, slots, residual, cross_gain,
            grad_two, query, key, value, dec, self_gain, bucket, feed_gain_grad, row_grad, bias, *weights,
        ),
        [
            shape_of(2, keys, width), shape_of(3 * tokens, width), shape_of(2 * tokens + rest, width),
            shape_of(tokens, width, kind=WIDE),
        ],
        [SCALARS] + [VMEM] * 20 + [SCALARS] + [HBM] * 5,
        [VMEM] * 4,
        [
            pltpu.VMEM((5, width, width), LOW),
            pltpu.VMEM((keys, tokens), WIDE),
            pltpu.VMEM((width, keys), LOW),
            pltpu.VMEM((width, tokens), LOW),
            pltpu.VMEM((2, tokens, width), LOW),
            pltpu.VMEM((tokens, width), WIDE),
            pltpu.VMEM((tokens, width), LOW),
            pltpu.VMEM((1, width), WIDE),
            pltpu.VMEM((heads // 2, BLOCK, 2 * BLOCK), WIDE),
            pltpu.VMEM((heads // 2, bucket.shape[0], 2 * BLOCK), WIDE),
            pltpu.VMEM((heads, buckets, BLOCK), WIDE),
            pltpu.VMEM((rest, width), WIDE),
            pltpu.SemaphoreType.DMA((5,)),
        ],
        0, 0, "backward",
    )


def encoder_weights_kernel(core_ref, first_ref, second_ref, third_ref, fourth_ref, grads_ref, other_ref, mine_ref, turned, whole):
    for spot, ref in enumerate((first_ref, second_ref, third_ref, fourth_ref)):
        rows = ref.shape[0]
        turned[:, spot * rows : (spot + 1) * rows] = ref[...].T
    quarter = whole.shape[0] // 4
    core = core_ref[0]
    for weight in range(2):
        whole[...] = mul(turned[...], grads_ref[weight]).astype(LOW)
        for chip in range(2):
            at = lambda side: pl.ds(pl.multiple_of((2 * chip + side) * quarter, quarter), quarter)
            mine_ref[weight, chip] = whole[at(core)]
            other_ref[weight, chip] = whole[at(1 - core)]


def encoder_weights(order, core, rows, grads):
    count, width = rows[0].shape
    shape = shape_of(2, 2, width // 4, width)
    return order.run(
        encoder_weights_kernel,
        (core, *rows, grads),
        [shape] * 2,
        [SCALARS] + [VMEM] * 5,
        [VMEM] * 2,
        [pltpu.VMEM((width, 4 * count), LOW), pltpu.VMEM((width, width), LOW)],
        16 * count * width * width, 8 * width * width, "encoder_weights",
    )


def encoder_rows_kernel(grads_ref, key_w, value_w, own_ref, near_ref, chip_ref, weight_buf, semaphores):
    copies = load_all((key_w, value_w), [weight_buf.at[0], weight_buf.at[1]], semaphores)
    for copy in copies:
        copy.wait()
    rows = own_ref.shape[0]
    for ref, start in ((own_ref, 0), (near_ref, rows), (chip_ref, 2 * rows)):
        part = slice(start, start + ref.shape[0])
        grad = mul_cols(grads_ref[0, part], weight_buf[0]) + mul_cols(grads_ref[1, part], weight_buf[1])
        ref[...] = grad.astype(ref.dtype)


def encoder_rows(order, grads, key_w, value_w):
    rows, width = grads.shape[1] // 4, grads.shape[2]
    return order.run(
        encoder_rows_kernel,
        (grads, key_w, value_w),
        [shape_of(rows, width, kind=WIDE), shape_of(rows, width), shape_of(2 * rows, width)],
        [VMEM] + [HBM] * 2,
        [VMEM] * 3,
        [pltpu.VMEM((2, width, width), LOW), pltpu.SemaphoreType.DMA((2,))],
        16 * rows * width * width, 8 * width * width, "encoder_rows", room=28,
    )


def stage_kernel(mode, weights, rows, extra, count, place_ref, *refs):
    stage, way = mode
    chip, pair = place_ref[0], place_ref[1]
    inputs, outs = refs[:count], refs[count:]

    def columns(matrix, side):
        if side is None:
            return matrix
        half = matrix.shape[1] // 2
        return jnp.where((pair == 0) == (side == 0), matrix[:, :half], matrix[:, half:])

    def value(weight, quarter, side):
        if len(weight) == 3:
            here, came, row = weight
            return columns(inputs[here][row:].astype(WIDE) + inputs[came][row:].astype(WIDE), side)
        if len(weight) == 4:
            here, spot, came, other = weight
            return columns(
                inputs[here][spot, quarter].astype(WIDE) + inputs[came][other, quarter].astype(WIDE), side
            )
        here, base, came, at, grads, grads_came, row = weight
        size, tokens = inputs[here].shape[1:]
        there = inputs[came][pl.ds(pl.multiple_of(at + quarter * size, 64), size)]
        if grads_came == came:
            near, far = inputs[grads][...], columns(mul_cols(there, inputs[came][row:]), side)
        else:
            spots = slice(row, row + tokens)
            near, far = inputs[grads][spots], mul(there, columns(inputs[grads_came][spots], side))
        return mul(inputs[here][base + quarter], columns(near, side)) + far

    at = 0
    for weight in list(weights) + ([] if extra is None else [extra]):
        if way == PAIR:
            totals = [value(weight, quarter, 1 if stage == 0 else 0) for quarter in range(2)]
        else:
            total = value(weight, (1 - chip) if stage == 0 else chip, None)
            half = total.shape[1] // 2
            totals = [total[:, :half], total[:, half:]]
        spots = slice(at, at + totals[0].shape[0])
        at = spots.stop
        if stage == 1:
            totals = [total + inputs[-1][part, spots].astype(WIDE) for part, total in enumerate(totals)]
        totals = [total.astype(LOW) for total in totals]
        if stage == 0 or way == WHOLE:
            outs[0][0, spots] = totals[0]
            outs[0][1, spots] = totals[1]
        else:
            low = (chip if way == PAIR else pair) == 0
            outs[0][spots] = jnp.where(low, totals[1], totals[0])
            outs[1][spots] = jnp.where(low, totals[0], totals[1])


def stage(order, spots, mode, weights, extra=None, came=None):
    arrays, described = [], []

    def spot_of(array):
        for spot, known in enumerate(arrays):
            if known is array:
                return spot
        arrays.append(array)
        return len(arrays) - 1

    for weight in weights:
        if len(weight) == 4:
            here, spot, other, member = weight
            described.append((spot_of(here), spot, spot_of(other), member))
            rows, columns = here.shape[-2:]
        else:
            here, base, other, at, grads, grads_came, row = weight
            described.append((spot_of(here), base, spot_of(other), at, spot_of(grads), spot_of(grads_came), row))
            rows, columns = here.shape[1], grads.shape[1]
    height = rows * len(weights)
    if extra is not None:
        height += extra[0].shape[0] - extra[2]
        extra = (spot_of(extra[0]), spot_of(extra[1]), extra[2])
    if came is not None:
        arrays.append(came)
    if mode[0] == 0 or mode[1] == WHOLE:
        shapes = [shape_of(2, height, columns // 2)]
    else:
        shapes = [shape_of(height, columns // 2)] * 2
    return order.run(
        functools.partial(stage_kernel, mode, described, rows, extra, len(arrays)),
        (spots, *arrays),
        shapes,
        [SCALARS] + [VMEM] * len(arrays),
        [VMEM] * len(shapes),
        [],
        0, 0, "stage", room=20,
    )


def feed_in_kernel(stage_index, place_ref, here_ref, came_ref, first_ref, last_ref, first_came_ref, last_came_ref, *refs):
    chip, pair, core = place_ref[0], place_ref[1], place_ref[2]
    half = pair if stage_index else 1 - pair
    part = last_ref.shape[2]
    low = chip == 0
    for side, (own, other) in enumerate(((last_ref, first_came_ref), (first_ref, last_came_ref))):
        block = core if side == 0 else 1 - core
        columns = pl.ds(pl.multiple_of(block * part, part), part)
        totals = []
        for quarter in range(2):
            size = here_ref.shape[1]
            start = 2 * part + quarter * size
            total = mul(here_ref[quarter], own[half]) + mul(came_ref[start : start + size], other[half])
            if stage_index:
                total += refs[0][quarter, :, columns].astype(WIDE)
            totals.append(total.astype(LOW))
        if stage_index:
            refs[1][:, columns] = jnp.where(low, totals[1], totals[0])
            refs[2][:, columns] = jnp.where(low, totals[0], totals[1])
        else:
            refs[0][0, :, columns] = totals[0]
            refs[0][1, :, columns] = totals[1]


def feed_in_stage(order, spots, stage_index, here, came, first, last, first_came, last_came, arrived=None):
    arrays = [here, came, first, last, first_came, last_came] + ([] if arrived is None else [arrived])
    rows = here.shape[1]
    half = 2 * first.shape[2]
    shapes = [shape_of(rows, half)] * 2 if stage_index else [shape_of(2, rows, half)]
    return order.run(
        functools.partial(feed_in_kernel, stage_index),
        (spots, *arrays),
        shapes,
        [SCALARS] + [VMEM] * len(arrays),
        [VMEM] * len(shapes),
        [],
        0, 0, "feed_in_stage", room=20,
    )


def combine_kernel(way, heights, place_ref, *refs):
    line, length = place_ref[3], place_ref[4]
    left = line < length // 2
    takes = (line == 0) | (line == length - 1)

    def add(first, second):
        return (first.astype(WIDE) + second.astype(WIDE)).astype(LOW)

    if way == ADD:
        refs[2][...] = add(refs[0][...], refs[1][...])
    elif way == SPLIT:
        sums = [add(refs[0][part], refs[1][part]) for part in range(2)]
        refs[2][...] = jnp.where(left, sums[0], sums[1])
        refs[3][...] = jnp.where(left, sums[1], sums[0])
    elif way == JOIN:
        refs[2][0] = jnp.where(left, refs[0][...], refs[1][...])
        refs[2][1] = jnp.where(left, refs[1][...], refs[0][...])
    elif way == TAKE:
        refs[2][...] = jnp.where(takes, refs[1][...], refs[0][...])
    else:
        at = 0
        for index, height in enumerate(heights):
            spots = slice(at, at + height)
            at += height
            if way == COLUMNS:
                first = place_ref[1] == 0
                mine, came = refs[0][spots], refs[1][spots]
                parts = (jnp.where(first, mine, came), jnp.where(first, came, mine))
            else:
                parts = [jnp.where(takes, refs[1][part, spots], refs[0][part, spots]) for part in range(2)]
            half = parts[0].shape[1]
            refs[2 + index][:, :half] = parts[0].astype(WIDE)
            refs[2 + index][:, half:] = parts[1].astype(WIDE)


def combine(order, spots, way, mine, came, heights):
    if way == SPLIT:
        shapes = [shape_of(*mine.shape[1:])] * 2
    elif way == JOIN:
        shapes = [shape_of(2, *mine.shape)]
    elif way in (ADD, TAKE):
        shapes = [shape_of(*mine.shape)]
    else:
        shapes = [shape_of(height, 2 * mine.shape[-1], kind=WIDE) for height in heights]
    results = order.run(
        functools.partial(combine_kernel, way, heights),
        (spots, mine, came),
        shapes,
        [SCALARS] + [VMEM] * 2,
        [VMEM] * len(shapes),
        [],
        0, 0, NAMES[way], room=12,
    )
    return results[0] if way in (ADD, TAKE, JOIN) else results


def hand_on_kernel(*refs):
    for source, target in zip(refs[: len(refs) // 2], refs[len(refs) // 2 :]):
        target[...] = source[...]


def hand_on(order, *arrays):
    shapes = [shape_of(*array.shape, kind=array.dtype) for array in arrays]
    return order.run(
        hand_on_kernel, arrays, shapes, [VMEM] * len(arrays), [VMEM] * len(arrays), [], 0, 0, "hand_on", room=16
    )


def place_rows_kernel(head_ref, own_ref, core_ref, chip_ref, far_ref, out_ref):
    for spot, ref in enumerate((own_ref, core_ref, chip_ref, far_ref)):

        @pl.when(pl.program_id(0) == spot)
        def _():
            out_ref[0] = ref[...].astype(WIDE)


def place_rows(order, head, own, core, chip, far):
    rows, width = own.shape
    return order.run(
        place_rows_kernel,
        (head, own, core, chip, far),
        [shape_of(4, rows, width, kind=WIDE)],
        [pl.BlockSpec((rows, width), lambda step, head: (0, 0))] * 4,
        [pl.BlockSpec((1, rows, width), lambda step, head: (head[0] ^ step, 0, 0))],
        [],
        0, 24 * rows * width, "place_rows", grid=(4,), prefetch=1, room=16,
    )[0]


AXES = ("dp", "head")


def device_maps(dp_size, head_size):
    length = dp_size // 2
    half = length // 2

    def of(move):
        pairs = []
        for outer in range(dp_size):
            for inner in range(head_size):
                goal = move(outer // 2, outer % 2, inner)
                if goal is not None:
                    spot, side, place = goal
                    pairs.append(
                        (outer * head_size + inner, (2 * spot + side) * head_size + place)
                    )
        return pairs

    def along(first, first_goal):
        def step(spot, side, place):
            if spot == first:
                return (first_goal, side, place)
            if spot == length - 1 - first:
                return (length - 1 - first_goal, side, place)
            return None

        return of(step)

    return {
        CORE: of(lambda spot, side, place: (spot, side, place ^ 1)),
        CHIP: of(lambda spot, side, place: (spot, side, place ^ 2)),
        FAR: of(lambda spot, side, place: (spot, side, place ^ 3)),
        PAIR: of(lambda spot, side, place: (spot, 1 - side, place)),
        MIDDLE_PAIR: of(
            lambda spot, side, place: (spot, 1 - side, place) if spot in (half - 1, half) else None
        ),
        INWARD: [along(step, step + 1) for step in range(half - 1)],
        MIDDLE: along(half - 1, half),
        OUTWARD: [along(step + 1, step) for step in range(half - 1)],
    }


class Made:
    pass


class Place:
    def __init__(self):
        dp_size, head_size = lax.axis_size("dp"), lax.axis_size("head")
        self.maps = device_maps(dp_size, head_size)
        self.length = dp_size // 2
        self.head = lax.axis_index("head")
        self.chip, self.core = self.head // 2, self.head % 2
        dp_index = lax.axis_index("dp")
        self.pair, self.line = dp_index % 2, dp_index // 2

    def move(self, array, name):
        return lax.ppermute(array, AXES, self.maps[name])

    def inward(self, part):
        perms = self.maps[INWARD]
        for perm in perms[:-1]:
            part = add_low(part, lax.ppermute(part, AXES, perm))
        return part, lax.ppermute(part, AXES, perms[-1])

    def outward(self, part):
        perms = self.maps[OUTWARD]
        for step in range(len(perms) - 1, 0, -1):
            came = lax.ppermute(part, AXES, perms[step])
            part = jnp.where(self.takes(step), came, part)
        return part, lax.ppermute(part, AXES, perms[0])

    def takes(self, step):
        return (self.line == step) | (self.line == self.length - 1 - step)


def add_low(first, second):
    kind = first.dtype
    return (first.astype(jnp.float32) + second.astype(jnp.float32)).astype(kind)


def picks(*values):
    return jnp.stack([jnp.asarray(value, jnp.int32) for value in values])


class Group:
    def __init__(self, place, order, spots, mode):
        self.place, self.order, self.spots, self.mode = place, order, spots, mode
        self.steps = [SECOND] + (
            [SPLIT, ADD, ADD, JOIN, LINES]
            if mode == WHOLE
            else [ADD_INWARD, ADD_MIDDLE, ADD_OUTWARD, TAKE, COLUMNS]
        )

    def first(self, weights, extra=None):
        self.weights, self.extra = weights, extra
        (sent,) = stage(self.order, self.spots, (0, self.mode), weights, extra)
        rows = 0 if extra is None else extra[0].shape[0] - extra[2]
        self.heights = [(sent.shape[1] - rows) // len(weights)] * len(weights) + [rows] * (rows > 0)
        self.came = self.place.move(sent, PAIR if self.mode == PAIR else CHIP)

    def first_feed_in(self, parts):
        self.parts, self.weights = parts, None
        (sent,) = feed_in_stage(self.order, self.spots, 0, *parts)
        self.heights = [sent.shape[1]]
        self.came = self.place.move(sent, PAIR)

    def step(self):
        place = self.place
        way = self.steps.pop(0)
        if way == SECOND:
            if self.weights is None:
                results = feed_in_stage(self.order, self.spots, 1, *self.parts, self.came)
            else:
                results = stage(self.order, self.spots, (1, self.mode), self.weights, self.extra, self.came)
            if self.mode == WHOLE:
                self.part, self.came = place.inward(results[0])
            else:
                self.part = results[1]
                self.came = place.move(results[0], CHIP if self.mode == PAIR else PAIR)
            return
        result = combine(self.order, self.spots, ADD if way in ADDS else way, self.part, self.came, self.heights)
        if way == SPLIT:
            self.part, other = result
            self.came = place.move(other, MIDDLE)
        elif way == ADD:
            self.part = result
            self.came = place.move(result, MIDDLE_PAIR if self.steps[0] == ADD else MIDDLE)
        elif way in (JOIN, ADD_OUTWARD):
            self.part, self.came = place.outward(result)
        elif way == ADD_INWARD:
            self.part, self.came = place.inward(result)
        elif way == ADD_MIDDLE:
            self.part, self.came = result, place.move(result, MIDDLE)
        elif way == TAKE:
            self.part, self.came = result, place.move(result, PAIR)
        else:
            self.result = result


MODES = {OUT: CHIP, IN: PAIR, SELF: PAIR, ASK: CHIP, KEEP: CHIP}
SEQUENCE = (
    BACK, SELF_PASS, OUT, ENCODER, IN, SELF_FIRST, ASK_FIRST, KEEP_PASS, OUT, IN, KEEP_FIRST, OUT, SELF, ASK, SELF,
    IN, OUT, ASK, ROWS, KEEP, SELF, IN, OUT, KEEP, ASK, SELF, IN, OUT, ROWS_SEND, ASK, SELF, KEEP, IN, ASK, KEEP,
    SELF, KEEP, ASK, ROWS_PASS, KEEP, ROWS_LAST,
)


def body(
    decoder_in,
    encoder_out,
    encoder_segment,
    slot_segment,
    position_bucket,
    self_gain,
    self_query,
    self_key,
    self_value,
    self_output,
    position_bias,
    cross_gain,
    cross_query,
    cross_key,
    cross_value,
    cross_output,
    feed_gain,
    feed_in,
    feed_out,
    score_row,
    grad_hidden,
    grad_score,
):
    place = Place()
    model_width = decoder_in.shape[1]
    heads = position_bias.shape[1]
    tokens = decoder_in.shape[0]
    head_index, core = place.head, place.core
    core_list, head_list = picks(core), picks(head_index)
    spots = picks(place.chip, place.pair, core, place.line, place.length)
    order = Order()
    to_chip, to_far, to_near, own_rows = regroup(order, head_list, encoder_out)
    from_chip, from_far, from_near = place.move(to_chip, CHIP), place.move(to_far, FAR), place.move(to_near, CORE)
    rows = [own_rows, from_near, from_chip, from_far]
    (
        act_one, query_one, key_one, value_one, mixed_one, residual_one, act_two, query_two, upstream_low,
        key_a, value_a, mixed_a, highest, mass,
    ) = self_cross(
        order, decoder_in, self_gain, cross_gain, grad_score, score_row, grad_hidden, position_bucket, position_bias,
        head_list, own_rows, from_near, encoder_segment, slot_segment,
        self_query, self_key, self_value, self_output, cross_query, cross_key, cross_value,
    )
    feed_parts = picks(1 - core, 3 - core, core, 2 + core)
    key_b, value_b, totals, residual_two, act_three, feed_other, pre_first, total, upward, mine = cross_feed(
        order, feed_parts, head_list, from_chip, from_far, encoder_segment, slot_segment, query_two, mixed_a, highest,
        mass, residual_one, feed_gain, upstream_low, act_one, mixed_one, act_two,
        cross_key, cross_value, cross_output, feed_in, feed_out, heads,
    )
    feed_came, pre_first_came = place.move(feed_other, CORE), place.move(pre_first, CORE)
    (
        hidden_mine, pre_last, hidden_out, ranking, row_grad, feed_gain_grad, grad_two, grad_two_low, grad_mixed,
    ) = feed_last(
        order, feed_parts, act_three, upstream_low, total, upward, residual_two, grad_hidden, grad_score, score_row,
        feed_gain, feed_in, feed_out, cross_output,
    )
    pre_last_came, grad_two_came = place.move(pre_last, CORE), place.move(grad_two_low, CORE)
    groups = {name: Group(place, order, spots, MODES[name]) for name in MODES}
    half = model_width // 2
    acts = feed_out.shape[0] // 2
    groups[OUT].first([(hidden_mine, 0, feed_came, 0, upstream_low, feed_came, acts + 5 * half)])
    order.need(grad_two_came)
    groups[IN].first_feed_in((mine, feed_came, pre_first, pre_last, pre_first_came, pre_last_came))
    made = Made()

    def back():
        made.kept, made.grads, made.asked, made.decoder = backward(
            order, head_list, query_two, key_a, value_a, key_b, value_b, totals, grad_mixed, encoder_segment, slot_segment,
            residual_one, cross_gain, grad_two, query_one, key_one, value_one, decoder_in, self_gain, position_bucket,
            feed_gain_grad, row_grad, position_bias, cross_query, self_output, self_query, self_key, self_value,
        )

    def self_pass():
        made.asked_came, made.grads_came = place.move(made.asked, CORE), place.move(made.grads, CORE)

    def self_copy():
        copies = hand_on(order, made.asked, made.grads)
        made.asked_came, made.grads_came = [place.move(copy, CORE) for copy in copies]

    def keep_copy():
        (other,) = hand_on(order, made.other)
        made.came = place.move(other, CORE)

    def keep_pass():
        made.came = place.move(made.other, CORE)

    def self_first():
        grads = made.grads
        groups[SELF].first(
            [(mine, 4, feed_came, acts + 2 * half, grads, made.grads_came, spot * tokens) for spot in range(3)]
        )

    def ask_first():
        asked, asked_came = made.asked, made.asked_came
        groups[ASK].first(
            [
                (mine, 2, feed_came, acts + half, grad_two_low, grad_two_came, 0),
                (mine, 8, feed_came, acts + 4 * half, asked, asked_came, 0),
                (mine, 6, feed_came, acts + 3 * half, asked, asked_came, tokens),
            ],
            (asked, asked_came, 2 * tokens),
        )

    def encoder_step():
        made.other, made.mine = encoder_weights(order, core_list, rows, made.kept)

    def keep_first():
        groups[KEEP].first([(made.mine, spot, made.came, spot) for spot in range(2)])

    def rows_step():
        made.own, made.to_near, made.to_chip = encoder_rows(order, made.kept, cross_key, cross_value)

    def rows_send():
        near, chip = hand_on(order, made.to_near, made.to_chip)
        made.chip, made.near = place.move(chip, CHIP), place.move(near, CORE)

    def rows_pass():
        count = made.chip.shape[0] // 2
        order.need(made.near)
        made.far = place.move(made.chip[count:], CORE)

    def rows_last():
        made.rows = place_rows(order, head_list, made.own, made.near, made.chip, made.far)

    tasks = {
        ASK_FIRST: ask_first,
        SELF_FIRST: self_first,
        SELF_PASS: self_pass,
        BACK: back,
        KEEP_PASS: keep_pass,
        SELF_COPY: self_copy,
        KEEP_COPY: keep_copy,
        ROWS_SEND: rows_send,
        KEEP_FIRST: keep_first,
        ENCODER: encoder_step,
        ROWS: rows_step,
        ROWS_PASS: rows_pass,
        ROWS_LAST: rows_last,
        NEED_KEEP: lambda: order.need(made.came),
    }
    for name in SEQUENCE:
        tasks.get(name, lambda: groups[name].step())()
    feed_out_grad, feed_in_grad = groups[OUT].result[0], groups[IN].result[0]
    self_query_grad, self_key_grad, self_value_grad = groups[SELF].result
    cross_output_grad, cross_query_grad, self_output_grad, small = groups[ASK].result
    cross_key_grad, cross_value_grad = groups[KEEP].result
    encoder_grad = made.rows
    width = model_width // 4
    gains = lax.dynamic_slice_in_dim(small[:4], head_index * width, width, axis=1)
    buckets = position_bias.shape[0] // 4
    bias_grad = lax.dynamic_slice_in_dim(small[4 : 4 + heads], head_index * buckets, buckets, axis=1).T
    return (
        hidden_out,
        ranking[0],
        made.decoder,
        encoder_grad,
        gains[0],
        self_query_grad,
        self_key_grad,
        self_value_grad,
        self_output_grad,
        bias_grad,
        gains[1],
        cross_query_grad,
        cross_key_grad,
        cross_value_grad,
        cross_output_grad,
        gains[2],
        feed_in_grad,
        feed_out_grad,
        gains[3],
    )


def solution(mesh):
    in_specs = (
        P(("dp", "head"), None),
        P("dp", "head", None),
        P("dp", None),
        P("dp", None),
        P(),
        P(),
        P(),
        P(),
        P(),
        P(),
        P(),
        P(),
        P(),
        P(),
        P(),
        P(),
        P(),
        P(),
        P(),
        P(),
        P(("dp", "head"), None),
        P(("dp", "head")),
    )
    out_specs = (
        P(("dp", "head"), None),
        P(("dp", "head")),
        P(("dp", "head"), None),
        P("dp", "head", None),
        P("head"),
        P("head", None),
        P("head", None),
        P("head", None),
        P("head", None),
        P("head", None),
        P("head"),
        P("head", None),
        P("head", None),
        P("head", None),
        P("head", None),
        P("head"),
        P("head", None),
        P("head", None),
        P("head"),
    )
    return jax.shard_map(body, mesh=mesh, in_specs=in_specs, out_specs=out_specs, check_vma=False)
```
